32 devices in a mesh: img: 4 (over z), hid: 8 (over y, x, core).
Axes of the slice: x: 2, y: 2, z: 4, core: 2. Of those that a mesh axis runs over, the one named last changes fastest.
Arguments:
- images: bfloat16 [64, 36, 36, 128], P(('img', 'hid')), may hold values from -6 to 6
- valid_sizes: int32 [64, 2], P(('img', 'hid')), may hold values from 12 to 36, as said below
- cotangent: bfloat16 [64, 18, 5760], P(('img', 'hid')), may hold values from -6 to 6
- mix_weight: bfloat16 [2, 3, 128, 128], replicated, may hold values from -0.5 to 0.5
- mix_bias: float32 [2, 2, 128], replicated, may hold values from -3 to 3
- squeeze_weight: float32 [2, 128, 32], replicated, may hold values from -1 to 1
- squeeze_bias: float32 [2, 32], replicated, may hold values from -3 to 3
- expand_weight: float32 [2, 32, 384], replicated, may hold values from -2 to 2
- expand_bias: float32 [2, 384], replicated, may hold values from -4 to 4
- project_weight: bfloat16 [2, 128, 128], replicated, may hold values from -0.75 to 0.75
- project_bias: float32 [2, 128], replicated, may hold values from -2 to 2
- norm_gain: float32 [2, 2, 128], replicated, may hold values from 0.5 to 1.5
- norm_bias: float32 [2, 2, 128], replicated, may hold values from -2 to 2
- inner_weight: bfloat16 [2, 128, 512], P(None, None, 'hid'), may hold values from -0.5 to 0.5
- inner_bias: bfloat16 [2, 512], P(None, 'hid'), may hold values from -3 to 3
- outer_weight: bfloat16 [2, 512, 128], P(None, 'hid'), may hold values from -0.5 to 0.5
- outer_bias: float32 [2, 128], replicated, may hold values from -2 to 2
- merge_weight: bfloat16 [1152, 320], replicated, may hold values from -0.1875 to 0.1875
- merge_bias: float32 [320], replicated, may hold values from -2 to 2
Outputs:
- features: bfloat16 [64, 18, 5760], P(('img', 'hid'))
- images_grad: float32 [64, 36, 36, 128], P(('img', 'hid'))
- grad_mix_weight: float32 [2, 3, 128, 128], replicated
- grad_mix_bias: float32 [2, 2, 128], replicated
- grad_squeeze_weight: float32 [2, 128, 32], replicated
- grad_squeeze_bias: float32 [2, 32], replicated
- grad_expand_weight: float32 [2, 32, 384], replicated
- grad_expand_bias: float32 [2, 384], replicated
- grad_project_weight: float32 [2, 128, 128], replicated
- grad_project_bias: float32 [2, 128], replicated
- grad_norm_gain: float32 [2, 2, 128], replicated
- grad_norm_bias: float32 [2, 2, 128], replicated
- grad_inner_weight: float32 [2, 128, 512], P(None, None, 'hid')
- grad_inner_bias: float32 [2, 512], P(None, 'hid')
- grad_outer_weight: float32 [2, 512, 128], P(None, 'hid')
- grad_outer_bias: float32 [2, 128], replicated
- grad_merge_weight: float32 [1152, 320], replicated
- grad_merge_bias: float32 [320], replicated
The draws below stay inside these ranges and needn't reach their ends.
Inputs may be any that keep to these rules, and one draw needn't show every extreme that they name: `valid_sizes`: each map's valid region holds its first rows and columns; some map is wholly valid and some map has 12 valid rows and columns.
All inputs are finite; a program needn't handle non-finite values.
Results may differ from the reference program's by a relative error of at most 0.025.
Values may be sent and summed in bfloat16 or wider, within the bound.
No kernel may reach another device: no remote copies, remote signals or barrier semaphores. Data moves between devices by JAX's collectives and lax.ppermute only.
A program may use at most 320 MiB of HBM per device.

```python
import jax
import jax.numpy as jnp
from jax import lax

C = 128
HID = 512
RED = 32
OUT = 320
SIDE = 36
LAYERS = 2
IMAGES = 64


def draw_valid_sizes(key, part):
    key = jax.random.fold_in(key, 11)
    key_sizes, key_wide, key_narrow = jax.random.split(key, 3)
    drawn = jax.random.randint(key_sizes, (IMAGES, 2), SIDE // 3, SIDE + 1)
    widest = jax.random.randint(key_wide, (), 0, IMAGES)
    narrowest = (widest + 1 + jax.random.randint(key_narrow, (), 0, IMAGES - 1)) % IMAGES
    drawn = drawn.at[widest].set(SIDE)
    drawn = drawn.at[narrowest].set(SIDE // 3)
    return drawn.astype(jnp.int32)


def levels(stream_key, shape, shards, low, largest):
    level, own = 1.0, jax.random.fold_in(stream_key, 6)
    for dim, blocks in shards:
        steps = jnp.exp(jax.random.uniform(jax.random.fold_in(own, dim), (blocks,), jnp.float32, low / len(shards), largest / len(shards)))
        level = level * jnp.repeat(steps, shape[dim] // blocks).reshape([-1 if axis == dim else 1 for axis in range(len(shape))])
    return level


def centred(rng, dims, deviation, limit, cuts=(), kind=jnp.bfloat16):
    level = levels(rng, dims, cuts, -0.22, 0.18) if cuts else 1.0
    values = jax.random.normal(rng, dims, jnp.float32) * deviation * level
    return jnp.minimum(jnp.maximum(values, -limit), limit).astype(kind)


def setup_inputs(seed: int = 0) -> dict:
    keys = jax.random.split(jax.random.key(seed), 20)
    images = centred(keys[0], (IMAGES, SIDE, SIDE, C), 1.0, 6.0, ((0, 32),))
    valid_sizes = draw_valid_sizes(jax.random.fold_in(keys[19], 71), 0)
    cotangent = centred(keys[2], (IMAGES, SIDE // 2, (SIDE // 2) * OUT), 1.0, 6.0, ((0, 32),))
    mix_weight = centred(keys[3], (LAYERS, 3, C, C), C ** -0.5, 0.5)
    mix_bias = centred(keys[4], (LAYERS, 2, C), 0.5, 3.0, (), jnp.float32)
    squeeze_weight = centred(keys[5], (LAYERS, C, RED), (C // 4) ** -0.5, 1.0, (), jnp.float32)
    squeeze_bias = centred(keys[6], (LAYERS, RED), 0.5, 3.0, (), jnp.float32)
    expand_weight = centred(keys[7], (LAYERS, RED, 3 * C), (RED // 4) ** -0.5, 2.0, (), jnp.float32)
    expand_bias = centred(keys[8], (LAYERS, 3 * C), 1.0, 4.0, (), jnp.float32)
    project_weight = centred(keys[9], (LAYERS, C, C), (C // 2) ** -0.5, 0.75)
    project_bias = centred(keys[10], (LAYERS, C), 0.3, 2.0, (), jnp.float32)
    norm_gain = jnp.clip(1.0 + 0.1 * jax.random.normal(keys[11], (LAYERS, 2, C), jnp.float32), 0.5, 1.5)
    norm_bias = centred(keys[12], (LAYERS, 2, C), 0.3, 2.0, (), jnp.float32)
    inner_weight = centred(keys[13], (LAYERS, C, HID), C ** -0.5, 0.5, ((2, 8),))
    inner_bias = centred(keys[14], (LAYERS, HID), 0.5, 3.0, ((1, 8),))
    outer_weight = centred(keys[15], (LAYERS, HID, C), (HID // 4) ** -0.5, 0.5, ((1, 8),))
    outer_bias = centred(keys[16], (LAYERS, C), 0.3, 2.0, (), jnp.float32)
    merge_weight = centred(keys[17], (9 * C, OUT), (9 * C) ** -0.5, 0.1875)
    merge_bias = centred(keys[18], (OUT,), 0.3, 2.0, (), jnp.float32)
    return {"images": images, "valid_sizes": valid_sizes, "cotangent": cotangent, "mix_weight": mix_weight, "mix_bias": mix_bias, "squeeze_weight": squeeze_weight, "squeeze_bias": squeeze_bias, "expand_weight": expand_weight, "expand_bias": expand_bias, "project_weight": project_weight, "project_bias": project_bias, "norm_gain": norm_gain, "norm_bias": norm_bias, "inner_weight": inner_weight, "inner_bias": inner_bias, "outer_weight": outer_weight, "outer_bias": outer_bias, "merge_weight": merge_weight, "merge_bias": merge_bias}


PRECISE = lax.Precision.HIGHEST

@jax.custom_vjp
def low(v):
    return lax.optimization_barrier(v.astype(jnp.bfloat16)).astype(jnp.float32)

@jax.custom_vjp
def low_back(v):
    return v

def low_keep(v):
    return (low(v), None)

def low_pass(kept, grad):
    return (grad,)

def back_keep(v):
    return (v, None)

def back_low(kept, grad):
    return (low(grad),)
low.defvjp(low_keep, low_pass)
low_back.defvjp(back_keep, back_low)

def layer_norm(values, gain_vec, bias_vec):
    average = lax.optimization_barrier(jnp.mean(values, axis=-1, keepdims=True))
    centered = values - average
    variance = lax.optimization_barrier(jnp.mean(centered * centered, axis=-1, keepdims=True))
    return centered * lax.rsqrt(variance + 1e-05) * gain_vec + bias_vec

def cycle_shift(grid_in, axis_dim, direction):
    channels = grid_in.shape[-1]
    offset = ((jnp.arange(channels) + 1) % 3 - 1) * direction
    widths = [(0, 0)] * grid_in.ndim
    widths[axis_dim] = (1, 1)
    padded = jnp.pad(grid_in, widths)
    length = grid_in.shape[axis_dim]
    lower_rows = lax.slice_in_dim(padded, 0, length, axis=axis_dim)
    middle = lax.slice_in_dim(padded, 1, length + 1, axis=axis_dim)
    upper_rows = lax.slice_in_dim(padded, 2, length + 2, axis=axis_dim)
    return jnp.where(offset == -1, lower_rows, jnp.where(offset == 0, middle, upper_rows))

def pixel_mask(valid_sizes, side_len):
    places = jnp.arange(side_len, dtype=jnp.int32)
    rows_ok = (places[None, :] < valid_sizes[:, 0:1]).astype(jnp.float32)
    cols_ok = (places[None, :] < valid_sizes[:, 1:2]).astype(jnp.float32)
    return rows_ok[:, :, None, None] * cols_ok[:, None, :, None]

def reweight_mix(h_branch, w_branch, c_branch, squeeze_w, squeeze_b, expand_w, expand_b, valid_mask, counts):
    branch_sum = h_branch + w_branch + c_branch
    pooled = lax.optimization_barrier(jnp.sum(branch_sum * valid_mask, axis=(1, 2))) / counts[:, None]
    hidden = jax.nn.gelu(jnp.dot(pooled, squeeze_w, precision=PRECISE) + squeeze_b, approximate=False)
    logits = jnp.dot(hidden, expand_w, precision=PRECISE) + expand_b
    logits = logits.reshape(logits.shape[0], -1, 3)
    weights = jax.nn.softmax(logits, axis=-1)
    return h_branch * weights[:, None, None, :, 0] + w_branch * weights[:, None, None, :, 1] + c_branch * weights[:, None, None, :, 2]

def product(left_op, right_op):
    return jnp.einsum('...k,km->...m', left_op, right_op, precision=PRECISE)

def patches(grid_in):
    side_len = grid_in.shape[1]
    padded = jnp.pad(grid_in, ((0, 0), (1, 1), (1, 1), (0, 0)))
    pieces = []
    for row_off in range(3):
        for col_off in range(3):
            pieces.append(padded[:, row_off:row_off + side_len:2, col_off:col_off + side_len:2, :])
    return jnp.concatenate(pieces, axis=-1)

def layer_forward(state, valid_mask, counts, params):
    normed = low(layer_norm(state, params[8][0], params[9][0]))
    h_branch = low_back(product(cycle_shift(normed, 1, 1), params[0][0]) + params[1][0])
    w_branch = low_back(product(cycle_shift(normed, 2, 1), params[0][1]) + params[1][1])
    c_branch = low_back(product(normed, params[0][2]))
    mixed = low(reweight_mix(h_branch, w_branch, c_branch, params[2], params[3], params[4], params[5], valid_mask, counts))
    token_out = low_back(product(mixed, params[6]) + params[7])
    halfway = state + valid_mask * token_out
    normed2 = low(layer_norm(halfway, params[8][1], params[9][1]))
    pre_act = low_back(product(normed2, params[10]) + params[11])
    hidden = low(jax.nn.gelu(pre_act, approximate=False))
    channel_out = low_back(product(hidden, params[12]) + params[13])
    return halfway + valid_mask * channel_out

def reference(images, valid_sizes, cotangent, mix_weight, mix_bias, squeeze_weight, squeeze_bias, expand_weight, expand_bias, project_weight, project_bias, norm_gain, norm_bias, inner_weight, inner_bias, outer_weight, outer_bias, merge_weight, merge_bias):
    valid_mask = pixel_mask(valid_sizes, SIDE)
    counts = (valid_sizes[:, 0] * valid_sizes[:, 1]).astype(jnp.float32)
    listed = [mix_weight, mix_bias, squeeze_weight, squeeze_bias, expand_weight, expand_bias, project_weight, project_bias, norm_gain, norm_bias, inner_weight, inner_bias, outer_weight, outer_bias, merge_weight, merge_bias]
    floats = [array.astype(jnp.float32) for array in listed]

    def forward(image_vals, *params):
        state = image_vals * valid_mask
        for layer_at in range(LAYERS):
            state = layer_forward(state, valid_mask, counts, [array[layer_at] for array in params[:14]])
        final_low = low(state)
        merged = product(patches(final_low), params[14]) + params[15]
        return merged.reshape(merged.shape[0], SIDE // 2, SIDE // 2 * OUT)
    merged, pullback = jax.vjp(forward, images.astype(jnp.float32), *floats)
    gradients = pullback(cotangent.astype(jnp.float32))
    return (merged.astype(jnp.bfloat16), gradients[0], gradients[1], gradients[2], gradients[3], gradients[4], gradients[5], gradients[6], gradients[7], gradients[8], gradients[9], gradients[10], gradients[11], gradients[12], gradients[13], gradients[14], gradients[15], gradients[16])
```

```python
from functools import partial

import jax
import jax.numpy as jnp
from jax import lax
from jax.experimental import pallas as pl
from jax.experimental.pallas import tpu as pltpu
from jax.sharding import PartitionSpec as P

F32 = jnp.float32
BF16 = jnp.bfloat16
PRECISE = lax.Precision.HIGHEST
GROUP = 8


def dot(a, b, dims=(1, 0), precision=None):
    return lax.dot_general(
        a, b, (((dims[0],), (dims[1],)), ((), ())), precision=precision, preferred_element_type=F32
    )


def fine(a, b, dims=(1, 0)):
    return dot(a, b, dims, PRECISE)


def rows8(v):
    return v.reshape(-1, 8, v.shape[-1]).sum(axis=0)


def gelu_pair(x):
    d = 1.0 + jnp.abs(x) * (0.3275911 * 0.7071067811865476)
    t = pl.reciprocal(d, approx=True)
    t = t * (2.0 - d * t)
    bell = jnp.exp(x * x * -0.5)
    poly = 0.5 * 1.061405429
    for coef in (-1.453152027, 1.421413741, -0.284496736, 0.254829592):
        poly = poly * t + 0.5 * coef
    tail = poly * t * bell
    cdf = jnp.where(x >= 0.0, 1.0 - tail, tail)
    return x * cdf, cdf + x * bell * 0.3989422804014327


def norm_parts(v):
    mean = jnp.mean(v, axis=-1, keepdims=True)
    centred = v - mean
    rstd = lax.rsqrt(jnp.mean(centred * centred, axis=-1, keepdims=True) + 1e-05)
    return centred * rstd, rstd


def norm_back(grad, unit, rstd, gain):
    scaled = grad * gain
    first = jnp.mean(scaled, axis=-1, keepdims=True)
    second = jnp.mean(scaled * unit, axis=-1, keepdims=True)
    return rstd * (scaled - first - unit * second)


class Sizes:
    def __init__(self, images, side, channels, hidden, red, out, layers):
        self.I, self.side, self.C, self.H, self.R, self.O, self.L = images, side, channels, hidden, red, out, layers
        self.pitch = -(-(side + 1) // 8) * 8
        self.N = side * self.pitch
        self.per = 6 if side % 6 == 0 else 2
        self.CH = self.per * self.pitch
        self.chunks = side // self.per
        self.half = side // 2
        self.hp = -(-self.half // 8) * 8
        self.base = 8 + self.pitch
        self.tall = 8 + self.pitch * (2 * self.hp + 2)


def pick(z, low, mid, high):
    kind = lax.broadcasted_iota(jnp.int32, (8, z.C), 1) % 3
    kind = jnp.broadcast_to(kind[None], (mid.shape[0] // 8, 8, z.C)).reshape(mid.shape)
    return jnp.where(kind == 2, low, jnp.where(kind == 0, mid, high))


def over(z, body):
    def step(c, carry):
        body(pl.multiple_of(c * z.CH, 16), c)
        return carry
    lax.fori_loop(0, z.chunks, step, 0)


def setup_phase(z, r):
    r.nrm[...] = jnp.zeros_like(r.nrm)
    r.sg[...] = jnp.zeros_like(r.sg)
    r.gw[...] = jnp.zeros_like(r.gw)
    cols = lax.broadcasted_iota(jnp.int32, (z.per, z.pitch, z.C), 1)
    r.colmask[...] = jnp.where(cols < z.side, 1.0, 0.0).reshape(z.CH, z.C)
    for i in range(z.I):
        high, wide = r.sizes[i, 0], r.sizes[i, 1]
        r.state[i, :, 32:, :] = jnp.zeros((z.side, z.pitch - 32, z.C), F32)

        def body(at, c, i=i, high=high, wide=wide):
            cols = lax.broadcasted_iota(jnp.int32, (z.per, z.pitch, z.C), 1)
            rows = lax.broadcasted_iota(jnp.int32, (z.per, z.pitch, z.C), 0) + c * z.per
            mask = jnp.where((cols < wide) & (rows < high), 1.0, 0.0)
            r.mask[i, pl.ds(at, z.CH), :] = mask.reshape(z.CH, z.C)
            take = r.images[i, pl.ds(c * z.per, z.per)].astype(F32)
            r.state[i, pl.ds(c * z.per, z.per), : z.side, :] = take * mask[:, : z.side]

        over(z, body)
    spots = lax.broadcasted_iota(jnp.int32, (3 * z.C, 3 * z.C), 0)
    ends = lax.broadcasted_iota(jnp.int32, (3 * z.C, 3 * z.C), 1)
    kind = ends // z.C
    r.perm[...] = jnp.where(spots == 3 * (ends - kind * z.C) + kind, 1.0, 0.0)
    for l in range(z.L):
        r.ewp[l] = fine(r.expand_weight[l], r.perm[...])
    r.ebp[...] = fine(r.expand_bias[...], r.perm[...])


def counts_of(z, r):
    rows = []
    for i in range(GROUP):
        if i < z.I:
            count = (r.sizes[i, 0] * r.sizes[i, 1]).astype(F32)
            rows.append(jnp.full((1, z.C), 1.0, F32) * count)
        else:
            rows.append(jnp.ones((1, z.C), F32))
    return jnp.concatenate(rows, axis=0)


def state_chunk(z, r, i, c):
    return r.state[i, pl.ds(c * z.per, z.per)].reshape(z.CH, z.C)


def norm_phase(z, r, l, i):
    gain, bias = r.norm_gain[l, 0:1], r.norm_bias[l, 0:1]

    def body(at, c):
        unit, rstd = norm_parts(state_chunk(z, r, i, c))
        r.xh1[l, i, pl.ds(at, z.CH), :] = unit
        r.rs1[l, i, pl.ds(at, z.CH), :] = jnp.broadcast_to(rstd, unit.shape)
        normed = (unit * gain + bias) * r.colmask[...]
        r.nrm[i, pl.ds(z.base + at, z.CH), :] = normed

    over(z, body)


def shift_phase(z, r, l, i):
    r.sums[...] = jnp.zeros_like(r.sums)

    def body(at, c):
        def view(off):
            return r.nrm[i, pl.ds(z.base + at + off, z.CH), :]
        mid = view(0)
        high = pick(z, view(-z.pitch), mid, view(z.pitch)).astype(BF16)
        wide = pick(z, view(-1), mid, view(1)).astype(BF16)
        mid = mid.astype(BF16)
        mask = r.mask[i, pl.ds(at, z.CH), :]
        for j, part in enumerate((high, wide, mid)):
            r.cat[l, i, pl.ds(at, z.CH), j * z.C : (j + 1) * z.C] = part
            r.sums[j] += rows8(part.astype(F32) * mask)

    over(z, body)
    for j in range(3):
        r.pool[l, j, i : i + 1] = r.sums[j].sum(axis=0, keepdims=True)


def weigh_phase(z, r, l):
    counts = counts_of(z, r)
    total = fine(r.pool[l, 0], r.mix_weight[l, 0].astype(F32))
    for j in (1, 2):
        total += fine(r.pool[l, j], r.mix_weight[l, j].astype(F32))
    pooled = total / counts + r.mix_bias[l, 0:1] + r.mix_bias[l, 1:2]
    r.pooled[l] = pooled
    act, slope = gelu_pair(fine(pooled, r.squeeze_weight[l]) + r.squeeze_bias[l : l + 1])
    r.act[l] = act
    r.slope[l] = slope
    logits = fine(act, r.ewp[l]) + r.ebp[l : l + 1]
    parts = [logits[:, j * z.C : (j + 1) * z.C] for j in range(3)]
    top = jnp.maximum(jnp.maximum(parts[0], parts[1]), parts[2])
    parts = [jnp.exp(part - top) for part in parts]
    whole = parts[0] + parts[1] + parts[2]
    for j in range(3):
        r.share[l, j] = parts[j] / whole
    for i in range(z.I):
        for j in range(3):
            scaled = r.mix_weight[l, j].astype(F32) * r.share[l, j, i : i + 1]
            r.wp[l, i, j * z.C : (j + 1) * z.C, :] = scaled.astype(BF16)


def mix_phase(z, r, l, i):
    bias = r.mix_bias[l, 0:1] * r.share[l, 0, i : i + 1] + r.mix_bias[l, 1:2] * r.share[l, 1, i : i + 1]
    gain2, bias2 = r.norm_gain[l, 1:2], r.norm_bias[l, 1:2]

    def body(at, c):
        rows = pl.ds(at, z.CH)
        mixed = (dot(r.cat[l, i, rows, :], r.wp[l, i]) + bias).astype(BF16)
        r.mixed[l, i, rows, :] = mixed
        token = dot(mixed, r.project_weight[l]) + r.project_bias[l : l + 1]
        halfway = state_chunk(z, r, i, c) + r.mask[i, rows, :] * token
        unit, rstd = norm_parts(halfway)
        r.xh2[l, i, rows, :] = unit
        r.rs2[l, i, rows, :] = jnp.broadcast_to(rstd, unit.shape)
        r.n2[l, i, rows, :] = (unit * gain2 + bias2).astype(BF16)
        r.state[i, pl.ds(c * z.per, z.per)] = halfway.reshape(z.per, z.pitch, z.C)

    over(z, body)


def feed_phase(z, r, l, i):
    def body(at, c):
        rows = pl.ds(at, z.CH)
        pre = dot(r.n2[l, i, rows, :], r.inner_weight[l]) + r.inner_bias[l : l + 1].astype(F32)
        act, slope = gelu_pair(pre)
        act = act.astype(BF16)
        r.hid[l, i, rows, :] = act
        r.gp[l, i, rows, :] = slope.astype(BF16)
        out = dot(act, r.outer_weight[l]) + r.outer_bias[l : l + 1]
        after = state_chunk(z, r, i, c) + r.mask[i, rows, :] * out
        r.state[i, pl.ds(c * z.per, z.per)] = after.reshape(z.per, z.pitch, z.C)

    over(z, body)


def merge_forward(z, r, i):
    def body(at, c):
        low = state_chunk(z, r, i, c)
        r.nrm[i, pl.ds(z.base + at, z.CH), :] = low

    over(z, body)
    for pair in range(z.half // 2):
        for k in range(9):
            dr, ds = divmod(k, 3)
            two = [
                r.nrm[i, pl.ds(8 + dr * z.pitch + 2 * b + ds - 1, z.hp, stride=2 * z.pitch), :]
                for b in (2 * pair, 2 * pair + 1)
            ]
            r.patch[i, 2 * pair * z.hp : (2 * pair + 2) * z.hp, k * z.C : (k + 1) * z.C] = jnp.concatenate(
                two, axis=0
            ).astype(BF16)
    for pair in range(z.half // 2):
        rows = slice(2 * pair * z.hp, (2 * pair + 2) * z.hp)
        merged = dot(r.patch[i, rows, :], r.merge_weight[...]) + r.merge_bias[...]
        wide = jnp.concatenate([merged[: z.half], merged[z.hp : z.hp + z.half]], axis=1)
        r.features[i, :, 2 * pair * z.O : (2 * pair + 2) * z.O] = wide.astype(BF16)


def merge_backward(z, r, i):
    pad = jnp.zeros((z.hp - z.half, z.O), F32)
    for pair in range(z.half // 2):
        wide = r.cotangent[i, :, 2 * pair * z.O : (2 * pair + 2) * z.O].astype(F32)
        both = jnp.concatenate([wide[:, : z.O], pad, wide[:, z.O :], pad], axis=0)
        r.cot[i, 2 * pair * z.hp : (2 * pair + 2) * z.hp, :] = both.astype(BF16)
        r.gmb[...] += rows8(both)
    for pair in range(z.half // 2):
        rows = slice(2 * pair * z.hp, (2 * pair + 2) * z.hp)
        r.pgrad[rows, :] = dot(r.cot[i, rows, :], r.merge_weight[...], (1, 1))

    def part(dr, ds, b, down=0):
        k = 3 * dr + ds
        return r.pgrad[pl.ds(b * z.hp + down, z.hp), k * z.C : (k + 1) * z.C]

    for b in range(z.half):
        last = b == z.half - 1
        planes = [
            part(1, 1, b),
            part(2, 1, b) + part(0, 1, b, 1),
            part(1, 2, b),
            part(2, 2, b) + part(0, 2, b, 1),
        ]
        if not last:
            planes[2] += part(1, 0, b + 1)
            planes[3] += part(2, 0, b + 1) + part(0, 0, b + 1, 1)
        for plane, start in zip(planes, (2 * b, z.pitch + 2 * b, 2 * b + 1, z.pitch + 2 * b + 1)):
            r.sg[i, pl.ds(start, z.hp, stride=2 * z.pitch), :] = plane


def merge_weights(z, r):
    total = dot(r.patch[0], r.cot[0], (0, 0))
    for i in range(1, z.I):
        total += dot(r.patch[i], r.cot[i], (0, 0))
    r.gmw[...] = total


def feed_back(z, r, l, i):
    gain2 = r.norm_gain[l, 1:2]

    def body(at, c):
        rows = pl.ds(at, z.CH)
        mask = r.mask[i, rows, :]
        grad = r.sg[i, rows, :]
        cg = (grad * mask).astype(BF16)
        r.vec[0] += rows8(cg.astype(F32))
        slope = r.gp[l, i, rows, :]
        pg = (dot(cg, r.outer_weight[l], (1, 1)) * slope.astype(F32)).astype(BF16)
        r.gib[...] += rows8(pg.astype(F32))
        r.gwo[...] += dot(cg, r.hid[l, i, rows, :], (0, 0))
        r.gwi[...] += dot(r.n2[l, i, rows, :], pg, (0, 0))
        ng = dot(pg, r.inner_weight[l], (1, 1))
        unit = r.xh2[l, i, rows, :]
        r.vec[1] += rows8(ng * unit)
        r.vec[2] += rows8(ng)
        grad = grad + norm_back(ng, unit, r.rs2[l, i, rows, :], gain2)
        r.sg[i, rows, :] = grad
        tg = (grad * mask).astype(BF16)
        r.vec[3] += rows8(tg.astype(F32))
        r.gpw[...] += dot(r.mixed[l, i, rows, :], tg, (0, 0))
        mg = dot(tg, r.project_weight[l], (1, 1)).astype(BF16)
        r.mg[i, rows, :] = mg
        r.smg[i] += rows8(mg.astype(F32))
        r.gt[i] += dot(mg, r.cat[l, i, rows, :], (0, 0))

    over(z, body)


def clear_layer(z, r):
    for ref in (r.vec, r.gib, r.gwo, r.gwi, r.gpw, r.smg, r.gt):
        ref[...] = jnp.zeros_like(ref)


def weigh_back(z, r, l):
    counts = counts_of(z, r)
    zeros = jnp.zeros((GROUP - z.I, z.C), F32)
    smg = jnp.concatenate([r.smg[i].sum(axis=0, keepdims=True) for i in range(z.I)] + [zeros], axis=0)
    share = [r.share[l, j] for j in range(3)]
    dp = []
    for j in range(3):
        weight = r.mix_weight[l, j].astype(F32)
        rows = []
        for i in range(z.I):
            tile = r.gt[i, :, j * z.C : (j + 1) * z.C].T
            rows.append((weight * tile).sum(axis=0, keepdims=True))
            if i == 0:
                r.g_mix_weight[l, j] = tile * share[j][i : i + 1]
            else:
                r.g_mix_weight[l, j] += tile * share[j][i : i + 1]
        dp.append(jnp.concatenate(rows + [zeros], axis=0))
    for j in range(2):
        dp[j] += smg * r.mix_bias[l, j : j + 1]
    even = dp[0] * share[0] + dp[1] * share[1] + dp[2] * share[2]
    dz = jnp.concatenate([share[j] * (dp[j] - even) for j in range(3)], axis=1)
    act, slope, pooled = r.act[l], r.slope[l], r.pooled[l]
    r.g_expand_weight[l] = fine(fine(act, dz, (0, 0)), r.perm[...], (1, 1))
    r.g_expand_bias[l : l + 1] = fine(dz, r.perm[...], (1, 1)).sum(axis=0, keepdims=True)
    dact = fine(dz, r.ewp[l], (1, 1)) * slope
    r.g_squeeze_weight[l] = fine(pooled, dact, (0, 0))
    r.g_squeeze_bias[l : l + 1] = dact.sum(axis=0, keepdims=True)
    dpool = fine(dact, r.squeeze_weight[l], (1, 1))
    push = dpool / counts
    for j in range(3):
        r.g_mix_weight[l, j] += fine(r.pool[l, j], push, (0, 0))
        r.push[j] = fine(push, r.mix_weight[l, j].astype(F32), (1, 1))
    for j in range(2):
        r.g_mix_bias[l, j : j + 1] = (share[j] * smg + dpool).sum(axis=0, keepdims=True)
    r.g_project_weight[l] = r.gpw[...]
    r.g_project_bias[l : l + 1] = r.vec[3].sum(axis=0, keepdims=True)
    r.g_outer_bias[l : l + 1] = r.vec[0].sum(axis=0, keepdims=True)
    r.g_norm_gain[l, 1:2] = r.vec[1].sum(axis=0, keepdims=True)
    r.g_norm_bias[l, 1:2] = r.vec[2].sum(axis=0, keepdims=True)
    r.g_inner_bias[l : l + 1] = r.gib[...].sum(axis=0, keepdims=True)
    r.g_feed[l, 0] = r.gwi[...].T
    r.g_feed[l, 1] = r.gwo[...].T


def mix_back(z, r, l, i):
    def body(at, c):
        rows = pl.ds(at, z.CH)
        mask = r.mask[i, rows, :]
        parts = dot(r.mg[i, rows, :], r.wp[l, i], (1, 1))
        for j, ref in enumerate((r.nrm, r.gw, r.gc)):
            ref[i, pl.ds(z.base + at, z.CH), :] = (
                parts[:, j * z.C : (j + 1) * z.C] + mask * r.push[j, i : i + 1]
            )

    over(z, body)


def norm_back_phase(z, r, l, i, images_grad=None):
    gain = r.norm_gain[l, 0:1]

    def body(at, c):
        rows = pl.ds(at, z.CH)

        def view(ref, off):
            return ref[i, pl.ds(z.base + at + off, z.CH), :]

        ng = (
            pick(z, view(r.nrm, z.pitch), view(r.nrm, 0), view(r.nrm, -z.pitch))
            + pick(z, view(r.gw, 1), view(r.gw, 0), view(r.gw, -1))
            + view(r.gc, 0)
        )
        unit = r.xh1[l, i, rows, :]
        r.vec[4] += rows8(ng * unit)
        r.vec[5] += rows8(ng * r.colmask[...])
        grad = r.sg[i, rows, :] + norm_back(ng, unit, r.rs1[l, i, rows, :], gain)
        if images_grad is None:
            r.sg[i, rows, :] = grad
        else:
            grad = (grad * r.mask[i, rows, :]).reshape(z.per, z.pitch, z.C)
            images_grad[i, pl.ds(c * z.per, z.per)] = grad[:, : z.side]

    over(z, body)


class Refs:
    pass


ARGS = (
    "images", "sizes", "cotangent", "mix_weight", "mix_bias", "squeeze_weight", "squeeze_bias", "expand_weight",
    "expand_bias", "project_weight", "project_bias", "norm_gain", "norm_bias", "inner_parts", "bias_parts",
    "outer_parts", "outer_bias", "merge_weight", "merge_bias",
)


def outputs_of(z):
    return {
        "features": ((z.I, z.half, z.half * z.O), BF16),
        "images_grad": ((z.I, z.side, z.side, z.C), F32),
        "feed": ((z.parts, 2 * z.L * z.units, z.C), BF16),
        "shared": ((z.total, z.C), BF16),
    }


def layout(z):
    at, where = 0, {}
    for name, rows in (
        ("mix", 3 * z.L * z.C), ("project", z.L * z.C), ("merge", 9 * z.C * 5 // 2), ("squeeze", z.C),
        ("expand", 3 * z.L * z.R), ("small", 64),
    ):
        where[name] = at
        at += rows
    return where, at


SMALL = ("mix_bias", "project_bias", "norm_gain", "norm_bias", "outer_bias", "inner_bias", "expand_bias", "merge_bias", "squeeze_bias")


def pack_phase(z, r):
    where, _ = layout(z)

    def put(at, value):
        r.shared[at : at + value.shape[0], :] = value.astype(BF16)

    for l in range(z.L):
        for j in range(3):
            put(where["mix"] + (3 * l + j) * z.C, r.g_mix_weight[l, j])
            put(where["expand"] + (3 * l + j) * z.R, r.g_expand_weight[l, :, j * z.C : (j + 1) * z.C])
        put(where["project"] + l * z.C, r.g_project_weight[l])
        for k in range(2):
            for h in range(z.parts):
                r.feed[h, (2 * l + k) * z.units : (2 * l + k + 1) * z.units, :] = r.g_feed[l, k, h * z.units : (h + 1) * z.units].astype(BF16)
    wide = 9 * z.C
    put(where["merge"], r.gmw[:, : z.C])
    put(where["merge"] + wide, r.gmw[:, z.C : 2 * z.C])
    put(where["merge"] + 2 * wide, jnp.concatenate([r.gmw[: wide // 2, 2 * z.C :], r.gmw[wide // 2 :, 2 * z.C :]], axis=1))
    put(where["squeeze"], jnp.concatenate([r.g_squeeze_weight[l] for l in range(z.L)] + [jnp.zeros((z.C, z.C - z.L * z.R), F32)], axis=1))
    rows = []
    for l in range(z.L):
        rows += [r.g_mix_bias[l], r.g_project_bias[l : l + 1], r.g_norm_gain[l], r.g_norm_bias[l], r.g_outer_bias[l : l + 1]]
        rows += [r.g_inner_bias[l : l + 1, k * z.C : (k + 1) * z.C] for k in range(z.H // z.C)]
        rows += [r.g_expand_bias[l : l + 1, k * z.C : (k + 1) * z.C] for k in range(3)]
    bias = r.gmb[...].sum(axis=0, keepdims=True)
    rows += [bias[:, : z.C], bias[:, z.C : 2 * z.C]]
    rows += [jnp.concatenate([bias[:, 2 * z.C :], r.g_squeeze_bias[0:1], r.g_squeeze_bias[1:2]], axis=1)]
    rows += [jnp.zeros((64 - sum(row.shape[0] for row in rows), z.C), F32)]
    put(where["small"], jnp.concatenate(rows, axis=0))


def final_outputs(z):
    return {
        "mix_weight": (z.L, 3, z.C, z.C),
        "mix_bias": (z.L, 2, z.C),
        "squeeze_weight": (z.L, z.C, z.R),
        "squeeze_bias": (z.L, z.R),
        "expand_weight": (z.L, z.R, 3 * z.C),
        "expand_bias": (z.L, 3 * z.C),
        "project_weight": (z.L, z.C, z.C),
        "project_bias": (z.L, z.C),
        "norm_gain": (z.L, 2, z.C),
        "norm_bias": (z.L, 2, z.C),
        "inner_weight": (z.L, z.C, z.units),
        "inner_bias": (z.L, z.H),
        "outer_weight": (z.L, z.units, z.C),
        "outer_bias": (z.L, z.C),
        "merge_weight": (9 * z.C, z.O),
        "merge_bias": (1, z.O),
    }


def unpack_kernel(z, shared, feed, *outs):
    where, _ = layout(z)
    o = Refs()
    for name, ref in zip(final_outputs(z), outs):
        setattr(o, name, ref)

    def get(at, rows):
        return shared[at : at + rows, :].astype(F32)

    small = get(where["small"], 64)
    at = 0
    squeeze = get(where["squeeze"], z.C)

    def take(rows):
        nonlocal at
        at += rows
        return small[at - rows : at]

    for l in range(z.L):
        for j in range(3):
            o.mix_weight[l, j] = get(where["mix"] + (3 * l + j) * z.C, z.C)
            o.expand_weight[l, :, j * z.C : (j + 1) * z.C] = get(where["expand"] + (3 * l + j) * z.R, z.R)
        o.project_weight[l] = get(where["project"] + l * z.C, z.C)
        o.squeeze_weight[l] = squeeze[:, l * z.R : (l + 1) * z.R]
        o.inner_weight[l] = feed[2 * l * z.units : (2 * l + 1) * z.units, :].astype(F32).T
        o.outer_weight[l] = feed[(2 * l + 1) * z.units : (2 * l + 2) * z.units, :].astype(F32)
        o.mix_bias[l] = take(2)
        o.project_bias[l : l + 1] = take(1)
        o.norm_gain[l] = take(2)
        o.norm_bias[l] = take(2)
        o.outer_bias[l : l + 1] = take(1)
        for k in range(z.H // z.C):
            o.inner_bias[l : l + 1, k * z.C : (k + 1) * z.C] = take(1)
        for k in range(3):
            o.expand_bias[l : l + 1, k * z.C : (k + 1) * z.C] = take(1)
    wide = 9 * z.C
    o.merge_weight[:, : z.C] = get(where["merge"], wide)
    o.merge_weight[:, z.C : 2 * z.C] = get(where["merge"] + wide, wide)
    pair = get(where["merge"] + 2 * wide, wide // 2)
    o.merge_weight[: wide // 2, 2 * z.C :] = pair[:, : z.O - 2 * z.C]
    o.merge_weight[wide // 2 :, 2 * z.C :] = pair[:, z.O - 2 * z.C :]
    o.merge_bias[:, : z.C] = take(1)
    o.merge_bias[:, z.C : 2 * z.C] = take(1)
    last = take(1)
    o.merge_bias[:, 2 * z.C :] = last[:, : z.O - 2 * z.C]
    for l in range(z.L):
        o.squeeze_bias[l : l + 1] = last[:, z.O - 2 * z.C + l * z.R : z.O - 2 * z.C + (l + 1) * z.R]


def scratch_of(z):
    return {
        "g_mix_weight": ((z.L, 3, z.C, z.C), F32),
        "g_mix_bias": ((z.L, 2, z.C), F32),
        "g_squeeze_weight": ((z.L, z.C, z.R), F32),
        "g_squeeze_bias": ((z.L, z.R), F32),
        "g_expand_weight": ((z.L, z.R, 3 * z.C), F32),
        "g_expand_bias": ((z.L, 3 * z.C), F32),
        "g_project_weight": ((z.L, z.C, z.C), F32),
        "g_project_bias": ((z.L, z.C), F32),
        "g_norm_gain": ((z.L, 2, z.C), F32),
        "g_norm_bias": ((z.L, 2, z.C), F32),
        "g_feed": ((z.L, 2, z.H, z.C), F32),
        "g_inner_bias": ((z.L, z.H), F32),
        "g_outer_bias": ((z.L, z.C), F32),
        "gmw": ((9 * z.C, z.O), F32),
        "gmb": ((8, z.O), F32),
        "inner_weight": ((z.L, z.C, z.H), BF16),
        "inner_bias": ((z.L, z.H), F32),
        "outer_weight": ((z.L, z.H, z.C), BF16),
        "nrm": ((z.I, z.tall, z.C), F32),
        "state": ((z.I, z.side, z.pitch, z.C), F32),
        "mask": ((z.I, z.N, z.C), F32),
        "colmask": ((z.CH, z.C), F32),
        "sg": ((z.I, 2 * z.hp * z.pitch, z.C), F32),
        "xh1": ((z.L, z.I, z.N, z.C), F32),
        "rs1": ((z.L, z.I, z.N, z.C), F32),
        "xh2": ((z.L, z.I, z.N, z.C), F32),
        "rs2": ((z.L, z.I, z.N, z.C), F32),
        "cat": ((z.L, z.I, z.N, 3 * z.C), BF16),
        "mixed": ((z.L, z.I, z.N, z.C), BF16),
        "n2": ((z.L, z.I, z.N, z.C), BF16),
        "hid": ((z.L, z.I, z.N, z.H), BF16),
        "gp": ((z.L, z.I, z.N, z.H), BF16),
        "sums": ((3, 8, z.C), F32),
        "pool": ((z.L, 3, GROUP, z.C), F32),
        "pooled": ((z.L, GROUP, z.C), F32),
        "act": ((z.L, GROUP, z.R), F32),
        "slope": ((z.L, GROUP, z.R), F32),
        "share": ((z.L, 3, GROUP, z.C), F32),
        "wp": ((z.L, z.I, 3 * z.C, z.C), BF16),
        "perm": ((3 * z.C, 3 * z.C), F32),
        "ewp": ((z.L, z.R, 3 * z.C), F32),
        "ebp": ((z.L, 3 * z.C), F32),
        "patch": ((z.I, z.half * z.hp, 9 * z.C), BF16),
        "cot": ((z.I, z.half * z.hp, z.O), BF16),
        "pgrad": ((z.half * z.hp + 8, 9 * z.C), F32),
        "vec": ((6, 8, z.C), F32),
        "gib": ((8, z.H), F32),
        "gwo": ((z.C, z.H), F32),
        "gwi": ((z.C, z.H), F32),
        "gpw": ((z.C, z.C), F32),
        "smg": ((z.I, 8, z.C), F32),
        "gt": ((z.I, z.C, 3 * z.C), F32),
        "mg": ((z.I, z.N, z.C), BF16),
        "push": ((3, GROUP, z.C), F32),
        "gw": ((z.I, z.base + z.N + z.pitch, z.C), F32),
        "gc": ((z.I, z.base + z.N, z.C), F32),
    }


def kernel(z, outs, scratch, *refs):
    r = Refs()
    for name, ref in zip(list(ARGS) + list(outs) + list(scratch), refs):
        setattr(r, name, ref)
    images = range(z.I)
    todo = []
    todo.append(("setup", lambda: setup_phase(z, r)))
    todo.append(("gather", lambda: gather_phase(z, r)))
    for l in range(z.L):
        todo.append((f"norm{l}", lambda l=l: [norm_phase(z, r, l, i) for i in images]))
        todo.append((f"shift{l}", lambda l=l: [shift_phase(z, r, l, i) for i in images]))
        todo.append((f"weigh{l}", lambda l=l: weigh_phase(z, r, l)))
        todo.append((f"mix{l}", lambda l=l: [mix_phase(z, r, l, i) for i in images]))
        todo.append((f"feed{l}", lambda l=l: [feed_phase(z, r, l, i) for i in images]))
    todo.append(("mergef", lambda: [merge_forward(z, r, i) for i in images]))

    def clear():
        r.gmb[...] = jnp.zeros_like(r.gmb)
        r.pgrad[...] = jnp.zeros_like(r.pgrad)
    todo.append(("clear", clear))
    todo.append(("mergeb", lambda: [merge_backward(z, r, i) for i in images]))
    todo.append(("mergew", lambda: merge_weights(z, r)))
    for l in reversed(range(z.L)):
        todo.append((f"clear{l}", lambda l=l: clear_layer(z, r)))
        todo.append((f"feedb{l}", lambda l=l: [feed_back(z, r, l, i) for i in images]))
        todo.append((f"weighb{l}", lambda l=l: weigh_back(z, r, l)))
        todo.append((f"mixb{l}", lambda l=l: [mix_back(z, r, l, i) for i in images]))

        def normb(l=l):
            for i in images:
                norm_back_phase(z, r, l, i, r.images_grad if l == 0 else None)
            r.g_norm_gain[l, 0:1] = r.vec[4].sum(axis=0, keepdims=True)
            r.g_norm_bias[l, 0:1] = r.vec[5].sum(axis=0, keepdims=True)
        todo.append((f"normb{l}", normb))
    todo.append(("pack", lambda: pack_phase(z, r)))
    for name, phase in todo:
        phase()


def gather_phase(z, r):
    for l in range(z.L):
        r.inner_weight[l] = jnp.concatenate([r.inner_parts[h, l] for h in range(z.parts)], axis=1)
        r.inner_bias[l : l + 1] = jnp.concatenate([r.bias_parts[h, l : l + 1].astype(F32) for h in range(z.parts)], axis=1)
        for h in range(z.parts):
            r.outer_weight[l, h * z.units : (h + 1) * z.units, :] = r.outer_parts[h, l]


def run_kernel(args, z):
    outs, scratch = outputs_of(z), scratch_of(z)
    vmem = pl.BlockSpec(memory_space=pltpu.VMEM)
    smem = pl.BlockSpec(memory_space=pltpu.SMEM)
    found = pl.pallas_call(
        partial(kernel, z, outs, scratch),
        out_shape=[jax.ShapeDtypeStruct(s, d) for s, d in outs.values()],
        in_specs=[smem if name == "sizes" else vmem for name in ARGS],
        out_specs=[vmem] * len(outs),
        scratch_shapes=[pltpu.VMEM(s, d) for s, d in scratch.values()],
        compiler_params=pltpu.CompilerParams(vmem_limit_bytes=62 * 2**20),
    )(*args)
    return dict(zip(outs, found))


def run_unpack(shared, feed, z):
    outs = final_outputs(z)
    vmem = pl.BlockSpec(memory_space=pltpu.VMEM)
    found = pl.pallas_call(
        partial(unpack_kernel, z),
        out_shape=[jax.ShapeDtypeStruct(s, F32) for s in outs.values()],
        in_specs=[vmem] * 2,
        out_specs=[vmem] * len(outs),
        compiler_params=pltpu.CompilerParams(vmem_limit_bytes=32 * 2**20),
    )(shared, feed)
    return dict(zip(outs, found))


def scatter_sum(x, axis, n):
    got = lax.all_to_all(x, axis, 0, 0, tiled=True)
    return got.reshape(n, -1, x.shape[-1]).astype(F32).sum(axis=0).astype(BF16)


def share_sum(x, axis, n):
    total = x.astype(F32)
    for step in range(1, n):
        total += lax.ppermute(x, axis, [(a, (a + step) % n) for a in range(n)]).astype(F32)
    return total.astype(BF16)


def per_device(
    img, hid, images, sizes, cotangent, mix_weight, mix_bias, squeeze_weight, squeeze_bias, expand_weight, expand_bias,
    project_weight, project_bias, norm_gain, norm_bias, inner_weight, inner_bias, outer_weight, outer_bias,
    merge_weight, merge_bias,
):
    z = Sizes(
        images.shape[0], images.shape[1], images.shape[3], inner_weight.shape[2] * hid, squeeze_weight.shape[2],
        merge_weight.shape[1], mix_weight.shape[0],
    )
    z.parts, z.units = hid, inner_weight.shape[2]
    step = hid * 16
    z.total = -(-layout(z)[1] // step) * step
    inner_parts, bias_parts, outer_parts = (
        lax.all_gather(part, "hid", axis=0) for part in (inner_weight, inner_bias, outer_weight)
    )
    found = run_kernel(
        (
            images, sizes, cotangent, mix_weight, mix_bias, squeeze_weight, squeeze_bias, expand_weight, expand_bias,
            project_weight, project_bias, norm_gain, norm_bias, inner_parts, bias_parts, outer_parts, outer_bias,
            merge_weight, merge_bias.reshape(1, -1),
        ),
        z,
    )
    feed = share_sum(scatter_sum(found["feed"].reshape(-1, z.C), "hid", hid), "img", img)
    shared = share_sum(scatter_sum(found["shared"], "hid", hid), "img", img)
    shared = lax.all_gather(shared, "hid", axis=0, tiled=True)
    g = run_unpack(shared, feed, z)
    inner_bias_grad = lax.dynamic_slice_in_dim(g["inner_bias"], lax.axis_index("hid") * z.units, z.units, axis=1)
    return (
        found["features"], found["images_grad"], g["mix_weight"], g["mix_bias"], g["squeeze_weight"], g["squeeze_bias"],
        g["expand_weight"], g["expand_bias"], g["project_weight"], g["project_bias"], g["norm_gain"], g["norm_bias"],
        g["inner_weight"], inner_bias_grad, g["outer_weight"], g["outer_bias"], g["merge_weight"],
        g["merge_bias"].reshape(-1),
    )


def solution(mesh):
    maps = ("img", "hid")
    in_specs = (
        P(maps, None, None, None), P(maps, None), P(maps, None, None), P(), P(), P(), P(), P(), P(), P(), P(), P(), P(),
        P(None, None, "hid"), P(None, "hid"), P(None, "hid", None), P(), P(), P(),
    )
    out_specs = (
        P(maps, None, None), P(maps, None, None, None), P(), P(), P(), P(), P(), P(), P(), P(), P(), P(),
        P(None, None, "hid"), P(None, "hid"), P(None, "hid", None), P(), P(), P(),
    )
    return jax.shard_map(
        partial(per_device, mesh.shape["img"], mesh.shape["hid"]),
        mesh=mesh, in_specs=in_specs, out_specs=out_specs, check_vma=False,
    )
```

```python
from functools import partial

import jax
import jax.numpy as jnp
from jax import lax
from jax.experimental import pallas as pl
from jax.experimental.pallas import tpu as pltpu
from jax.sharding import PartitionSpec as P

F32 = jnp.float32
BF16 = jnp.bfloat16
PRECISE = lax.Precision.HIGHEST
GROUP = 8
MIB = 2**20


def dot(a, b, dims=(1, 0), precision=None):
    return lax.dot_general(
        a, b, (((dims[0],), (dims[1],)), ((), ())), precision=precision, preferred_element_type=F32
    )


def fine(a, b, dims=(1, 0)):
    return dot(a, b, dims, PRECISE)


def rows8(v):
    return v.reshape(-1, 8, v.shape[-1]).sum(axis=0)


def total(v):
    return v.sum(axis=0, keepdims=True)


def tile(v, rows):
    return jnp.broadcast_to(v[None], (rows // 8, 8, v.shape[-1])).reshape(rows, v.shape[-1])


def gelu_pair(x):
    cdf = 0.5 * lax.erf(x * 0.7071067811865476) + 0.5
    bell = jnp.exp2(x * x * (-0.5 * 1.4426950408889634))
    return x * cdf, cdf + x * bell * 0.3989422804014327


def norm_parts(v, ones):
    high = v.astype(BF16)
    low = (v - high.astype(F32)).astype(BF16)
    centred = v - dot(jnp.concatenate([high, low], axis=1), ones)
    rstd = lax.rsqrt(dot((centred * centred).astype(BF16), ones[: v.shape[1]]) + 1e-05)
    return centred * rstd, rstd


def norm_back(grad, unit, rstd, gain, ones):
    width = grad.shape[1]
    scaled = grad * gain
    first = dot(scaled.astype(BF16), ones[:width])
    second = dot((scaled * unit).astype(BF16), ones[:width])
    return rstd * (scaled - first - unit * second)


def mean_matrix(z):
    return jnp.full((2 * z.C, z.C), 1.0 / z.C, BF16)


class Sizes:
    def __init__(self, images, side, channels, hidden, red, out, layers, parts):
        self.I, self.side, self.C, self.H, self.R, self.O, self.L = images, side, channels, hidden, red, out, layers
        self.parts, self.units = parts, hidden // parts
        self.W = side * images
        self.N0 = side * self.W
        self.CH = 384
        self.N = -(-self.N0 // self.CH) * self.CH
        self.chunks = self.N // self.CH
        self.half = side // 2
        self.hp = -(-self.half // 8) * 8
        self.M = self.half * self.hp
        self.base = self.W
        self.tall = self.W * (2 * self.hp + 2)
        self.long = self.base + self.N + self.W
        self.at_project = 3 * channels
        self.at_expand = self.at_project + channels
        self.at_squeeze = self.at_expand + 3 * red
        self.at_small = self.at_squeeze + red
        self.shared = -(-(self.at_small + 16) // (16 * parts)) * 16
        self.merge = -(-(9 * out + 3) // (16 * parts)) * 16


class Refs:
    pass


def call(body, ins, outs, scratch, limit, smem=()):
    vmem = pl.BlockSpec(memory_space=pltpu.VMEM)
    scalar = pl.BlockSpec(memory_space=pltpu.SMEM)
    names = list(ins) + list(outs) + list(scratch)

    def kernel(*refs):
        r = Refs()
        for name, ref in zip(names, refs):
            setattr(r, name, ref)
        body(r)

    found = pl.pallas_call(
        kernel,
        out_shape=list(outs.values()),
        in_specs=[scalar if name in smem else vmem for name in ins],
        out_specs=[vmem] * len(outs),
        scratch_shapes=list(scratch.values()),
        compiler_params=pltpu.CompilerParams(vmem_limit_bytes=limit * MIB),
    )(*ins.values())
    return dict(zip(outs, found))


def arr(*shape, dtype=F32):
    return jax.ShapeDtypeStruct(shape, dtype)


def kept(*shape, dtype=F32):
    return pltpu.VMEM(shape, dtype)


def over(z, body):
    def step(c, carry):
        body(pl.ds(pl.multiple_of(c * z.CH, 128), z.CH), c * z.CH)
        return carry

    lax.fori_loop(0, z.chunks, step, 0)


def near(ref, start, off, size):
    return ref[pl.ds(start + off, size), :]


def parity(z, i):
    rows = lax.broadcasted_iota(jnp.int32, (8, z.C), 0)
    return jnp.where(rows % z.I == i, 1.0, 0.0)


def kinds(z, rows):
    return tile(lax.broadcasted_iota(jnp.int32, (8, z.C), 1) % 3, rows)


def weave(z, v):
    out = v[0:1] * parity(z, 0)
    for i in range(1, z.I):
        out += v[i : i + 1] * parity(z, i)
    return out


def split(z, v):
    rows = [total(v * parity(z, i)) for i in range(z.I)]
    return jnp.concatenate(rows + [jnp.zeros((GROUP - z.I, z.C), F32)], axis=0)


def front_kernel(z, r):
    rows = lax.broadcasted_iota(jnp.int32, (z.W, z.C), 0)
    lanes = lax.broadcasted_iota(jnp.int32, (z.W, z.C), 1) % 3
    image = rows % z.I
    col = rows // z.I
    high = jnp.zeros((z.W, z.C), jnp.int32)
    wide = jnp.zeros((z.W, z.C), jnp.int32)
    for i in range(z.I):
        high = jnp.where(image == i, r.sizes[i, 0], high)
        wide = jnp.where(image == i, r.sizes[i, 1], wide)
    inside = jnp.where(col < wide, 1.0, 0.0)
    first, last = col == 0, col == z.side - 1
    edge = jnp.where((first & (lanes == 2)) | (last & (lanes == 1)), 0.0, 1.0)
    back = jnp.where((last & (lanes == 2)) | (first & (lanes == 1)), 0.0, 1.0)

    def step(row, carry):
        at = pl.ds(pl.multiple_of(row * z.W, 8), z.W)
        r.mask[at, :] = jnp.where(high > row, inside, 0.0)
        r.edge[at, :] = edge
        r.back[at, :] = back
        return carry

    lax.fori_loop(0, z.side, step, 0)
    pad = jnp.zeros((z.N - z.N0, z.C), F32)
    for ref in (r.mask, r.edge, r.back):
        ref[z.N0 :, :] = pad
    pad = jnp.zeros((z.hp - z.half, z.O), F32)
    r.pgrad[z.M :, :] = jnp.zeros((8, 9 * z.C), F32)
    sums = jnp.zeros((8, z.O), F32)
    for i in range(z.I):
        for pair in range(z.half // 2):
            both = r.cotangent[i, :, 2 * pair * z.O : (2 * pair + 2) * z.O].astype(F32)
            both = jnp.concatenate([both[:, : z.O], pad, both[:, z.O :], pad], axis=0)
            at = i * z.M + 2 * pair * z.hp
            r.cot[at : at + 2 * z.hp, :] = both.astype(BF16)
            sums += rows8(both)
        step = z.M // 2
        for at in range(0, z.M, step):
            r.pgrad[at : at + step, :] = dot(r.cot[i * z.M + at : i * z.M + at + step, :], r.merge_weight[...])

        def part(dr, ds, b, down=0):
            k = 3 * dr + ds
            return r.pgrad[pl.ds(b * z.hp + down, z.hp), k * z.C : (k + 1) * z.C]

        for b in range(z.half):
            planes = [
                part(1, 1, b),
                part(2, 1, b) + part(0, 1, b, 1),
                part(1, 2, b),
                part(2, 2, b) + part(0, 2, b, 1),
            ]
            if b < z.half - 1:
                planes[2] += part(1, 0, b + 1)
                planes[3] += part(2, 0, b + 1) + part(0, 0, b + 1, 1)
            for plane, (down, right) in zip(planes, ((0, 0), (1, 0), (0, 1), (1, 1))):
                start = down * z.W + (2 * b + right) * z.I + i
                r.grad[pl.ds(start, z.hp, stride=2 * z.W), :] = plane
    r.merge_bias_sums[...] = sums


def shift_phase(z, r, cat):
    r.sums[...] = jnp.zeros_like(r.sums)

    def body(rows, at):
        start = z.base + at
        kind = kinds(z, z.CH)
        mid = near(r.normed, start, 0, z.CH)
        high = jnp.where(kind == 2, near(r.normed, start, -z.W, z.CH), near(r.normed, start, z.W, z.CH))
        wide = jnp.where(kind == 2, near(r.normed, start, -z.I, z.CH), near(r.normed, start, z.I, z.CH))
        high = jnp.where(kind == 0, mid, high).astype(BF16)
        wide = jnp.where(kind == 0, mid, wide * r.edge[rows, :]).astype(BF16)
        mask = r.mask[rows, :]
        for j, piece in enumerate((high, wide, mid.astype(BF16))):
            cat[rows, j * z.C : (j + 1) * z.C] = piece
            r.sums[j] += rows8(piece.astype(F32) * mask)

    over(z, body)


def counts_of(z, r):
    rows = []
    for i in range(GROUP):
        count = (r.sizes[i, 0] * r.sizes[i, 1]).astype(F32) if i < z.I else 1.0
        rows.append(jnp.full((1, z.C), 1.0, F32) * count)
    return jnp.concatenate(rows, axis=0)


def weigh_phase(z, r, l, o):
    pooled = r.mix_bias[l, 0:1] + r.mix_bias[l, 1:2]
    counts = counts_of(z, r)
    for j in range(3):
        pool = split(z, r.sums[j])
        o.pool[j] = pool
        pooled = pooled + fine(pool, r.mix_weight[l, j].astype(F32)) / counts
    o.pooled[...] = pooled
    act, slope = gelu_pair(fine(pooled, r.squeeze_weight[l], (1, 1)) + r.squeeze_bias[l : l + 1])
    o.act[...] = act
    o.slope[...] = slope
    logits = fine(act, r.ewp[l]) + r.ebp[l : l + 1]
    parts = [logits[:, j * z.C : (j + 1) * z.C] for j in range(3)]
    top = jnp.maximum(jnp.maximum(parts[0], parts[1]), parts[2])
    parts = [jnp.exp(part - top) for part in parts]
    whole = parts[0] + parts[1] + parts[2]
    for j in range(3):
        o.share[j] = parts[j] / whole


def mix_phase(z, r, l, o):
    ones = mean_matrix(z)
    share = [weave(z, o.share[j]) for j in range(3)]
    bias = tile(r.mix_bias[l, 0:1] * share[0] + r.mix_bias[l, 1:2] * share[1], z.CH)
    share = [tile(s, z.CH) for s in share]
    gain, shift = r.norm_gain[l, 1:2], r.norm_bias[l, 1:2]

    def body(rows, at):
        mixed = bias
        for j in range(3):
            mixed = mixed + dot(o.cat[rows, j * z.C : (j + 1) * z.C], r.mix_weight[l, j]) * share[j]
        mixed = mixed.astype(BF16)
        o.mixed[rows, :] = mixed
        token = dot(mixed, r.project_weight[l]) + r.project_bias[l : l + 1]
        halfway = r.state[rows, :] + r.mask[rows, :] * token
        unit, rstd = norm_parts(halfway, ones)
        o.unit2[rows, :] = unit
        o.rstd2[rows, :] = rstd
        o.normed2[rows, :] = (unit * gain + shift).astype(BF16)
        r.state[rows, :] = halfway

    over(z, body)


def norm_store(z, r, l, o, rows, at, state):
    unit, rstd = norm_parts(state, mean_matrix(z))
    o.unit1[rows, :] = unit
    o.rstd1[rows, :] = rstd
    r.normed[pl.ds(z.base + at, z.CH), :] = unit * r.norm_gain[l, 0:1] + r.norm_bias[l, 0:1]


def clear_edges(z, ref):
    ref[: z.base, :] = jnp.zeros((z.base, z.C), F32)
    ref[z.base + z.N0 :, :] = jnp.zeros((ref.shape[0] - z.base - z.N0, z.C), F32)


def feed_phase(z, r, l, o, after):
    def body(rows, at):
        pre = dot(o.normed2[rows, :], r.inner[l], (1, 1)) + r.inner_bias[l : l + 1]
        act, slope = gelu_pair(pre)
        act = act.astype(BF16)
        o.act_rows[rows, :] = act
        o.slope_rows[rows, :] = slope.astype(BF16)
        out = dot(act, r.outer[l]) + r.outer_bias[l : l + 1]
        state = r.state[rows, :] + r.mask[rows, :] * out
        after(rows, at, state)

    over(z, body)


def saved_early(z):
    return dict(
        unit1=kept(z.N, z.C), rstd1=kept(z.N, z.C), cat=kept(z.N, 3 * z.C, dtype=BF16), mixed=kept(z.N, z.C, dtype=BF16),
        unit2=kept(z.N, z.C), rstd2=kept(z.N, z.C), normed2=kept(z.N, z.C, dtype=BF16), pool=kept(3, GROUP, z.C),
        pooled=kept(GROUP, z.C), act=kept(GROUP, z.R), slope=kept(GROUP, z.R), share=kept(3, GROUP, z.C),
    )


def saved_late(z):
    return dict(act_rows=kept(z.N, z.H, dtype=BF16), slope_rows=kept(z.N, z.H, dtype=BF16))


def first_kernel(z, r):
    spots = lax.broadcasted_iota(jnp.int32, (3 * z.C, 3 * z.C), 0)
    ends = lax.broadcasted_iota(jnp.int32, (3 * z.C, 3 * z.C), 1)
    kind = jnp.where(ends >= 2 * z.C, 2, jnp.where(ends >= z.C, 1, 0))
    r.perm[...] = jnp.where(spots == 3 * (ends - kind * z.C) + kind, 1.0, 0.0)
    for l in range(z.L):
        r.ewp[l] = fine(r.expand_weight[l], r.perm[...])
    r.ebp[...] = fine(r.expand_bias[...], r.perm[...])
    whole = z.N0 // z.CH

    def step(c, carry):
        rows = pl.ds(pl.multiple_of(c * z.CH, 128), z.CH)
        state = r.images[rows, :].astype(F32) * r.mask[rows, :]
        r.state[rows, :] = state
        norm_store(z, r, 0, r, rows, c * z.CH, state)
        return carry

    lax.fori_loop(0, whole, step, 0)
    if whole < z.chunks:
        at = whole * z.CH
        left = z.N0 - at
        tail = r.images[at:, :].astype(F32) * r.mask[at : z.N0, :]
        state = jnp.concatenate([tail, jnp.zeros((z.CH - left, z.C), F32)], axis=0)
        r.state[at:, :] = state
        norm_store(z, r, 0, r, pl.ds(at, z.CH), at, state)
    clear_edges(z, r.normed)
    shift_phase(z, r, r.cat)
    weigh_phase(z, r, 0, r)
    mix_phase(z, r, 0, r)


def second_kernel(z, r):
    for h in range(z.parts):
        for l in range(z.L):
            at = h * z.units
            r.inner[l, at : at + z.units, :] = r.gathered[h, 2 * l * z.units : (2 * l + 1) * z.units, :]
            r.outer[l, at : at + z.units, :] = r.gathered[h, (2 * l + 1) * z.units : (2 * l + 2) * z.units, :]
    for l in range(z.L):
        row = 2 * z.L * z.units + l
        r.inner_bias[l : l + 1] = jnp.concatenate(
            [r.gathered[h, row : row + 1, : z.units].astype(F32) for h in range(z.parts)], axis=1
        )
    early, late = [Refs() for _ in range(z.L)], [Refs() for _ in range(z.L)]
    for l in range(z.L):
        early[l].normed2 = r.normed2_0 if l == 0 else r.normed2
        early[l].act_rows = r.act_rows_0 if l == 0 else r.act_rows
        early[l].slope_rows = r.slope_rows_0 if l == 0 else r.slope_rows

    def then_norm(rows, at, state):
        r.state[rows, :] = state
        norm_store(z, r, 1, r, rows, at, state)

    r.state[...] = r.state_in[...]
    feed_phase(z, r, 0, early[0], then_norm)
    clear_edges(z, r.normed)
    shift_phase(z, r, r.cat)
    weigh_phase(z, r, 1, r)
    mix_phase(z, r, 1, r)

    def then_keep(rows, at, state):
        r.normed[pl.ds(z.base + at, z.CH), :] = state

    feed_phase(z, r, 1, early[1], then_keep)
    for i in range(z.I):
        for pair in range(z.half // 2):
            at = i * z.M + 2 * pair * z.hp
            for k in range(9):
                dr, ds = divmod(k, 3)
                two = []
                for b in (2 * pair, 2 * pair + 1):
                    col = 2 * b + ds - 1
                    if col < 0:
                        two.append(jnp.zeros((z.hp, z.C), F32))
                    else:
                        two.append(r.normed[pl.ds(dr * z.W + col * z.I + i, z.hp, stride=2 * z.W), :])
                r.patch[at : at + 2 * z.hp, k * z.C : (k + 1) * z.C] = jnp.concatenate(two, axis=0).astype(BF16)
    for i in range(z.I):
        for pair in range(z.half // 2):
            at = i * z.M + 2 * pair * z.hp
            merged = dot(r.patch[at : at + 2 * z.hp, :], r.merge_weight[...], (1, 1)) + r.merge_bias[...]
            wide = jnp.concatenate([merged[: z.half], merged[z.hp : z.hp + z.half]], axis=1)
            r.features[i, :, 2 * pair * z.O : (2 * pair + 2) * z.O] = wide.astype(BF16)
    for k in range(9):
        grad = dot(r.cot[...], r.patch[:, k * z.C : (k + 1) * z.C], (0, 0))
        r.merge_rows[k * z.O : (k + 1) * z.O, :] = grad.astype(BF16)
    bias = total(r.merge_bias_sums[...])
    rest = z.O - 2 * z.C
    rows = [bias[:, : z.C], bias[:, z.C : 2 * z.C]]
    rows += [jnp.concatenate([bias[:, 2 * z.C :], jnp.zeros((1, z.C - rest), F32)], axis=1)]
    rows += [jnp.zeros((z.parts * z.merge - 9 * z.O - 3, z.C), F32)]
    r.merge_rows[9 * z.O :, :] = jnp.concatenate(rows, axis=0).astype(BF16)


def feed_back_kernel(z, l, r):
    ones = mean_matrix(z)
    gain = r.norm_gain[l, 1:2]
    sums = (r.vec, r.inner_sums, r.g_outer, r.g_inner, r.g_project, r.g_mix)
    for ref in sums:
        ref[...] = jnp.zeros_like(ref)
    even, odd = tile(parity(z, 0), z.CH), tile(parity(z, 1), z.CH)

    def body(rows, at):
        mask = r.mask[rows, :]
        grad = r.grad[rows, :]
        out = (grad * mask).astype(BF16)
        r.vec[0] += rows8(out.astype(F32))
        pre = (dot(out, r.outer[l], (1, 1)) * r.slope_rows[rows, :].astype(F32)).astype(BF16)
        r.inner_sums[...] += rows8(pre.astype(F32))
        r.g_outer[...] += dot(out, r.act_rows[rows, :], (0, 0))
        r.g_inner[...] += dot(r.normed2[rows, :], pre, (0, 0))
        normed_grad = dot(pre, r.inner[l])
        unit = r.unit2[rows, :]
        r.vec[1] += rows8(normed_grad * unit)
        r.vec[2] += rows8(normed_grad)
        grad = grad + norm_back(normed_grad, unit, r.rstd2[rows, :], gain, ones)
        r.half_grad[rows, :] = grad
        token = (grad * mask).astype(BF16)
        r.vec[3] += rows8(token.astype(F32))
        r.g_project[...] += dot(r.mixed[rows, :], token, (0, 0))
        mixed_grad = dot(token, r.project_weight[l], (1, 1))
        r.vec[4] += rows8(mixed_grad)
        both = jnp.concatenate([(mixed_grad * even).astype(BF16), (mixed_grad * odd).astype(BF16)], axis=1)
        r.mixed_grad[rows, :] = both
        r.g_mix[...] += dot(both, r.cat[rows, :], (0, 0))

    over(z, body)
    counts = counts_of(z, r)
    zeros = jnp.zeros((GROUP - z.I, z.C), F32)
    summed = split(z, r.vec[4])
    share = [r.share[j] for j in range(3)]
    mix, dp = [], []
    for j in range(3):
        weight = r.mix_weight[l, j].astype(F32)
        rows = []
        found = 0.0
        for i in range(z.I):
            block = r.g_mix[i * z.C : (i + 1) * z.C, j * z.C : (j + 1) * z.C].T
            rows.append(total(weight * block))
            found = found + block * share[j][i : i + 1]
            scaled = weight * share[j][i : i + 1]
            r.scaled[j * z.C : (j + 1) * z.C, i * z.C : (i + 1) * z.C] = scaled.astype(BF16)
        mix.append(found)
        dp.append(jnp.concatenate(rows + [zeros], axis=0))
    for j in range(2):
        dp[j] += summed * r.mix_bias[l, j : j + 1]
    even = dp[0] * share[0] + dp[1] * share[1] + dp[2] * share[2]
    dz = jnp.concatenate([share[j] * (dp[j] - even) for j in range(3)], axis=1)
    act, slope, pooled = r.act[...], r.slope[...], r.pooled[...]
    expand = fine(fine(act, dz, (0, 0)), r.perm[...], (1, 1))
    expand_bias = total(fine(dz, r.perm[...], (1, 1)))
    dact = fine(dz, r.ewp[l], (1, 1)) * slope
    squeeze = fine(dact, pooled, (0, 0))
    dpool = fine(dact, r.squeeze_weight[l])
    push = dpool / counts
    for j in range(3):
        mix[j] += fine(r.pool[j], push, (0, 0))
        r.push[j] = weave(z, fine(push, r.mix_weight[l, j].astype(F32), (1, 1)))
    for j in range(3):
        r.rows[j * z.C : (j + 1) * z.C, :] = mix[j].astype(BF16)
    r.rows[z.at_project : z.at_expand, :] = r.g_project[...].astype(BF16)
    for j in range(3):
        at = z.at_expand + j * z.R
        r.rows[at : at + z.R, :] = expand[:, j * z.C : (j + 1) * z.C].astype(BF16)
    r.rows[z.at_squeeze : z.at_small, :] = squeeze.astype(BF16)
    inner = total(r.inner_sums[...])
    small = [total(share[j] * summed + dpool) for j in range(2)]
    small += [total(r.vec[k]) for k in (3, 0, 1, 2)]
    small += [inner[:, k * z.C : (k + 1) * z.C] for k in range(z.H // z.C)]
    small += [expand_bias[:, j * z.C : (j + 1) * z.C] for j in range(3)]
    small += [jnp.concatenate([total(dact), jnp.zeros((1, z.C - z.R), F32)], axis=1)]
    small += [jnp.zeros((z.parts * z.shared - z.at_small - len(small), z.C), F32)]
    r.rows[z.at_small :, :] = jnp.concatenate(small, axis=0).astype(BF16)
    inner, outer = r.g_inner[...].T, r.g_outer[...].T
    u = z.units
    for h in range(z.parts):
        r.blocks[h, :u, :] = inner[h * u : (h + 1) * u].astype(BF16)
        r.blocks[h, u : 2 * u, :] = outer[h * u : (h + 1) * u].astype(BF16)
        r.blocks[h, 2 * u :, :] = r.rows[h * z.shared : (h + 1) * z.shared, :]


def mix_back_kernel(z, l, last, r):
    ones = mean_matrix(z)
    for ref in (r.back_h, r.back_w):
        clear_edges(z, ref)
    gain = r.norm_gain[l, 0:1]
    push = [tile(r.push[j], z.CH) for j in range(3)]

    def spread(rows, at):
        mask = r.mask[rows, :]
        parts = dot(r.mixed_grad[rows, :], r.scaled[...], (1, 1))
        for j, ref in enumerate((r.back_h, r.back_w, r.back_c)):
            ref[pl.ds(z.base + at, z.CH), :] = parts[:, j * z.C : (j + 1) * z.C] + mask * push[j]

    over(z, spread)
    r.vec[...] = jnp.zeros_like(r.vec)

    def body(rows, at):
        start = z.base + at
        kind = kinds(z, z.CH)
        high = jnp.where(kind == 2, near(r.back_h, start, z.W, z.CH), near(r.back_h, start, -z.W, z.CH))
        wide = jnp.where(kind == 2, near(r.back_w, start, z.I, z.CH), near(r.back_w, start, -z.I, z.CH))
        high = jnp.where(kind == 0, near(r.back_h, start, 0, z.CH), high)
        wide = jnp.where(kind == 0, near(r.back_w, start, 0, z.CH), wide * r.back[rows, :])
        grad = high + wide + near(r.back_c, start, 0, z.CH)
        unit = r.unit1[rows, :]
        r.vec[0] += rows8(grad * unit)
        r.vec[1] += rows8(grad)
        grad = r.half_grad[rows, :] + norm_back(grad, unit, r.rstd1[rows, :], gain, ones)
        if not last:
            r.state_grad[rows, :] = grad
            return
        grad = grad * r.mask[rows, :]
        left = z.N0 - (z.chunks - 1) * z.CH

        @pl.when(at < z.N0 - z.CH + 1)
        def _():
            r.state_grad[rows, :] = grad

        @pl.when(at > z.N0 - z.CH)
        def _():
            r.state_grad[z.N0 - left :, :] = grad[:left]

    over(z, body)
    stray = r.back_h[z.base + z.N0 - z.W : z.base + z.N0, :]
    r.vec[1] -= rows8(jnp.where(kinds(z, z.W) == 1, stray, 0.0))
    r.first_norm[...] = jnp.concatenate([total(r.vec[0]), total(r.vec[1])], axis=0)


def final_outputs(z):
    return dict(
        mix_weight=arr(z.L, 3, z.C, z.C), mix_bias=arr(z.L, 2, z.C), squeeze_weight=arr(z.L, z.R, z.C),
        squeeze_bias=arr(z.L, z.R), expand_weight=arr(z.L, z.R, 3 * z.C), expand_bias=arr(z.L, 3 * z.C),
        project_weight=arr(z.L, z.C, z.C), project_bias=arr(z.L, z.C), norm_gain=arr(z.L, 2, z.C),
        norm_bias=arr(z.L, 2, z.C), inner_weight=arr(z.L, z.units, z.C), inner_bias=arr(z.L, z.H),
        outer_weight=arr(z.L, z.units, z.C), outer_bias=arr(z.L, z.C), merge_weight=arr(z.O, 9 * z.C),
        merge_bias=arr(1, z.O),
    )


def last_kernel(z, r):
    for l in range(z.L):
        rows = r.shared_rows.at[l]

        def get(at, count):
            return rows[at : at + count, :].astype(F32)

        for j in range(3):
            r.mix_weight[l, j] = get(j * z.C, z.C)
            r.expand_weight[l, :, j * z.C : (j + 1) * z.C] = get(z.at_expand + j * z.R, z.R)
        r.project_weight[l] = get(z.at_project, z.C)
        r.squeeze_weight[l] = get(z.at_squeeze, z.R)
        small = get(z.at_small, 16)
        r.mix_bias[l] = small[0:2]
        r.project_bias[l : l + 1] = small[2:3]
        r.outer_bias[l : l + 1] = small[3:4]
        r.norm_gain[l] = jnp.concatenate([r.norms[2 * l : 2 * l + 1, :].astype(F32), small[4:5]], axis=0)
        r.norm_bias[l] = jnp.concatenate([r.norms[2 * l + 1 : 2 * l + 2, :].astype(F32), small[5:6]], axis=0)
        at = 6
        for k in range(z.H // z.C):
            r.inner_bias[l : l + 1, k * z.C : (k + 1) * z.C] = small[at : at + 1]
            at += 1
        for j in range(3):
            r.expand_bias[l : l + 1, j * z.C : (j + 1) * z.C] = small[at : at + 1]
            at += 1
        r.squeeze_bias[l : l + 1] = small[at : at + 1, : z.R]
        r.inner_weight[l] = r.feed_rows[l, : z.units, :].astype(F32)
        r.outer_weight[l] = r.feed_rows[l, z.units :, :].astype(F32)
    for k in range(9):
        r.merge_weight[:, k * z.C : (k + 1) * z.C] = r.merge_rows[k * z.O : (k + 1) * z.O, :].astype(F32)
    small = r.merge_rows[9 * z.O : 9 * z.O + 16, :].astype(F32)
    r.merge_bias[:, : z.C] = small[0:1]
    r.merge_bias[:, z.C : 2 * z.C] = small[1:2]
    r.merge_bias[:, 2 * z.C :] = small[2:3, : z.O - 2 * z.C]


def swap(x, axis, n, bit):
    return lax.ppermute(x, axis, [(a, a ^ bit) for a in range(n)])


def bits_of(n):
    return [1 << k for k in range(n.bit_length() - 1)]


def scatter_bits(x, axis, n):
    me = lax.axis_index(axis)
    for bit in bits_of(n):
        mine = (me // bit) % 2
        x = x.reshape((-1, 2) + x.shape[1:])
        away = lax.dynamic_index_in_dim(x, 1 - mine, 1, keepdims=False)
        here = lax.dynamic_index_in_dim(x, mine, 1, keepdims=False)
        x = (here.astype(F32) + swap(away, axis, n, bit).astype(F32)).astype(BF16)
    return x[0]


def sum_bits(x, axis, n):
    for bit in bits_of(n):
        x = (x.astype(F32) + swap(x, axis, n, bit).astype(F32)).astype(BF16)
    return x


def gather_bits(x, axis, n, order):
    me = lax.axis_index(axis)
    have = x[None]
    dims = []
    for bit in order:
        got = swap(have, axis, n, bit)
        mine = (me // bit) % 2
        have = jnp.where(mine == 0, jnp.stack([have, got]), jnp.stack([got, have]))
        dims.append(bit)
    count = len(dims)
    have = have.reshape((2,) * count + x.shape)
    place = [count - 1 - dims.index(bit) for bit in sorted(dims, reverse=True)]
    have = have.transpose(place + list(range(count, have.ndim)))
    return have.reshape((n,) + x.shape)


def per_device(
    img, hid, images, sizes, cotangent, mix_weight, mix_bias, squeeze_weight, squeeze_bias, expand_weight, expand_bias,
    project_weight, project_bias, norm_gain, norm_bias, inner_weight, inner_bias, outer_weight, outer_bias,
    merge_weight, merge_bias,
):
    z = Sizes(
        images.shape[0], images.shape[1], images.shape[3], inner_weight.shape[2] * hid, squeeze_weight.shape[2],
        merge_weight.shape[1], mix_weight.shape[0], hid,
    )
    flat = images.transpose(1, 2, 0, 3).reshape(z.N0, z.C)
    merge_t = merge_weight.T
    squeeze_t = squeeze_weight.transpose(0, 2, 1)
    block = jnp.stack([inner_weight.transpose(0, 2, 1), outer_weight], axis=1).reshape(-1, z.C)
    bias_rows = jnp.pad(inner_bias, ((0, 16 - z.L), (0, z.C - z.units)))
    block = jnp.concatenate([block, bias_rows], axis=0)
    order = bits_of(hid)[1:] + [1]
    gathered = gather_bits(block, "hid", hid, order)
    smem = dict(sizes=0)
    small = dict(
        mix_weight=mix_weight, mix_bias=mix_bias, squeeze_weight=squeeze_t, squeeze_bias=squeeze_bias,
        project_weight=project_weight, project_bias=project_bias, norm_gain=norm_gain, norm_bias=norm_bias,
    )
    a = call(
        partial(front_kernel, z),
        dict(sizes=sizes, cotangent=cotangent, merge_weight=merge_t),
        dict(
            mask=kept(z.N, z.C), edge=kept(z.N, z.C), back=kept(z.N, z.C), cot=kept(z.I * z.M, z.O, dtype=BF16),
            grad=kept(z.tall, z.C), merge_bias_sums=kept(8, z.O),
        ),
        dict(pgrad=kept(z.M + 8, 9 * z.C)),
        12, smem,
    )
    b = call(
        partial(first_kernel, z),
        dict(
            images=flat, sizes=sizes, mask=a["mask"], edge=a["edge"], expand_weight=expand_weight, expand_bias=expand_bias,
            **small,
        ),
        dict(
            state=kept(z.N, z.C), perm=kept(3 * z.C, 3 * z.C), ewp=kept(z.L, z.R, 3 * z.C), ebp=kept(z.L, 3 * z.C),
            **saved_early(z),
        ),
        dict(normed=kept(z.long, z.C), sums=kept(3, 8, z.C)),
        12, smem,
    )
    late = saved_late(z)
    c = call(
        partial(second_kernel, z),
        dict(
            sizes=sizes, mask=a["mask"], edge=a["edge"], state_in=b["state"], normed2_0=b["normed2"], gathered=gathered,
            ewp=b["ewp"], ebp=b["ebp"], outer_bias=outer_bias, merge_weight=merge_t, merge_bias=merge_bias.reshape(1, -1),
            cot=a["cot"], merge_bias_sums=a["merge_bias_sums"], **small,
        ),
        dict(
            features=arr(z.I, z.half, z.half * z.O, dtype=BF16),
            merge_rows=arr(z.parts * z.merge, z.C, dtype=BF16),
            inner=kept(z.L, z.H, z.C, dtype=BF16), outer=kept(z.L, z.H, z.C, dtype=BF16),
            act_rows_0=late["act_rows"], slope_rows_0=late["slope_rows"], **saved_early(z), **late,
        ),
        dict(
            state=kept(z.N, z.C), normed=kept(z.tall, z.C), sums=kept(3, 8, z.C), inner_bias=kept(z.L, z.H),
            patch=kept(z.I * z.M, 9 * z.C, dtype=BF16),
        ),
        16, smem,
    )
    first = dict(b, act_rows=c["act_rows_0"], slope_rows=c["slope_rows_0"])
    grad, blocks, norms = a["grad"], [None] * z.L, [None] * z.L
    for l in reversed(range(z.L)):
        s = c if l else first
        d = call(
            partial(feed_back_kernel, z, l),
            dict(
                sizes=sizes, mask=a["mask"], grad=grad, inner=c["inner"], outer=c["outer"], perm=b["perm"], ewp=b["ewp"],
                **{
                    name: s[name]
                    for name in dict(
                        act_rows=0, slope_rows=0, normed2=0, unit2=0, rstd2=0, mixed=0, cat=0, share=0, pool=0, pooled=0,
                        act=0, slope=0,
                    )
                },
                **small,
            ),
            dict(
                half_grad=kept(z.N, z.C), mixed_grad=kept(z.N, z.I * z.C, dtype=BF16),
                scaled=kept(3 * z.C, z.I * z.C, dtype=BF16), push=kept(3, 8, z.C),
                blocks=arr(z.parts, 2 * z.units + z.shared, z.C, dtype=BF16),
            ),
            dict(
                vec=kept(5, 8, z.C), inner_sums=kept(8, z.H), g_outer=kept(z.C, z.H), g_inner=kept(z.C, z.H),
                g_project=kept(z.C, z.C), g_mix=kept(z.I * z.C, 3 * z.C), rows=kept(z.parts * z.shared, z.C, dtype=BF16),
            ),
            12, smem,
        )
        blocks[l] = d["blocks"]
        e = call(
            partial(mix_back_kernel, z, l, l == 0),
            dict(
                mask=a["mask"], back=a["back"], mixed_grad=d["mixed_grad"], scaled=d["scaled"], push=d["push"],
                unit1=s["unit1"], rstd1=s["rstd1"], half_grad=d["half_grad"], norm_gain=norm_gain,
            ),
            dict(state_grad=kept(z.N, z.C) if l else arr(z.N0, z.C), first_norm=arr(2, z.C)),
            dict(back_h=kept(z.long, z.C), back_w=kept(z.long, z.C), back_c=kept(z.long, z.C), vec=kept(2, 8, z.C)),
            12,
        )
        grad, norms[l] = e["state_grad"], e["first_norm"]
    images_grad = grad.reshape(z.side, z.side, z.I, z.C).transpose(2, 0, 1, 3)

    back = bits_of(hid)[::-1]
    merge_rows = sum_bits(scatter_bits(c["merge_rows"].reshape(hid, z.merge, z.C), "hid", hid), "img", img)
    merge_rows = gather_bits(merge_rows, "hid", hid, back).reshape(hid * z.merge, z.C)
    both = jnp.stack(blocks, axis=1)
    norm_rows = jnp.pad(jnp.concatenate(norms, axis=0), ((0, 16 - 2 * z.L), (0, 0))).astype(BF16)
    norm_rows = jnp.broadcast_to(norm_rows[None], (hid, 16, z.C))
    every = jnp.concatenate([both.reshape(hid, -1, z.C), norm_rows], axis=1)
    every = sum_bits(scatter_bits(every, "hid", hid), "img", img)
    norm_rows = every[-16:]
    every = every[:-16].reshape(z.L, 2 * z.units + z.shared, z.C)
    feed_rows = every[:, : 2 * z.units]
    shared_rows = gather_bits(every[:, 2 * z.units :], "hid", hid, back)
    shared_rows = shared_rows.transpose(1, 0, 2, 3).reshape(z.L, hid * z.shared, z.C)
    g = call(
        partial(last_kernel, z),
        dict(shared_rows=shared_rows, feed_rows=feed_rows, merge_rows=merge_rows, norms=norm_rows),
        final_outputs(z), {}, 16,
    )
    inner_bias_grad = lax.dynamic_slice_in_dim(g["inner_bias"], lax.axis_index("hid") * z.units, z.units, axis=1)
    return (
        c["features"], images_grad, g["mix_weight"], g["mix_bias"], g["squeeze_weight"].transpose(0, 2, 1),
        g["squeeze_bias"], g["expand_weight"], g["expand_bias"], g["project_weight"], g["project_bias"], g["norm_gain"],
        g["norm_bias"], g["inner_weight"].transpose(0, 2, 1), inner_bias_grad, g["outer_weight"], g["outer_bias"],
        g["merge_weight"].T, g["merge_bias"].reshape(-1),
    )


def solution(mesh):
    maps = ("img", "hid")
    in_specs = (
        P(maps, None, None, None), P(maps, None), P(maps, None, None), P(), P(), P(), P(), P(), P(), P(), P(), P(), P(),
        P(None, None, "hid"), P(None, "hid"), P(None, "hid", None), P(), P(), P(),
    )
    out_specs = (
        P(maps, None, None), P(maps, None, None, None), P(), P(), P(), P(), P(), P(), P(), P(), P(), P(),
        P(None, None, "hid"), P(None, "hid"), P(None, "hid", None), P(), P(), P(),
    )
    return jax.shard_map(
        partial(per_device, mesh.shape["img"], mesh.shape["hid"]),
        mesh=mesh, in_specs=in_specs, out_specs=out_specs, check_vma=False,
    )
```

```python
from functools import partial

import jax
import jax.numpy as jnp
from jax import lax
from jax.experimental import pallas as pl
from jax.experimental.pallas import tpu as pltpu
from jax.sharding import PartitionSpec as P

F32 = jnp.float32
BF16 = jnp.bfloat16
GROUP = 8
MIB = 2**20


def dot(a, b, dims=(1, 0)):
    return lax.dot_general(a, b, (((dims[0],), (dims[1],)), ((), ())), preferred_element_type=F32)


def halves(v):
    high = v.astype(BF16)
    return high, (v - high.astype(F32)).astype(BF16)


def fine(a, b, dims=(1, 0)):
    high, low = halves(a)
    if b.dtype == BF16:
        return dot(high, b, dims) + dot(low, b, dims)
    b_high, b_low = halves(b)
    return dot(high, b_high, dims) + (dot(low, b_high, dims) + dot(high, b_low, dims))


def rows8(v):
    return v.reshape(-1, 8, v.shape[-1]).sum(axis=0)


def total(v):
    return v.sum(axis=0, keepdims=True)


def tile(v, rows):
    return jnp.broadcast_to(v[None], (rows // 8, 8, v.shape[-1])).reshape(rows, v.shape[-1])


def gelu_pair(x):
    cdf = 0.5 * lax.erf(x * 0.7071067811865476) + 0.5
    bell = jnp.exp2(x * x * (-0.5 * 1.4426950408889634))
    return x * cdf, cdf + x * bell * 0.3989422804014327


def norm_parts(v, ones):
    high = v.astype(BF16)
    low = (v - high.astype(F32)).astype(BF16)
    centred = v - dot(jnp.concatenate([high, low], axis=1), ones)
    rstd = lax.rsqrt(dot((centred * centred).astype(BF16), ones[: v.shape[1]]) + 1e-05)
    return centred * rstd, rstd


def norm_back(grad, unit, rstd, gain, ones):
    width = grad.shape[1]
    scaled = grad * gain
    first = dot(scaled.astype(BF16), ones[:width])
    second = dot((scaled * unit).astype(BF16), ones[:width])
    return rstd * (scaled - first - unit * second)


def mean_matrix(z):
    return jnp.full((2 * z.C, z.C), 1.0 / z.C, BF16)


class Sizes:
    def __init__(self, images, side, channels, hidden, red, out, layers, parts):
        self.I, self.side, self.C, self.H, self.R, self.O, self.L = images, side, channels, hidden, red, out, layers
        self.parts, self.units = parts, hidden // parts
        self.W = side * images
        self.N0 = side * self.W
        self.CH = 384
        self.N = -(-self.N0 // self.CH) * self.CH
        self.chunks = self.N // self.CH
        self.half = side // 2
        self.hp = -(-self.half // 8) * 8
        self.M = self.half * self.hp
        self.base = self.W
        self.tall = self.W * (2 * self.hp + 2)
        self.long = self.base + self.N + self.W
        self.at_project = 3 * channels
        self.at_expand = self.at_project + channels
        self.at_squeeze = self.at_expand + 3 * red
        self.at_small = self.at_squeeze + red
        self.shared = -(-(self.at_small + 16) // (16 * parts)) * 16
        self.merge = -(-(9 * out + 3) // (16 * parts)) * 16


class Refs:
    pass


def call(body, ins, outs, scratch, limit, micros, smem=(), after=None):
    if after is not None:
        ins = dict(ins, after=after)
    vmem = pl.BlockSpec(memory_space=pltpu.VMEM)
    scalar = pl.BlockSpec(memory_space=pltpu.SMEM)
    waits = dict(after=0)
    names = list(ins) + list(outs) + list(scratch)

    def kernel(*refs):
        r = Refs()
        for name, ref in zip(names, refs):
            setattr(r, name, ref)
        body(r)

    found = pl.pallas_call(
        kernel,
        out_shape=list(outs.values()),
        in_specs=[scalar if name in smem else (pl.BlockSpec(memory_space=pl.ANY) if name in waits else vmem) for name in ins],
        out_specs=[vmem] * len(outs),
        scratch_shapes=list(scratch.values()),
        compiler_params=pltpu.CompilerParams(vmem_limit_bytes=limit * MIB),
        cost_estimate=pl.CostEstimate(flops=int(micros * 1.15e9), bytes_accessed=0, transcendentals=0),
    )(*ins.values())
    return dict(zip(outs, found))


def arr(*shape, dtype=F32):
    return jax.ShapeDtypeStruct(shape, dtype)


def kept(*shape, dtype=F32):
    return pltpu.VMEM(shape, dtype)


def over(z, body):
    def step(c, carry):
        body(pl.ds(pl.multiple_of(c * z.CH, 128), z.CH), c * z.CH)
        return carry

    lax.fori_loop(0, z.chunks, step, 0)


def near(ref, start, off, size):
    return ref[pl.ds(start + off, size), :]


def parity(z, i):
    rows = lax.broadcasted_iota(jnp.int32, (8, z.C), 0)
    return jnp.where(rows % z.I == i, 1.0, 0.0)


def kinds(z, rows):
    return tile(lax.broadcasted_iota(jnp.int32, (8, z.C), 1) % 3, rows)


def weave(z, v):
    out = v[0:1] * parity(z, 0)
    for i in range(1, z.I):
        out += v[i : i + 1] * parity(z, i)
    return out


def split(z, v):
    rows = [total(v * parity(z, i)) for i in range(z.I)]
    return jnp.concatenate(rows + [jnp.zeros((GROUP - z.I, z.C), F32)], axis=0)


def front_kernel(z, r):
    rows = lax.broadcasted_iota(jnp.int32, (z.W, z.C), 0)
    lanes = lax.broadcasted_iota(jnp.int32, (z.W, z.C), 1) % 3
    image = rows % z.I
    col = rows // z.I
    high = jnp.zeros((z.W, z.C), jnp.int32)
    wide = jnp.zeros((z.W, z.C), jnp.int32)
    for i in range(z.I):
        high = jnp.where(image == i, r.sizes[i, 0], high)
        wide = jnp.where(image == i, r.sizes[i, 1], wide)
    inside = jnp.where(col < wide, 1.0, 0.0)
    first, last = col == 0, col == z.side - 1
    edge = jnp.where((first & (lanes == 2)) | (last & (lanes == 1)), 0.0, 1.0)
    back = jnp.where((last & (lanes == 2)) | (first & (lanes == 1)), 0.0, 1.0)

    def step(row, carry):
        at = pl.ds(pl.multiple_of(row * z.W, 8), z.W)
        r.mask[at, :] = jnp.where(high > row, inside, 0.0)
        return carry

    lax.fori_loop(0, z.side, step, 0)
    edge = jnp.concatenate([edge, edge], axis=0).astype(BF16)
    back = jnp.concatenate([back, back], axis=0).astype(BF16)

    def step2(row, carry):
        at = pl.ds(pl.multiple_of(row * 2 * z.W, 16), 2 * z.W)
        r.edge[at, :] = edge
        r.back[at, :] = back
        return carry

    lax.fori_loop(0, z.side // 2, step2, 0)
    pad = jnp.zeros((z.N - z.N0, z.C), F32)
    for ref in (r.mask, r.edge, r.back):
        ref[z.N0 :, :] = pad.astype(ref.dtype)
    pad = jnp.zeros((z.hp - z.half, z.O), F32)
    r.pgrad[z.M :, :] = jnp.zeros((8, 9 * z.C), F32)
    sums = jnp.zeros((8, z.O), F32)
    for i in range(z.I):
        for pair in range(z.half // 2):
            both = r.cotangent[i, :, 2 * pair * z.O : (2 * pair + 2) * z.O].astype(F32)
            both = jnp.concatenate([both[:, : z.O], pad, both[:, z.O :], pad], axis=0)
            at = i * z.M + 2 * pair * z.hp
            r.cot[at : at + 2 * z.hp, :] = both.astype(BF16)
            sums += rows8(both)
        step = z.M // 2
        for at in range(0, z.M, step):
            r.pgrad[at : at + step, :] = dot(r.cot[i * z.M + at : i * z.M + at + step, :], r.merge_weight[...])

        def part(dr, ds, b, down=0):
            k = 3 * dr + ds
            return r.pgrad[pl.ds(b * z.hp + down, z.hp), k * z.C : (k + 1) * z.C]

        for b in range(z.half):
            planes = [
                part(1, 1, b),
                part(2, 1, b) + part(0, 1, b, 1),
                part(1, 2, b),
                part(2, 2, b) + part(0, 2, b, 1),
            ]
            if b < z.half - 1:
                planes[2] += part(1, 0, b + 1)
                planes[3] += part(2, 0, b + 1) + part(0, 0, b + 1, 1)
            for plane, (down, right) in zip(planes, ((0, 0), (1, 0), (0, 1), (1, 1))):
                start = down * z.W + (2 * b + right) * z.I + i
                r.grad[pl.ds(start, z.hp, stride=2 * z.W), :] = plane
    r.merge_bias_sums[...] = sums
    r.token[...] = jnp.zeros_like(r.token)


def shift_phase(z, r, cat):
    r.sums[...] = jnp.zeros_like(r.sums)

    def body(rows, at):
        start = z.base + at
        kind = kinds(z, z.CH)
        mid = near(r.normed, start, 0, z.CH)
        high = jnp.where(kind == 2, near(r.normed, start, -z.W, z.CH), near(r.normed, start, z.W, z.CH))
        wide = jnp.where(kind == 2, near(r.normed, start, -z.I, z.CH), near(r.normed, start, z.I, z.CH))
        high = jnp.where(kind == 0, mid, high).astype(BF16)
        wide = jnp.where(kind == 0, mid, wide * r.edge[rows, :].astype(F32)).astype(BF16)
        mask = r.mask[rows, :]
        for j, piece in enumerate((high, wide, mid.astype(BF16))):
            cat[rows, j * z.C : (j + 1) * z.C] = piece
            r.sums[j] += rows8(piece.astype(F32) * mask)

    over(z, body)


def counts_of(z, r):
    rows = []
    for i in range(GROUP):
        count = (r.sizes[i, 0] * r.sizes[i, 1]).astype(F32) if i < z.I else 1.0
        rows.append(jnp.full((1, z.C), 1.0, F32) * count)
    return jnp.concatenate(rows, axis=0)


def weigh_phase(z, r, l, o):
    pooled = r.mix_bias[l, 0:1] + r.mix_bias[l, 1:2]
    counts = counts_of(z, r)
    for j in range(3):
        pool = split(z, r.sums[j])
        o.pool[j] = pool
        pooled = pooled + fine(pool, r.mix_weight[l, j]) / counts
    o.pooled[...] = pooled
    act, slope = gelu_pair(fine(pooled, r.squeeze_weight[l], (1, 1)) + r.squeeze_bias[l : l + 1])
    o.act[...] = act
    o.slope[...] = slope
    logits = fine(act, r.ewp[l]) + r.ebp[l : l + 1]
    parts = [logits[:, j * z.C : (j + 1) * z.C] for j in range(3)]
    top = jnp.maximum(jnp.maximum(parts[0], parts[1]), parts[2])
    parts = [jnp.exp(part - top) for part in parts]
    whole = parts[0] + parts[1] + parts[2]
    for j in range(3):
        o.share[j] = parts[j] / whole


def mix_phase(z, r, l, o):
    ones = mean_matrix(z)
    share = [weave(z, o.share[j]) for j in range(3)]
    bias = tile(r.mix_bias[l, 0:1] * share[0] + r.mix_bias[l, 1:2] * share[1], z.CH)
    share = [tile(s, z.CH) for s in share]
    gain, shift = r.norm_gain[l, 1:2], r.norm_bias[l, 1:2]

    def body(rows, at):
        mixed = bias
        for j in range(3):
            mixed = mixed + dot(o.cat[rows, j * z.C : (j + 1) * z.C], r.mix_weight[l, j]) * share[j]
        mixed = mixed.astype(BF16)
        o.mixed[rows, :] = mixed
        token = dot(mixed, r.project_weight[l]) + r.project_bias[l : l + 1]
        halfway = r.state[rows, :] + r.mask[rows, :] * token
        unit, rstd = norm_parts(halfway, ones)
        o.unit2[rows, :] = unit.astype(BF16)
        o.rstd2[rows, :] = rstd.astype(BF16)
        o.normed2[rows, :] = (unit * gain + shift).astype(BF16)
        r.state[rows, :] = halfway

    over(z, body)


def norm_store(z, r, l, o, rows, at, state):
    unit, rstd = norm_parts(state, mean_matrix(z))
    o.unit1[rows, :] = unit.astype(BF16)
    o.rstd1[rows, :] = rstd.astype(BF16)
    r.normed[pl.ds(z.base + at, z.CH), :] = unit * r.norm_gain[l, 0:1] + r.norm_bias[l, 0:1]


def clear_edges(z, ref):
    ref[: z.base, :] = jnp.zeros((z.base, z.C), F32)
    ref[z.base + z.N0 :, :] = jnp.zeros((ref.shape[0] - z.base - z.N0, z.C), F32)


def feed_phase(z, r, l, o, after):
    def body(rows, at):
        pre = dot(o.normed2[rows, :], r.inner[l], (1, 1)) + r.inner_bias[l : l + 1]
        act, slope = gelu_pair(pre)
        act = act.astype(BF16)
        o.act_rows[rows, :] = act
        o.slope_rows[rows, :] = slope.astype(BF16)
        out = dot(act, r.outer[l]) + r.outer_bias[l : l + 1]
        state = r.state[rows, :] + r.mask[rows, :] * out
        after(rows, at, state)

    over(z, body)


def saved_early(z):
    return dict(
        unit1=kept(z.N, z.C, dtype=BF16), rstd1=kept(z.N, z.C, dtype=BF16), cat=kept(z.N, 3 * z.C, dtype=BF16), mixed=kept(z.N, z.C, dtype=BF16),
        unit2=kept(z.N, z.C, dtype=BF16), rstd2=kept(z.N, z.C, dtype=BF16), normed2=kept(z.N, z.C, dtype=BF16), pool=kept(3, GROUP, z.C),
        pooled=kept(GROUP, z.C), act=kept(GROUP, z.R), slope=kept(GROUP, z.R), share=kept(3, GROUP, z.C),
    )


def saved_late(z):
    return dict(act_rows=kept(z.N, z.H, dtype=BF16), slope_rows=kept(z.N, z.H, dtype=BF16))


def first_kernel(z, r):
    spots = lax.broadcasted_iota(jnp.int32, (3 * z.C, 3 * z.C), 0)
    ends = lax.broadcasted_iota(jnp.int32, (3 * z.C, 3 * z.C), 1)
    kind = jnp.where(ends >= 2 * z.C, 2, jnp.where(ends >= z.C, 1, 0))
    r.perm[...] = jnp.where(spots == 3 * (ends - kind * z.C) + kind, 1.0, 0.0).astype(BF16)
    for l in range(z.L):
        r.ewp[l] = fine(r.expand_weight[l], r.perm[...])
    r.ebp[...] = fine(r.expand_bias[...], r.perm[...])
    whole = z.N0 // z.CH

    def step(c, carry):
        rows = pl.ds(pl.multiple_of(c * z.CH, 128), z.CH)
        state = r.images[rows, :].astype(F32) * r.mask[rows, :]
        r.state[rows, :] = state
        norm_store(z, r, 0, r, rows, c * z.CH, state)
        return carry

    lax.fori_loop(0, whole, step, 0)
    if whole < z.chunks:
        at = whole * z.CH
        left = z.N0 - at
        tail = r.images[at:, :].astype(F32) * r.mask[at : z.N0, :]
        state = jnp.concatenate([tail, jnp.zeros((z.CH - left, z.C), F32)], axis=0)
        r.state[at:, :] = state
        norm_store(z, r, 0, r, pl.ds(at, z.CH), at, state)
    clear_edges(z, r.normed)
    shift_phase(z, r, r.cat)
    weigh_phase(z, r, 0, r)
    mix_phase(z, r, 0, r)
    r.token[...] = jnp.zeros_like(r.token)


def rank(z, e):
    at, half = 0, z.parts // 2
    while half:
        at, e, half = at + half * (e % 2), e // 2, half // 2
    return at


def put_blocks(z, me, rows, size, here, away, start=0):
    half = z.parts // 2
    for e in range(z.parts):
        at = rank(z, e)
        block = rows[pl.ds(pl.multiple_of((me ^ e) * size, 16), size), :]
        if at < half:
            here[at, start : start + size, :] = block
        else:
            away[at - half, start : start + size, :] = block


def second_kernel(z, r):
    me = r.place[0]
    for k, e in enumerate(z.found):
        at = pl.multiple_of((me ^ e) * z.units, z.units)
        for l in range(z.L):
            r.inner[l, pl.ds(at, z.units), :] = r.gathered[k, 2 * l * z.units : (2 * l + 1) * z.units, :]
            r.outer[l, pl.ds(at, z.units), :] = r.gathered[k, (2 * l + 1) * z.units : (2 * l + 2) * z.units, :]
        at = 2 * z.L * z.units
        r.bias_rows[me ^ e] = r.gathered[k, at : at + 16, :].astype(F32)
    for l in range(z.L):
        r.inner_bias[l : l + 1] = jnp.concatenate([r.bias_rows[h, l : l + 1, : z.units] for h in range(z.parts)], axis=1)
    early, late = [Refs() for _ in range(z.L)], [Refs() for _ in range(z.L)]
    for l in range(z.L):
        early[l].normed2 = r.normed2_0 if l == 0 else r.normed2
        early[l].act_rows = r.act_rows_0 if l == 0 else r.act_rows
        early[l].slope_rows = r.slope_rows_0 if l == 0 else r.slope_rows

    def then_norm(rows, at, state):
        r.state[rows, :] = state
        norm_store(z, r, 1, r, rows, at, state)

    r.state[...] = r.state_in[...]
    feed_phase(z, r, 0, early[0], then_norm)
    clear_edges(z, r.normed)
    shift_phase(z, r, r.cat)
    weigh_phase(z, r, 1, r)
    mix_phase(z, r, 1, r)

    def then_keep(rows, at, state):
        r.normed[pl.ds(z.base + at, z.CH), :] = state

    feed_phase(z, r, 1, early[1], then_keep)
    for i in range(z.I):
        for pair in range(z.half // 2):
            at = i * z.M + 2 * pair * z.hp
            for k in range(9):
                dr, ds = divmod(k, 3)
                two = []
                for b in (2 * pair, 2 * pair + 1):
                    col = 2 * b + ds - 1
                    if col < 0:
                        two.append(jnp.zeros((z.hp, z.C), F32))
                    else:
                        two.append(r.normed[pl.ds(dr * z.W + col * z.I + i, z.hp, stride=2 * z.W), :])
                r.patch[at : at + 2 * z.hp, k * z.C : (k + 1) * z.C] = jnp.concatenate(two, axis=0).astype(BF16)
    for i in range(z.I):
        for pair in range(z.half // 2):
            at = i * z.M + 2 * pair * z.hp
            merged = dot(r.patch[at : at + 2 * z.hp, :], r.merge_weight[...], (1, 1)) + r.merge_bias[...]
            wide = jnp.concatenate([merged[: z.half], merged[z.hp : z.hp + z.half]], axis=1)
            r.features[i, :, 2 * pair * z.O : (2 * pair + 2) * z.O] = wide.astype(BF16)
    for k in range(9):
        grad = dot(r.cot[...], r.patch[:, k * z.C : (k + 1) * z.C], (0, 0))
        r.merge_rows[k * z.O : (k + 1) * z.O, :] = grad.astype(BF16)
    bias = total(r.merge_bias_sums[...])
    rest = z.O - 2 * z.C
    rows = [bias[:, : z.C], bias[:, z.C : 2 * z.C]]
    rows += [jnp.concatenate([bias[:, 2 * z.C :], jnp.zeros((1, z.C - rest), F32)], axis=1)]
    rows += [jnp.zeros((z.parts * z.merge - 9 * z.O - 3, z.C), F32)]
    r.merge_rows[9 * z.O :, :] = jnp.concatenate(rows, axis=0).astype(BF16)
    put_blocks(z, me, r.merge_rows, z.merge, r.merge_here, r.merge_away)


def feed_back_kernel(z, l, r):
    ones = mean_matrix(z)
    gain = r.norm_gain[l, 1:2]
    for ref in (r.vec, r.inner_sums, r.g_outer, r.g_inner):
        ref[...] = jnp.zeros_like(ref)

    def body(rows, at):
        mask = r.mask[rows, :]
        grad = r.grad[rows, :]
        out = (grad * mask).astype(BF16)
        r.vec[0] += rows8(out.astype(F32))
        pre = (dot(out, r.outer[l], (1, 1)) * r.slope_rows[rows, :].astype(F32)).astype(BF16)
        r.inner_sums[...] += rows8(pre.astype(F32))
        r.g_outer[...] += dot(out, r.act_rows[rows, :], (0, 0))
        r.g_inner[...] += dot(r.normed2[rows, :], pre, (0, 0))
        normed_grad = dot(pre, r.inner[l])
        unit = r.unit2[rows, :].astype(F32)
        r.vec[1] += rows8(normed_grad * unit)
        r.vec[2] += rows8(normed_grad)
        r.half_grad[rows, :] = grad + norm_back(normed_grad, unit, r.rstd2[rows, :].astype(F32), gain, ones)

    over(z, body)
    inner = total(r.inner_sums[...])
    small = [total(r.vec[k]) for k in range(3)]
    small += [inner[:, k * z.C : (k + 1) * z.C] for k in range(z.H // z.C)]
    small += [jnp.zeros((1, z.C), F32)]
    r.feed_small[...] = jnp.concatenate(small, axis=0)
    r.turned[0] = r.g_inner[...].T.astype(BF16)
    r.turned[1] = r.g_outer[...].T.astype(BF16)
    for k in range(2):
        put_blocks(z, r.place[0], r.turned.at[k], z.units, r.here, r.away, k * z.units)
    r.token[...] = jnp.zeros_like(r.token)


def token_back_kernel(z, l, r):
    for ref in (r.vec, r.g_project, r.g_mix):
        ref[...] = jnp.zeros_like(ref)
    even, odd = tile(parity(z, 0), z.CH), tile(parity(z, 1), z.CH)

    def body(rows, at):
        token = (r.half_grad[rows, :] * r.mask[rows, :]).astype(BF16)
        r.vec[0] += rows8(token.astype(F32))
        r.g_project[...] += dot(r.mixed[rows, :], token, (0, 0))
        mixed_grad = dot(token, r.project_weight[l], (1, 1))
        r.vec[1] += rows8(mixed_grad)
        both = jnp.concatenate([(mixed_grad * even).astype(BF16), (mixed_grad * odd).astype(BF16)], axis=1)
        r.mixed_grad[rows, :] = both
        r.g_mix[...] += dot(both, r.cat[rows, :], (0, 0))

    over(z, body)
    counts = counts_of(z, r)
    zeros = jnp.zeros((GROUP - z.I, z.C), F32)
    summed = split(z, r.vec[1])
    share = [r.share[j] for j in range(3)]
    mix, dp = [], []
    for j in range(3):
        weight = r.mix_weight[l, j].astype(F32)
        rows = []
        found = 0.0
        for i in range(z.I):
            block = r.g_mix[i * z.C : (i + 1) * z.C, j * z.C : (j + 1) * z.C].T
            rows.append(total(weight * block))
            found = found + block * share[j][i : i + 1]
            scaled = weight * share[j][i : i + 1]
            r.scaled[j * z.C : (j + 1) * z.C, i * z.C : (i + 1) * z.C] = scaled.astype(BF16)
        mix.append(found)
        dp.append(jnp.concatenate(rows + [zeros], axis=0))
    for j in range(2):
        dp[j] += summed * r.mix_bias[l, j : j + 1]
    even = dp[0] * share[0] + dp[1] * share[1] + dp[2] * share[2]
    dz = jnp.concatenate([share[j] * (dp[j] - even) for j in range(3)], axis=1)
    act, slope, pooled = r.act[...], r.slope[...], r.pooled[...]
    expand = fine(fine(act, dz, (0, 0)), r.perm[...], (1, 1))
    expand_bias = total(fine(dz, r.perm[...], (1, 1)))
    dact = fine(dz, r.ewp[l], (1, 1)) * slope
    squeeze = fine(dact, pooled, (0, 0))
    dpool = fine(dact, r.squeeze_weight[l])
    push = dpool / counts
    for j in range(3):
        mix[j] += fine(r.pool[j], push, (0, 0))
        r.push[j] = weave(z, fine(push, r.mix_weight[l, j], (1, 1)))
    for j in range(3):
        r.rows[j * z.C : (j + 1) * z.C, :] = mix[j].astype(BF16)
    r.rows[z.at_project : z.at_expand, :] = r.g_project[...].astype(BF16)
    for j in range(3):
        at = z.at_expand + j * z.R
        r.rows[at : at + z.R, :] = expand[:, j * z.C : (j + 1) * z.C].astype(BF16)
    r.rows[z.at_squeeze : z.at_small, :] = squeeze.astype(BF16)
    small = [total(share[j] * summed + dpool) for j in range(2)]
    small += [total(r.vec[0]), r.feed_small[: 3 + z.H // z.C, :]]
    small += [expand_bias[:, j * z.C : (j + 1) * z.C] for j in range(3)]
    small += [jnp.concatenate([total(dact), jnp.zeros((1, z.C - z.R), F32)], axis=1)]
    used = sum(row.shape[0] for row in small)
    small += [jnp.zeros((z.parts * z.shared - z.at_small - used, z.C), F32)]
    r.rows[z.at_small :, :] = jnp.concatenate(small, axis=0).astype(BF16)
    put_blocks(z, r.place[0], r.rows, z.shared, r.here, r.away)
    r.token[...] = jnp.zeros_like(r.token)


def mix_back_kernel(z, l, last, r):
    ones = mean_matrix(z)
    for ref in (r.back_h, r.back_w):
        clear_edges(z, ref)
    gain = r.norm_gain[l, 0:1]
    push = [tile(r.push[j], z.CH) for j in range(3)]

    def spread(rows, at):
        mask = r.mask[rows, :]
        parts = dot(r.mixed_grad[rows, :], r.scaled[...], (1, 1))
        for j, ref in enumerate((r.back_h, r.back_w, r.back_c)):
            ref[pl.ds(z.base + at, z.CH), :] = parts[:, j * z.C : (j + 1) * z.C] + mask * push[j]

    over(z, spread)
    r.vec[...] = jnp.zeros_like(r.vec)

    def body(rows, at):
        start = z.base + at
        kind = kinds(z, z.CH)
        high = jnp.where(kind == 2, near(r.back_h, start, z.W, z.CH), near(r.back_h, start, -z.W, z.CH))
        wide = jnp.where(kind == 2, near(r.back_w, start, z.I, z.CH), near(r.back_w, start, -z.I, z.CH))
        high = jnp.where(kind == 0, near(r.back_h, start, 0, z.CH), high)
        wide = jnp.where(kind == 0, near(r.back_w, start, 0, z.CH), wide * r.back[rows, :].astype(F32))
        grad = high + wide + near(r.back_c, start, 0, z.CH)
        unit = r.unit1[rows, :].astype(F32)
        r.vec[0] += rows8(grad * unit)
        r.vec[1] += rows8(grad)
        grad = r.half_grad[rows, :] + norm_back(grad, unit, r.rstd1[rows, :].astype(F32), gain, ones)
        if not last:
            r.state_grad[rows, :] = grad
            return
        grad = grad * r.mask[rows, :]
        left = z.N0 - (z.chunks - 1) * z.CH

        @pl.when(at < z.N0 - z.CH + 1)
        def _():
            r.state_grad[rows, :] = grad

        @pl.when(at > z.N0 - z.CH)
        def _():
            r.state_grad[z.N0 - left :, :] = grad[:left]

    over(z, body)
    stray = r.back_h[z.base + z.N0 - z.W : z.base + z.N0, :]
    r.vec[1] -= rows8(jnp.where(kinds(z, z.W) == 1, stray, 0.0))
    r.first_norm[...] = jnp.concatenate([total(r.vec[0]), total(r.vec[1])], axis=0)
    r.token[...] = jnp.zeros_like(r.token)


def final_outputs(z):
    return dict(
        mix_weight=arr(z.L, 3, z.C, z.C), mix_bias=arr(z.L, 2, z.C), squeeze_weight=arr(z.L, z.R, z.C),
        squeeze_bias=arr(z.L, z.R), expand_weight=arr(z.L, z.R, 3 * z.C), expand_bias=arr(z.L, 3 * z.C),
        project_weight=arr(z.L, z.C, z.C), project_bias=arr(z.L, z.C), norm_gain=arr(z.L, 2, z.C),
        norm_bias=arr(z.L, 2, z.C), inner_weight=arr(z.L, z.units, z.C), inner_bias=arr(z.L, z.units),
        outer_weight=arr(z.L, z.units, z.C), outer_bias=arr(z.L, z.C), merge_weight=arr(z.O, 9 * z.C),
        merge_bias=arr(1, z.O),
    )


def last_kernel(z, r):
    me = r.place[0]
    half = z.parts // 2
    size = z.shared
    for at in range(z.parts):
        spot = me ^ z.ranks[at]
        have, merge = (r.have, r.merge_have) if at < half else (r.got, r.merge_got)
        k = at % half
        rows = pl.ds(pl.multiple_of(spot * z.shared, 16), z.shared)
        r.rows[0, rows, :] = have[k * size : (k + 1) * size, :]
        r.rows[1, rows, :] = merge[k, :size, :]
        r.merge_rows[pl.ds(pl.multiple_of(spot * z.merge, 16), z.merge), :] = merge[k, size:, :]
    norms = r.have[half * size :, :].astype(F32) + r.got[half * size :, :].astype(F32)
    for l in range(z.L):
        rows = r.rows.at[l]

        def get(at, count):
            return rows[at : at + count, :].astype(F32)

        for j in range(3):
            r.mix_weight[l, j] = get(j * z.C, z.C)
            r.expand_weight[l, :, j * z.C : (j + 1) * z.C] = get(z.at_expand + j * z.R, z.R)
        r.project_weight[l] = get(z.at_project, z.C)
        r.squeeze_weight[l] = get(z.at_squeeze, z.R)
        small = get(z.at_small, 16)
        r.mix_bias[l] = small[0:2]
        r.project_bias[l : l + 1] = small[2:3]
        r.outer_bias[l : l + 1] = small[3:4]
        r.norm_gain[l] = jnp.concatenate([norms[2 * l : 2 * l + 1], small[4:5]], axis=0)
        r.norm_bias[l] = jnp.concatenate([norms[2 * l + 1 : 2 * l + 2], small[5:6]], axis=0)
        at = 6
        inner = jnp.zeros((1, z.units), F32)
        for k in range(z.H // z.C):
            for c in range(0, z.C, z.units):
                mine = jnp.where(me == (k * z.C + c) // z.units, 1.0, 0.0)
                inner = inner + small[at : at + 1, c : c + z.units] * mine
            at += 1
        r.inner_bias[l : l + 1] = inner
        for j in range(3):
            r.expand_bias[l : l + 1, j * z.C : (j + 1) * z.C] = small[at : at + 1]
            at += 1
        r.squeeze_bias[l : l + 1] = small[at : at + 1, : z.R]
        feed = r.feed_rows[2 * l * z.units : 2 * (l + 1) * z.units, :].astype(F32)
        r.inner_weight[l] = feed[: z.units]
        r.outer_weight[l] = feed[z.units :]
    for k in range(9):
        r.merge_weight[:, k * z.C : (k + 1) * z.C] = r.merge_rows[k * z.O : (k + 1) * z.O, :].astype(F32)
    small = r.merge_rows[9 * z.O : 9 * z.O + 16, :].astype(F32)
    r.merge_bias[:, : z.C] = small[0:1]
    r.merge_bias[:, z.C : 2 * z.C] = small[1:2]
    r.merge_bias[:, 2 * z.C :] = small[2:3, : z.O - 2 * z.C]


def pack_kernel(z, r):
    u = z.units
    for l in range(z.L):
        r.block[2 * l * u : (2 * l + 1) * u, :] = r.inner_weight[l]
        r.block[(2 * l + 1) * u : (2 * l + 2) * u, :] = r.outer_weight[l]
    bias = r.inner_bias[...].astype(F32)
    if u < z.C:
        bias = jnp.concatenate([bias, jnp.zeros((z.L, z.C - u), F32)], axis=1)
    bias = jnp.concatenate([bias, jnp.zeros((16 - z.L, z.C), F32)], axis=0)
    r.block[2 * z.L * u :, :] = bias.astype(BF16)


def swap(x, axis, n, bit):
    return lax.ppermute(x, axis, [(a, a ^ bit) for a in range(n)])


def bits_of(n):
    return [1 << k for k in range(n.bit_length() - 1)]


def add(here, got, token):
    out = here.astype(F32) + got.astype(F32)
    if token is not None:
        out = out + token[0]
    return out.astype(BF16)


def take(tokens):
    return tokens.pop(0) if tokens else None


class Chain:
    def __init__(self, parts, hid, img):
        self.here = jnp.concatenate([part["here"] for part in parts], axis=1)
        self.away = jnp.concatenate([part["away"] for part in parts], axis=1)
        self.left = [("hid", hid, bit) for bit in bits_of(hid)] + [("img", img, bit) for bit in bits_of(img)]

    def held(self):
        return self.here

    def step(self, token=None, extra=None):
        axis, n, bit = self.left.pop(0)
        x = add(self.here, swap(self.away, axis, n, bit), token)
        if x.shape[0] > 1:
            half = x.shape[0] // 2
            self.here, self.away = x[:half], x[half:]
        else:
            if extra is not None and axis == "hid":
                x = jnp.concatenate([x, extra[None]], axis=1)
            self.here = self.away = x

    def finish(self, extra=None):
        while self.left:
            self.step(None, extra)
        return self.here[0]


def per_device(
    img, hid, images, sizes, cotangent, mix_weight, mix_bias, squeeze_weight, squeeze_bias, expand_weight, expand_bias,
    project_weight, project_bias, norm_gain, norm_bias, inner_weight, inner_bias, outer_weight, outer_bias,
    merge_weight, merge_bias,
):
    z = Sizes(
        images.shape[0], images.shape[1], images.shape[3], inner_weight.shape[2] * hid, squeeze_weight.shape[2],
        merge_weight.shape[1], mix_weight.shape[0], hid,
    )
    z.ranks = sorted(range(hid), key=partial(rank, z))
    place = lax.axis_index("hid").reshape(1)
    flat = images.transpose(1, 2, 0, 3).reshape(z.N0, z.C)
    merge_t = merge_weight.T
    squeeze_t = squeeze_weight.transpose(0, 2, 1)
    block = call(
        partial(pack_kernel, z),
        dict(inner_weight=inner_weight.transpose(0, 2, 1), outer_weight=outer_weight, inner_bias=inner_bias, place=place),
        dict(block=kept(2 * z.L * z.units + 16, z.C, dtype=BF16)), {}, 2, 1, dict(place=0),
    )
    block = block["block"]
    smem = dict(sizes=0, place=0)
    small = dict(
        mix_weight=mix_weight, mix_bias=mix_bias, squeeze_weight=squeeze_t, squeeze_bias=squeeze_bias,
        project_weight=project_weight, project_bias=project_bias, norm_gain=norm_gain, norm_bias=norm_bias,
    )
    token = dict(token=arr(1, z.C))
    a = call(
        partial(front_kernel, z),
        dict(sizes=sizes, cotangent=cotangent, merge_weight=merge_t),
        dict(
            mask=kept(z.N, z.C), edge=kept(z.N, z.C, dtype=BF16), back=kept(z.N, z.C, dtype=BF16), cot=kept(z.I * z.M, z.O, dtype=BF16),
            grad=kept(z.tall, z.C), merge_bias_sums=kept(8, z.O), **token,
        ),
        dict(pgrad=kept(z.M + 8, 9 * z.C)),
        4, 3, smem,
    )
    order = bits_of(hid)[1:] + [1]

    def widen(have, bit, token):
        got = swap(have, "hid", hid, bit)
        return jnp.concatenate([have, got if token is None else got + token.astype(BF16)], axis=0)

    z.found = [0]
    for bit in order:
        z.found = z.found + [e ^ bit for e in z.found]
    have = widen(block[None], order[0], a["token"])
    b = call(
        partial(first_kernel, z),
        dict(
            images=flat, sizes=sizes, mask=a["mask"], edge=a["edge"], expand_weight=expand_weight, expand_bias=expand_bias,
            **small,
        ),
        dict(
            state=kept(z.N, z.C), perm=kept(3 * z.C, 3 * z.C, dtype=BF16), ewp=kept(z.L, z.R, 3 * z.C),
            ebp=kept(z.L, 3 * z.C), **saved_early(z), **token,
        ),
        dict(normed=kept(z.long, z.C), sums=kept(3, 8, z.C)),
        5, 10, smem, have,
    )
    for bit in order[1:]:
        have = widen(have, bit, b["token"] if bit == order[1] else None)
    late = saved_late(z)
    c = call(
        partial(second_kernel, z),
        dict(
            sizes=sizes, mask=a["mask"], edge=a["edge"], state_in=b["state"], normed2_0=b["normed2"], gathered=have, place=place,
            ewp=b["ewp"], ebp=b["ebp"], outer_bias=outer_bias, merge_weight=merge_t, merge_bias=merge_bias.reshape(1, -1),
            cot=a["cot"], merge_bias_sums=a["merge_bias_sums"], **small,
        ),
        dict(
            features=arr(z.I, z.half, z.half * z.O, dtype=BF16),
            merge_here=kept(z.parts // 2, z.merge, z.C, dtype=BF16), merge_away=kept(z.parts // 2, z.merge, z.C, dtype=BF16),
            inner=kept(z.L, z.H, z.C, dtype=BF16), outer=kept(z.L, z.H, z.C, dtype=BF16),
            act_rows_0=late["act_rows"], slope_rows_0=late["slope_rows"], **saved_early(z), **late,
        ),
        dict(
            state=kept(z.N, z.C), normed=kept(z.tall, z.C), sums=kept(3, 8, z.C), inner_bias=kept(z.L, z.H), bias_rows=kept(z.parts, 16, z.C),
            patch=kept(z.I * z.M, 9 * z.C, dtype=BF16), merge_rows=kept(z.parts * z.merge, z.C, dtype=BF16),
        ),
        13, 22, smem,
    )
    first = dict(b, act_rows=c["act_rows_0"], slope_rows=c["slope_rows_0"])

    def some(s, **names):
        return {name: s[name] for name in names}

    grad = a["grad"]
    shares, norms = [None] * z.L, [None] * z.L
    chain = None
    for l in reversed(range(z.L)):
        s = c if l else first
        d = call(
            partial(feed_back_kernel, z, l),
            dict(
                place=place, mask=a["mask"], grad=grad, inner=c["inner"], outer=c["outer"], norm_gain=norm_gain,
                **some(s, act_rows=0, slope_rows=0, normed2=0, unit2=0, rstd2=0),
            ),
            dict(
                half_grad=kept(z.N, z.C), feed_small=arr(8, z.C), here=kept(z.parts // 2, 2 * z.units, z.C, dtype=BF16),
                away=kept(z.parts // 2, 2 * z.units, z.C, dtype=BF16), **token,
            ),
            dict(
                vec=kept(3, 8, z.C), inner_sums=kept(8, z.H), g_outer=kept(z.C, z.H), g_inner=kept(z.C, z.H),
                turned=kept(2, z.H, z.C, dtype=BF16),
            ),
            6, 6, smem, chain and chain.held(),
        )
        if chain:
            chain.step(d["token"])
        t = call(
            partial(token_back_kernel, z, l),
            dict(
                sizes=sizes, place=place, mask=a["mask"], half_grad=d["half_grad"], feed_small=d["feed_small"],
                perm=b["perm"], ewp=b["ewp"], **some(s, mixed=0, cat=0, share=0, pool=0, pooled=0, act=0, slope=0), **small,
            ),
            dict(
                mixed_grad=kept(z.N, z.I * z.C, dtype=BF16), scaled=kept(3 * z.C, z.I * z.C, dtype=BF16),
                push=kept(3, 8, z.C), here=kept(z.parts // 2, z.shared, z.C, dtype=BF16),
                away=kept(z.parts // 2, z.shared, z.C, dtype=BF16), **token,
            ),
            dict(
                vec=kept(2, 8, z.C), g_project=kept(z.C, z.C), g_mix=kept(z.I * z.C, 3 * z.C),
                rows=kept(z.parts * z.shared, z.C, dtype=BF16),
            ),
            5, 6, smem, chain and chain.held(),
        )
        parts = [d, t]
        if chain:
            chain.step(t["token"])
        elif l:
            parts += [dict(here=c["merge_here"], away=c["merge_away"])]
            chain = Chain(parts, hid, img)
        if not l:
            tail = Chain(parts, hid, img)
        e = call(
            partial(mix_back_kernel, z, l, l == 0),
            dict(
                mask=a["mask"], back=a["back"], norm_gain=norm_gain, half_grad=d["half_grad"],
                **some(t, mixed_grad=0, scaled=0, push=0), **some(s, unit1=0, rstd1=0),
            ),
            dict(state_grad=kept(z.N, z.C) if l else arr(z.N0, z.C), first_norm=arr(2, z.C), **token),
            dict(back_h=kept(z.long, z.C), back_w=kept(z.long, z.C), back_c=kept(z.long, z.C), vec=kept(2, 8, z.C)),
            6, 4, (), chain and chain.held(),
        )
        if chain:
            chain.step(e["token"])
        grad, norms[l] = e["state_grad"], e["first_norm"]
    images_grad = grad.reshape(z.side, z.side, z.I, z.C).transpose(2, 0, 1, 3)

    early = chain.finish()
    tail.step(e["token"])
    norm_rows = jnp.pad(jnp.concatenate(norms, axis=0), ((0, 16 - 2 * z.L), (0, 0))).astype(BF16)
    late_rows = tail.finish(norm_rows)
    feed = 2 * z.units
    cut = feed + z.shared
    feed_rows = jnp.concatenate([late_rows[:feed], early[:feed]], axis=0)
    have, norm_rows = late_rows[feed:cut], late_rows[cut:]
    merge = early[None, feed:]
    for bit in bits_of(hid)[::-1]:
        sent = jnp.concatenate([have, norm_rows], axis=0)
        got, merge_got = swap(sent, "hid", hid, bit), swap(merge, "hid", hid, bit)
        if bit > 1:
            have = jnp.concatenate([have, got[:-16]], axis=0)
            norm_rows = add(norm_rows, got[-16:], None)
            merge = jnp.concatenate([merge, merge_got], axis=0)
    g = call(
        partial(last_kernel, z),
        dict(place=place, have=sent, got=got, merge_have=merge, merge_got=merge_got, feed_rows=feed_rows),
        final_outputs(z),
        dict(rows=kept(z.L, z.parts * z.shared, z.C, dtype=BF16), merge_rows=kept(z.parts * z.merge, z.C, dtype=BF16)),
        8, 2, smem,
    )
    return (
        c["features"], images_grad, g["mix_weight"], g["mix_bias"], g["squeeze_weight"].transpose(0, 2, 1),
        g["squeeze_bias"], g["expand_weight"], g["expand_bias"], g["project_weight"], g["project_bias"], g["norm_gain"],
        g["norm_bias"], g["inner_weight"].transpose(0, 2, 1), g["inner_bias"], g["outer_weight"], g["outer_bias"],
        g["merge_weight"].T, g["merge_bias"].reshape(-1),
    )


def solution(mesh):
    maps = ("img", "hid")
    in_specs = (
        P(maps, None, None, None), P(maps, None), P(maps, None, None), P(), P(), P(), P(), P(), P(), P(), P(), P(), P(),
        P(None, None, "hid"), P(None, "hid"), P(None, "hid", None), P(), P(), P(),
    )
    out_specs = (
        P(maps, None, None), P(maps, None, None, None), P(), P(), P(), P(), P(), P(), P(), P(), P(), P(),
        P(None, None, "hid"), P(None, "hid"), P(None, "hid", None), P(), P(), P(),
    )
    return jax.shard_map(
        partial(per_device, mesh.shape["img"], mesh.shape["hid"]),
        mesh=mesh, in_specs=in_specs, out_specs=out_specs, check_vma=False,
    )
```

```python
from functools import partial

import jax
import jax.numpy as jnp
from jax import lax
from jax.experimental import pallas as pl
from jax.experimental.pallas import tpu as pltpu
from jax.sharding import PartitionSpec as P

F32 = jnp.float32
BF16 = jnp.bfloat16
GROUP = 8
MIB = 2**20


def dot(a, b, dims=(1, 0)):
    return lax.dot_general(a, b, (((dims[0],), (dims[1],)), ((), ())), preferred_element_type=F32)


def halves(v):
    high = v.astype(BF16)
    return high, (v - high.astype(F32)).astype(BF16)


def fine(a, b, dims=(1, 0)):
    high, low = halves(a)
    if b.dtype == BF16:
        return dot(high, b, dims) + dot(low, b, dims)
    b_high, b_low = halves(b)
    return dot(high, b_high, dims) + (dot(low, b_high, dims) + dot(high, b_low, dims))


def rows8(v):
    return v.reshape(-1, 8, v.shape[-1]).sum(axis=0)


def total(v):
    return v.sum(axis=0, keepdims=True)


def tile(v, rows):
    return jnp.broadcast_to(v[None], (rows // 8, 8, v.shape[-1])).reshape(rows, v.shape[-1])


def gelu_pair(x):
    cdf = 0.5 * lax.erf(x * 0.7071067811865476) + 0.5
    bell = jnp.exp2(x * x * (-0.5 * 1.4426950408889634))
    return x * cdf, cdf + x * bell * 0.3989422804014327


def norm_parts(v):
    centred = v - jnp.mean(v, axis=-1, keepdims=True)
    rstd = lax.rsqrt(jnp.mean(centred * centred, axis=-1, keepdims=True) + 1e-05)
    return centred * rstd, jnp.broadcast_to(rstd, v.shape)


def norm_back(grad, unit, rstd, gain):
    scaled = grad * gain
    first = jnp.mean(scaled, axis=-1, keepdims=True)
    second = jnp.mean(scaled * unit, axis=-1, keepdims=True)
    return rstd * (scaled - first - unit * second)


class Sizes:
    def __init__(self, images, side, channels, hidden, red, out, layers, parts):
        self.I, self.side, self.C, self.H, self.R, self.O, self.L = images, side, channels, hidden, red, out, layers
        self.parts, self.units = parts, hidden // parts
        self.W = side * images
        self.N0 = side * self.W
        self.N = -(-self.N0 // 384) * 384
        self.run_first = self.run_back = self.run_mix = self.N
        self.run_second = self.N // 7
        self.half = side // 2
        self.hp = -(-self.half // 8) * 8
        self.M = self.half * self.hp
        self.base = self.W
        self.tall = self.W * (2 * self.hp + 2)
        self.long = self.base + self.N + self.W
        self.at_project = 3 * channels
        self.at_expand = self.at_project + channels
        self.at_squeeze = self.at_expand + 3 * red
        self.at_small = self.at_squeeze + red
        self.shared = -(-(self.at_small + 16) // (16 * parts)) * 16
        self.merge = -(-(9 * out + 3) // (16 * parts)) * 16


class Refs:
    pass


def call(body, ins, outs, scratch, limit, micros, smem=(), after=None):
    if after is not None:
        ins = dict(ins, after=after)
    vmem = pl.BlockSpec(memory_space=pltpu.VMEM)
    scalar = pl.BlockSpec(memory_space=pltpu.SMEM)
    waits = dict(after=0)
    names = list(ins) + list(outs) + list(scratch)

    def kernel(*refs):
        r = Refs()
        for name, ref in zip(names, refs):
            setattr(r, name, ref)
        body(r)

    found = pl.pallas_call(
        kernel,
        out_shape=list(outs.values()),
        in_specs=[scalar if name in smem else (pl.BlockSpec(memory_space=pl.ANY) if name in waits else vmem) for name in ins],
        out_specs=[vmem] * len(outs),
        scratch_shapes=list(scratch.values()),
        compiler_params=pltpu.CompilerParams(vmem_limit_bytes=limit * MIB),
        cost_estimate=pl.CostEstimate(flops=int(micros * 1.15e9), bytes_accessed=0, transcendentals=0),
    )(*ins.values())
    return dict(zip(outs, found))


def arr(*shape, dtype=F32):
    return jax.ShapeDtypeStruct(shape, dtype)


def kept(*shape, dtype=F32):
    return pltpu.VMEM(shape, dtype)


def over(z, body, size):
    for at in range(0, z.N, size):
        body(slice(at, at + size), at)


def near(ref, start, off, size):
    return ref[start + off : start + off + size, :]


def parity(z, i):
    rows = lax.broadcasted_iota(jnp.int32, (8, z.C), 0)
    return jnp.where(rows % z.I == i, 1.0, 0.0)


def kinds(z, rows):
    return tile(lax.broadcasted_iota(jnp.int32, (8, z.C), 1) % 3, rows)


def weave(z, v):
    out = v[0:1] * parity(z, 0)
    for i in range(1, z.I):
        out += v[i : i + 1] * parity(z, i)
    return out


def split(z, v):
    rows = [total(v * parity(z, i)) for i in range(z.I)]
    return jnp.concatenate(rows + [jnp.zeros((GROUP - z.I, z.C), F32)], axis=0)


def front_kernel(z, r):
    rows = lax.broadcasted_iota(jnp.int32, (z.W, z.C), 0)
    lanes = lax.broadcasted_iota(jnp.int32, (z.W, z.C), 1) % 3
    image = rows % z.I
    col = rows // z.I
    high = jnp.zeros((z.W, z.C), jnp.int32)
    wide = jnp.zeros((z.W, z.C), jnp.int32)
    for i in range(z.I):
        high = jnp.where(image == i, r.sizes[i, 0], high)
        wide = jnp.where(image == i, r.sizes[i, 1], wide)
    inside = jnp.where(col < wide, 1.0, 0.0)
    first, last = col == 0, col == z.side - 1
    edge = jnp.where((first & (lanes == 2)) | (last & (lanes == 1)), 0.0, 1.0)
    back = jnp.where((last & (lanes == 2)) | (first & (lanes == 1)), 0.0, 1.0)

    def step(row, carry):
        at = pl.ds(pl.multiple_of(row * z.W, 8), z.W)
        r.mask[at, :] = jnp.where(high > row, inside, 0.0)
        return carry

    lax.fori_loop(0, z.side, step, 0)
    edge = jnp.concatenate([edge, edge], axis=0).astype(BF16)
    back = jnp.concatenate([back, back], axis=0).astype(BF16)

    def step2(row, carry):
        at = pl.ds(pl.multiple_of(row * 2 * z.W, 16), 2 * z.W)
        r.edge[at, :] = edge
        r.back[at, :] = back
        return carry

    lax.fori_loop(0, z.side // 2, step2, 0)
    pad = jnp.zeros((z.N - z.N0, z.C), F32)
    for ref in (r.mask, r.edge, r.back):
        ref[z.N0 :, :] = pad.astype(ref.dtype)
    pad = jnp.zeros((z.hp - z.half, z.O), F32)
    r.pgrad[z.M :, :] = jnp.zeros((8, 9 * z.C), F32)
    sums = jnp.zeros((8, z.O), F32)
    for i in range(z.I):
        for pair in range(z.half // 2):
            both = r.cotangent[i, :, 2 * pair * z.O : (2 * pair + 2) * z.O].astype(F32)
            both = jnp.concatenate([both[:, : z.O], pad, both[:, z.O :], pad], axis=0)
            at = i * z.M + 2 * pair * z.hp
            r.cot[at : at + 2 * z.hp, :] = both.astype(BF16)
            sums += rows8(both)
        step = z.M // 2
        for at in range(0, z.M, step):
            r.pgrad[at : at + step, :] = dot(r.cot[i * z.M + at : i * z.M + at + step, :], r.merge_weight[...])

        def part(dr, ds, b, down=0):
            k = 3 * dr + ds
            return r.pgrad[pl.ds(b * z.hp + down, z.hp), k * z.C : (k + 1) * z.C]

        for b in range(z.half):
            planes = [
                part(1, 1, b),
                part(2, 1, b) + part(0, 1, b, 1),
                part(1, 2, b),
                part(2, 2, b) + part(0, 2, b, 1),
            ]
            if b < z.half - 1:
                planes[2] += part(1, 0, b + 1)
                planes[3] += part(2, 0, b + 1) + part(0, 0, b + 1, 1)
            for plane, (down, right) in zip(planes, ((0, 0), (1, 0), (0, 1), (1, 1))):
                start = down * z.W + (2 * b + right) * z.I + i
                r.grad[pl.ds(start, z.hp, stride=2 * z.W), :] = plane
    r.merge_bias_sums[...] = sums
    r.token[...] = jnp.zeros_like(r.token)


def shift_phase(z, r, cat, size):
    r.sums[...] = jnp.zeros_like(r.sums)

    def body(rows, at):
        start = z.base + at
        kind = kinds(z, size)
        mid = near(r.normed, start, 0, size)
        high = jnp.where(kind == 2, near(r.normed, start, -z.W, size), near(r.normed, start, z.W, size))
        wide = jnp.where(kind == 2, near(r.normed, start, -z.I, size), near(r.normed, start, z.I, size))
        high = jnp.where(kind == 0, mid, high).astype(BF16)
        wide = jnp.where(kind == 0, mid, wide * r.edge[rows, :].astype(F32)).astype(BF16)
        mask = r.mask[rows, :]
        for j, piece in enumerate((high, wide, mid.astype(BF16))):
            cat[rows, j * z.C : (j + 1) * z.C] = piece
            r.sums[j] += rows8(piece.astype(F32) * mask)

    over(z, body, size)


def counts_of(z, r):
    rows = []
    for i in range(GROUP):
        count = (r.sizes[i, 0] * r.sizes[i, 1]).astype(F32) if i < z.I else 1.0
        rows.append(jnp.full((1, z.C), 1.0, F32) * count)
    return jnp.concatenate(rows, axis=0)


def weigh_phase(z, r, l, o):
    pooled = r.mix_bias[l, 0:1] + r.mix_bias[l, 1:2]
    counts = counts_of(z, r)
    for j in range(3):
        pool = split(z, r.sums[j])
        o.pool[j] = pool
        pooled = pooled + fine(pool, r.mix_weight[l, j]) / counts
    o.pooled[...] = pooled
    act, slope = gelu_pair(fine(pooled, r.squeeze_weight[l], (1, 1)) + r.squeeze_bias[l : l + 1])
    o.act[...] = act
    o.slope[...] = slope
    logits = fine(act, r.ewp[l]) + r.ebp[l : l + 1]
    parts = [logits[:, j * z.C : (j + 1) * z.C] for j in range(3)]
    top = jnp.maximum(jnp.maximum(parts[0], parts[1]), parts[2])
    parts = [jnp.exp(part - top) for part in parts]
    whole = parts[0] + parts[1] + parts[2]
    for j in range(3):
        o.share[j] = parts[j] / whole


def mix_phase(z, r, l, o, size):
    share = [weave(z, o.share[j]) for j in range(3)]
    bias = tile(r.mix_bias[l, 0:1] * share[0] + r.mix_bias[l, 1:2] * share[1], size)
    share = [tile(s, size) for s in share]
    gain, shift = r.norm_gain[l, 1:2], r.norm_bias[l, 1:2]

    def body(rows, at):
        mixed = bias
        for j in range(3):
            mixed = mixed + dot(o.cat[rows, j * z.C : (j + 1) * z.C], r.mix_weight[l, j]) * share[j]
        mixed = mixed.astype(BF16)
        o.mixed[rows, :] = mixed
        token = dot(mixed, r.project_weight[l]) + r.project_bias[l : l + 1]
        halfway = r.state[rows, :] + r.mask[rows, :] * token
        unit, rstd = norm_parts(halfway)
        o.unit2[rows, :] = unit.astype(BF16)
        o.rstd2[rows, :] = rstd.astype(BF16)
        o.normed2[rows, :] = (unit * gain + shift).astype(BF16)
        r.state[rows, :] = halfway

    over(z, body, size)


def norm_store(z, r, l, o, rows, at, state):
    unit, rstd = norm_parts(state)
    o.unit1[rows, :] = unit.astype(BF16)
    o.rstd1[rows, :] = rstd.astype(BF16)
    r.normed[z.base + at : z.base + at + rows.stop - rows.start, :] = unit * r.norm_gain[l, 0:1] + r.norm_bias[l, 0:1]


def clear_edges(z, ref):
    ref[: z.base, :] = jnp.zeros((z.base, z.C), F32)
    ref[z.base + z.N0 :, :] = jnp.zeros((ref.shape[0] - z.base - z.N0, z.C), F32)


def feed_phase(z, r, l, o, after):
    def body(rows, at):
        pre = dot(o.normed2[rows, :], r.inner[l], (1, 1)) + r.inner_bias[l : l + 1]
        act, slope = gelu_pair(pre)
        act = act.astype(BF16)
        o.act_rows[rows, :] = act
        o.slope_rows[rows, :] = slope.astype(BF16)
        out = dot(act, r.outer[l]) + r.outer_bias[l : l + 1]
        state = r.state[rows, :] + r.mask[rows, :] * out
        after(rows, at, state)

    over(z, body, z.run_second)


def saved_early(z):
    return dict(
        unit1=kept(z.N, z.C, dtype=BF16), rstd1=kept(z.N, z.C, dtype=BF16), cat=kept(z.N, 3 * z.C, dtype=BF16), mixed=kept(z.N, z.C, dtype=BF16),
        unit2=kept(z.N, z.C, dtype=BF16), rstd2=kept(z.N, z.C, dtype=BF16), normed2=kept(z.N, z.C, dtype=BF16), pool=kept(3, GROUP, z.C),
        pooled=kept(GROUP, z.C), act=kept(GROUP, z.R), slope=kept(GROUP, z.R), share=kept(3, GROUP, z.C),
    )


def saved_late(z):
    return dict(act_rows=kept(z.N, z.H, dtype=BF16), slope_rows=kept(z.N, z.H, dtype=BF16))


def first_kernel(z, r):
    spots = lax.broadcasted_iota(jnp.int32, (3 * z.C, 3 * z.C), 0)
    ends = lax.broadcasted_iota(jnp.int32, (3 * z.C, 3 * z.C), 1)
    kind = jnp.where(ends >= 2 * z.C, 2, jnp.where(ends >= z.C, 1, 0))
    r.perm[...] = jnp.where(spots == 3 * (ends - kind * z.C) + kind, 1.0, 0.0).astype(BF16)
    for l in range(z.L):
        r.ewp[l] = fine(r.expand_weight[l], r.perm[...])
    r.ebp[...] = fine(r.expand_bias[...], r.perm[...])

    def begin(rows, at):
        real = min(rows.stop, z.N0) - at
        state = r.images[at : at + real, :].astype(F32) * r.mask[at : at + real, :]
        if real < rows.stop - at:
            state = jnp.concatenate([state, jnp.zeros((rows.stop - at - real, z.C), F32)], axis=0)
        r.state[rows, :] = state
        norm_store(z, r, 0, r, rows, at, state)

    over(z, begin, z.run_first)
    clear_edges(z, r.normed)
    shift_phase(z, r, r.cat, z.run_first)
    weigh_phase(z, r, 0, r)
    mix_phase(z, r, 0, r, z.run_first)
    r.token[...] = jnp.zeros_like(r.token)


def rank(z, e):
    at, half = 0, z.parts // 2
    while half:
        at, e, half = at + half * (e % 2), e // 2, half // 2
    return at


def put_blocks(z, me, rows, size, here, away, start=0):
    half = z.parts // 2
    for e in range(z.parts):
        at = rank(z, e)
        block = rows[pl.ds(pl.multiple_of((me ^ e) * size, 16), size), :]
        if at < half:
            here[at, start : start + size, :] = block
        else:
            away[at - half, start : start + size, :] = block


def second_kernel(z, r):
    me = r.place[0]
    for k, e in enumerate(z.found):
        at = pl.multiple_of((me ^ e) * z.units, z.units)
        for l in range(z.L):
            r.inner[l, pl.ds(at, z.units), :] = r.gathered[k, 2 * l * z.units : (2 * l + 1) * z.units, :]
            r.outer[l, pl.ds(at, z.units), :] = r.gathered[k, (2 * l + 1) * z.units : (2 * l + 2) * z.units, :]
        at = 2 * z.L * z.units
        r.bias_rows[me ^ e] = r.gathered[k, at : at + 16, :].astype(F32)
    for l in range(z.L):
        r.inner_bias[l : l + 1] = jnp.concatenate([r.bias_rows[h, l : l + 1, : z.units] for h in range(z.parts)], axis=1)
    early, late = [Refs() for _ in range(z.L)], [Refs() for _ in range(z.L)]
    for l in range(z.L):
        early[l].normed2 = r.normed2_0 if l == 0 else r.normed2
        early[l].act_rows = r.act_rows_0 if l == 0 else r.act_rows
        early[l].slope_rows = r.slope_rows_0 if l == 0 else r.slope_rows

    def then_norm(rows, at, state):
        r.state[rows, :] = state
        norm_store(z, r, 1, r, rows, at, state)

    r.state[...] = r.state_in[...]
    feed_phase(z, r, 0, early[0], then_norm)
    clear_edges(z, r.normed)
    shift_phase(z, r, r.cat, z.run_second)
    weigh_phase(z, r, 1, r)
    mix_phase(z, r, 1, r, z.run_second)

    def then_keep(rows, at, state):
        r.normed[z.base + at : z.base + at + rows.stop - rows.start, :] = state

    feed_phase(z, r, 1, early[1], then_keep)
    for i in range(z.I):
        for pair in range(z.half // 2):
            at = i * z.M + 2 * pair * z.hp
            for k in range(9):
                dr, ds = divmod(k, 3)
                two = []
                for b in (2 * pair, 2 * pair + 1):
                    col = 2 * b + ds - 1
                    if col < 0:
                        two.append(jnp.zeros((z.hp, z.C), F32))
                    else:
                        two.append(r.normed[pl.ds(dr * z.W + col * z.I + i, z.hp, stride=2 * z.W), :])
                r.patch[at : at + 2 * z.hp, k * z.C : (k + 1) * z.C] = jnp.concatenate(two, axis=0).astype(BF16)
    for i in range(z.I):
        for pair in range(z.half // 2):
            at = i * z.M + 2 * pair * z.hp
            merged = dot(r.patch[at : at + 2 * z.hp, :], r.merge_weight[...], (1, 1)) + r.merge_bias[...]
            wide = jnp.concatenate([merged[: z.half], merged[z.hp : z.hp + z.half]], axis=1)
            r.features[i, :, 2 * pair * z.O : (2 * pair + 2) * z.O] = wide.astype(BF16)
    for k in range(9):
        grad = dot(r.cot[...], r.patch[:, k * z.C : (k + 1) * z.C], (0, 0))
        r.merge_rows[k * z.O : (k + 1) * z.O, :] = grad.astype(BF16)
    bias = total(r.merge_bias_sums[...])
    rest = z.O - 2 * z.C
    rows = [bias[:, : z.C], bias[:, z.C : 2 * z.C]]
    rows += [jnp.concatenate([bias[:, 2 * z.C :], jnp.zeros((1, z.C - rest), F32)], axis=1)]
    rows += [jnp.zeros((z.parts * z.merge - 9 * z.O - 3, z.C), F32)]
    r.merge_rows[9 * z.O :, :] = jnp.concatenate(rows, axis=0).astype(BF16)
    put_blocks(z, me, r.merge_rows, z.merge, r.merge_here, r.merge_away)


def feed_back_kernel(z, l, r):
    gain = r.norm_gain[l, 1:2]
    for ref in (r.vec, r.inner_sums, r.g_outer, r.g_inner):
        ref[...] = jnp.zeros_like(ref)

    def body(rows, at):
        mask = r.mask[rows, :]
        grad = r.grad[rows, :]
        out = (grad * mask).astype(BF16)
        r.vec[0] += rows8(out.astype(F32))
        pre = (dot(out, r.outer[l], (1, 1)) * r.slope_rows[rows, :].astype(F32)).astype(BF16)
        r.inner_sums[...] += rows8(pre.astype(F32))
        r.g_outer[...] += dot(out, r.act_rows[rows, :], (0, 0))
        r.g_inner[...] += dot(r.normed2[rows, :], pre, (0, 0))
        normed_grad = dot(pre, r.inner[l])
        unit = r.unit2[rows, :].astype(F32)
        r.vec[1] += rows8(normed_grad * unit)
        r.vec[2] += rows8(normed_grad)
        r.half_grad[rows, :] = grad + norm_back(normed_grad, unit, r.rstd2[rows, :].astype(F32), gain)

    over(z, body, z.run_back)
    inner = total(r.inner_sums[...])
    small = [total(r.vec[k]) for k in range(3)]
    small += [inner[:, k * z.C : (k + 1) * z.C] for k in range(z.H // z.C)]
    small += [jnp.zeros((1, z.C), F32)]
    r.feed_small[...] = jnp.concatenate(small, axis=0)
    r.turned[0] = r.g_inner[...].T.astype(BF16)
    r.turned[1] = r.g_outer[...].T.astype(BF16)
    for k in range(2):
        put_blocks(z, r.place[0], r.turned.at[k], z.units, r.here, r.away, k * z.units)
    r.token[...] = jnp.zeros_like(r.token)


def token_back_kernel(z, l, r):
    for ref in (r.vec, r.g_project, r.g_mix):
        ref[...] = jnp.zeros_like(ref)
    even, odd = tile(parity(z, 0), z.run_back), tile(parity(z, 1), z.run_back)

    def body(rows, at):
        token = (r.half_grad[rows, :] * r.mask[rows, :]).astype(BF16)
        r.vec[0] += rows8(token.astype(F32))
        r.g_project[...] += dot(r.mixed[rows, :], token, (0, 0))
        mixed_grad = dot(token, r.project_weight[l], (1, 1))
        r.vec[1] += rows8(mixed_grad)
        both = jnp.concatenate([(mixed_grad * even).astype(BF16), (mixed_grad * odd).astype(BF16)], axis=1)
        r.mixed_grad[rows, :] = both
        r.g_mix[...] += dot(both, r.cat[rows, :], (0, 0))

    over(z, body, z.run_back)
    counts = counts_of(z, r)
    zeros = jnp.zeros((GROUP - z.I, z.C), F32)
    summed = split(z, r.vec[1])
    share = [r.share[j] for j in range(3)]
    mix, dp = [], []
    for j in range(3):
        weight = r.mix_weight[l, j].astype(F32)
        rows = []
        found = 0.0
        for i in range(z.I):
            block = r.g_mix[i * z.C : (i + 1) * z.C, j * z.C : (j + 1) * z.C].T
            rows.append(total(weight * block))
            found = found + block * share[j][i : i + 1]
            scaled = weight * share[j][i : i + 1]
            r.scaled[j * z.C : (j + 1) * z.C, i * z.C : (i + 1) * z.C] = scaled.astype(BF16)
        mix.append(found)
        dp.append(jnp.concatenate(rows + [zeros], axis=0))
    for j in range(2):
        dp[j] += summed * r.mix_bias[l, j : j + 1]
    even = dp[0] * share[0] + dp[1] * share[1] + dp[2] * share[2]
    dz = jnp.concatenate([share[j] * (dp[j] - even) for j in range(3)], axis=1)
    act, slope, pooled = r.act[...], r.slope[...], r.pooled[...]
    expand = fine(fine(act, dz, (0, 0)), r.perm[...], (1, 1))
    expand_bias = total(fine(dz, r.perm[...], (1, 1)))
    dact = fine(dz, r.ewp[l], (1, 1)) * slope
    squeeze = fine(dact, pooled, (0, 0))
    dpool = fine(dact, r.squeeze_weight[l])
    push = dpool / counts
    for j in range(3):
        mix[j] += fine(r.pool[j], push, (0, 0))
        r.push[j] = weave(z, fine(push, r.mix_weight[l, j], (1, 1)))
    for j in range(3):
        r.rows[j * z.C : (j + 1) * z.C, :] = mix[j].astype(BF16)
    r.rows[z.at_project : z.at_expand, :] = r.g_project[...].astype(BF16)
    for j in range(3):
        at = z.at_expand + j * z.R
        r.rows[at : at + z.R, :] = expand[:, j * z.C : (j + 1) * z.C].astype(BF16)
    r.rows[z.at_squeeze : z.at_small, :] = squeeze.astype(BF16)
    small = [total(share[j] * summed + dpool) for j in range(2)]
    small += [total(r.vec[0]), r.feed_small[: 3 + z.H // z.C, :]]
    small += [expand_bias[:, j * z.C : (j + 1) * z.C] for j in range(3)]
    small += [jnp.concatenate([total(dact), jnp.zeros((1, z.C - z.R), F32)], axis=1)]
    used = sum(row.shape[0] for row in small)
    small += [jnp.zeros((z.parts * z.shared - z.at_small - used, z.C), F32)]
    r.rows[z.at_small :, :] = jnp.concatenate(small, axis=0).astype(BF16)
    put_blocks(z, r.place[0], r.rows, z.shared, r.here, r.away)
    r.token[...] = jnp.zeros_like(r.token)


def mix_back_kernel(z, l, last, r):
    for ref in (r.back_h, r.back_w):
        clear_edges(z, ref)
    gain = r.norm_gain[l, 0:1]
    size = z.run_mix
    push = [tile(r.push[j], size) for j in range(3)]

    def spread(rows, at):
        mask = r.mask[rows, :]
        parts = dot(r.mixed_grad[rows, :], r.scaled[...], (1, 1))
        for j, ref in enumerate((r.back_h, r.back_w, r.back_c)):
            ref[z.base + at : z.base + at + size, :] = parts[:, j * z.C : (j + 1) * z.C] + mask * push[j]

    over(z, spread, size)
    r.vec[...] = jnp.zeros_like(r.vec)

    def body(rows, at):
        start = z.base + at
        kind = kinds(z, size)
        high = jnp.where(kind == 2, near(r.back_h, start, z.W, size), near(r.back_h, start, -z.W, size))
        wide = jnp.where(kind == 2, near(r.back_w, start, z.I, size), near(r.back_w, start, -z.I, size))
        high = jnp.where(kind == 0, near(r.back_h, start, 0, size), high)
        wide = jnp.where(kind == 0, near(r.back_w, start, 0, size), wide * r.back[rows, :].astype(F32))
        grad = high + wide + near(r.back_c, start, 0, size)
        unit = r.unit1[rows, :].astype(F32)
        r.vec[0] += rows8(grad * unit)
        r.vec[1] += rows8(grad)
        grad = r.half_grad[rows, :] + norm_back(grad, unit, r.rstd1[rows, :].astype(F32), gain)
        if last:
            real = min(rows.stop, z.N0) - at
            r.state_grad[at : at + real, :] = (grad * r.mask[rows, :])[:real]
        else:
            r.state_grad[rows, :] = grad

    over(z, body, size)
    stray = r.back_h[z.base + z.N0 - z.W : z.base + z.N0, :]
    r.vec[1] -= rows8(jnp.where(kinds(z, z.W) == 1, stray, 0.0))
    r.first_norm[...] = jnp.concatenate([total(r.vec[0]), total(r.vec[1])], axis=0)
    r.token[...] = jnp.zeros_like(r.token)


def final_outputs(z):
    return dict(
        mix_weight=arr(z.L, 3, z.C, z.C), mix_bias=arr(z.L, 2, z.C), squeeze_weight=arr(z.L, z.R, z.C),
        squeeze_bias=arr(z.L, z.R), expand_weight=arr(z.L, z.R, 3 * z.C), expand_bias=arr(z.L, 3 * z.C),
        project_weight=arr(z.L, z.C, z.C), project_bias=arr(z.L, z.C), norm_gain=arr(z.L, 2, z.C),
        norm_bias=arr(z.L, 2, z.C), inner_weight=arr(z.L, z.units, z.C), inner_bias=arr(z.L, z.units),
        outer_weight=arr(z.L, z.units, z.C), outer_bias=arr(z.L, z.C), merge_weight=arr(z.O, 9 * z.C),
        merge_bias=arr(1, z.O),
    )


def last_kernel(z, r):
    me = r.place[0]
    half = z.parts // 2
    size = z.shared
    for at in range(z.parts):
        spot = me ^ z.ranks[at]
        have, merge = (r.have, r.merge_have) if at < half else (r.got, r.merge_got)
        k = at % half
        rows = pl.ds(pl.multiple_of(spot * z.shared, 16), z.shared)
        r.rows[0, rows, :] = have[k * size : (k + 1) * size, :]
        r.rows[1, rows, :] = merge[k, :size, :]
        r.merge_rows[pl.ds(pl.multiple_of(spot * z.merge, 16), z.merge), :] = merge[k, size:, :]
    norms = r.have[half * size :, :].astype(F32) + r.got[half * size :, :].astype(F32)
    for l in range(z.L):
        rows = r.rows.at[l]

        def get(at, count):
            return rows[at : at + count, :].astype(F32)

        for j in range(3):
            r.mix_weight[l, j] = get(j * z.C, z.C)
            r.expand_weight[l, :, j * z.C : (j + 1) * z.C] = get(z.at_expand + j * z.R, z.R)
        r.project_weight[l] = get(z.at_project, z.C)
        r.squeeze_weight[l] = get(z.at_squeeze, z.R)
        small = get(z.at_small, 16)
        r.mix_bias[l] = small[0:2]
        r.project_bias[l : l + 1] = small[2:3]
        r.outer_bias[l : l + 1] = small[3:4]
        r.norm_gain[l] = jnp.concatenate([norms[2 * l : 2 * l + 1], small[4:5]], axis=0)
        r.norm_bias[l] = jnp.concatenate([norms[2 * l + 1 : 2 * l + 2], small[5:6]], axis=0)
        at = 6
        inner = jnp.zeros((1, z.units), F32)
        for k in range(z.H // z.C):
            for c in range(0, z.C, z.units):
                mine = jnp.where(me == (k * z.C + c) // z.units, 1.0, 0.0)
                inner = inner + small[at : at + 1, c : c + z.units] * mine
            at += 1
        r.inner_bias[l : l + 1] = inner
        for j in range(3):
            r.expand_bias[l : l + 1, j * z.C : (j + 1) * z.C] = small[at : at + 1]
            at += 1
        r.squeeze_bias[l : l + 1] = small[at : at + 1, : z.R]
        feed = r.feed_rows[2 * l * z.units : 2 * (l + 1) * z.units, :].astype(F32)
        r.inner_weight[l] = feed[: z.units]
        r.outer_weight[l] = feed[z.units :]
    for k in range(9):
        r.merge_weight[:, k * z.C : (k + 1) * z.C] = r.merge_rows[k * z.O : (k + 1) * z.O, :].astype(F32)
    small = r.merge_rows[9 * z.O : 9 * z.O + 16, :].astype(F32)
    r.merge_bias[:, : z.C] = small[0:1]
    r.merge_bias[:, z.C : 2 * z.C] = small[1:2]
    r.merge_bias[:, 2 * z.C :] = small[2:3, : z.O - 2 * z.C]


def pack_kernel(z, r):
    u = z.units
    for l in range(z.L):
        r.block[2 * l * u : (2 * l + 1) * u, :] = r.inner_weight[l]
        r.block[(2 * l + 1) * u : (2 * l + 2) * u, :] = r.outer_weight[l]
    bias = r.inner_bias[...].astype(F32)
    if u < z.C:
        bias = jnp.concatenate([bias, jnp.zeros((z.L, z.C - u), F32)], axis=1)
    bias = jnp.concatenate([bias, jnp.zeros((16 - z.L, z.C), F32)], axis=0)
    r.block[2 * z.L * u :, :] = bias.astype(BF16)


def swap(x, axis, n, bit):
    return lax.ppermute(x, axis, [(a, a ^ bit) for a in range(n)])


def bits_of(n):
    return [1 << k for k in range(n.bit_length() - 1)]


def add(here, got, token):
    out = here.astype(F32) + got.astype(F32)
    if token is not None:
        out = out + token[0]
    return out.astype(BF16)


def take(tokens):
    return tokens.pop(0) if tokens else None


class Chain:
    def __init__(self, parts, hid, img):
        self.here = jnp.concatenate([part["here"] for part in parts], axis=1)
        self.away = jnp.concatenate([part["away"] for part in parts], axis=1)
        self.left = [("hid", hid, bit) for bit in bits_of(hid)] + [("img", img, bit) for bit in bits_of(img)]

    def held(self):
        return self.here

    def step(self, token=None, extra=None):
        axis, n, bit = self.left.pop(0)
        x = add(self.here, swap(self.away, axis, n, bit), token)
        if x.shape[0] > 1:
            half = x.shape[0] // 2
            self.here, self.away = x[:half], x[half:]
        else:
            if extra is not None and axis == "hid":
                x = jnp.concatenate([x, extra[None]], axis=1)
            self.here = self.away = x

    def finish(self, extra=None):
        while self.left:
            self.step(None, extra)
        return self.here[0]


def per_device(
    img, hid, images, sizes, cotangent, mix_weight, mix_bias, squeeze_weight, squeeze_bias, expand_weight, expand_bias,
    project_weight, project_bias, norm_gain, norm_bias, inner_weight, inner_bias, outer_weight, outer_bias,
    merge_weight, merge_bias,
):
    z = Sizes(
        images.shape[0], images.shape[1], images.shape[3], inner_weight.shape[2] * hid, squeeze_weight.shape[2],
        merge_weight.shape[1], mix_weight.shape[0], hid,
    )
    z.ranks = sorted(range(hid), key=partial(rank, z))
    place = lax.axis_index("hid").reshape(1)
    flat = images.transpose(1, 2, 0, 3).reshape(z.N0, z.C)
    merge_t = merge_weight.T
    squeeze_t = squeeze_weight.transpose(0, 2, 1)
    block = call(
        partial(pack_kernel, z),
        dict(inner_weight=inner_weight.transpose(0, 2, 1), outer_weight=outer_weight, inner_bias=inner_bias, place=place),
        dict(block=kept(2 * z.L * z.units + 16, z.C, dtype=BF16)), {}, 2, 1, dict(place=0),
    )
    block = block["block"]
    smem = dict(sizes=0, place=0)
    small = dict(
        mix_weight=mix_weight, mix_bias=mix_bias, squeeze_weight=squeeze_t, squeeze_bias=squeeze_bias,
        project_weight=project_weight, project_bias=project_bias, norm_gain=norm_gain, norm_bias=norm_bias,
    )
    token = dict(token=arr(1, z.C))
    a = call(
        partial(front_kernel, z),
        dict(sizes=sizes, cotangent=cotangent, merge_weight=merge_t),
        dict(
            mask=kept(z.N, z.C), edge=kept(z.N, z.C, dtype=BF16), back=kept(z.N, z.C, dtype=BF16), cot=kept(z.I * z.M, z.O, dtype=BF16),
            grad=kept(z.tall, z.C), merge_bias_sums=kept(8, z.O), **token,
        ),
        dict(pgrad=kept(z.M + 8, 9 * z.C)),
        4, 3, smem,
    )
    order = bits_of(hid)[1:] + [1]

    def widen(have, bit, token):
        got = swap(have, "hid", hid, bit)
        return jnp.concatenate([have, got if token is None else got + token.astype(BF16)], axis=0)

    z.found = [0]
    for bit in order:
        z.found = z.found + [e ^ bit for e in z.found]
    have = widen(block[None], order[0], a["token"])
    b = call(
        partial(first_kernel, z),
        dict(
            images=flat, sizes=sizes, mask=a["mask"], edge=a["edge"], expand_weight=expand_weight, expand_bias=expand_bias,
            **small,
        ),
        dict(
            state=kept(z.N, z.C), perm=kept(3 * z.C, 3 * z.C, dtype=BF16), ewp=kept(z.L, z.R, 3 * z.C),
            ebp=kept(z.L, 3 * z.C), **saved_early(z), **token,
        ),
        dict(normed=kept(z.long, z.C), sums=kept(3, 8, z.C)),
        5, 5, smem, have,
    )
    for bit in order[1:]:
        have = widen(have, bit, b["token"] if bit == order[1] else None)
    late = saved_late(z)
    c = call(
        partial(second_kernel, z),
        dict(
            sizes=sizes, mask=a["mask"], edge=a["edge"], state_in=b["state"], normed2_0=b["normed2"], gathered=have, place=place,
            ewp=b["ewp"], ebp=b["ebp"], outer_bias=outer_bias, merge_weight=merge_t, merge_bias=merge_bias.reshape(1, -1),
            cot=a["cot"], merge_bias_sums=a["merge_bias_sums"], **small,
        ),
        dict(
            features=arr(z.I, z.half, z.half * z.O, dtype=BF16),
            merge_here=kept(z.parts // 2, z.merge, z.C, dtype=BF16), merge_away=kept(z.parts // 2, z.merge, z.C, dtype=BF16),
            inner=kept(z.L, z.H, z.C, dtype=BF16), outer=kept(z.L, z.H, z.C, dtype=BF16),
            act_rows_0=late["act_rows"], slope_rows_0=late["slope_rows"], **saved_early(z), **late,
        ),
        dict(
            state=kept(z.N, z.C), normed=kept(z.tall, z.C), sums=kept(3, 8, z.C), inner_bias=kept(z.L, z.H), bias_rows=kept(z.parts, 16, z.C),
            patch=kept(z.I * z.M, 9 * z.C, dtype=BF16), merge_rows=kept(z.parts * z.merge, z.C, dtype=BF16),
        ),
        11, 16, smem,
    )
    first = dict(b, act_rows=c["act_rows_0"], slope_rows=c["slope_rows_0"])

    def some(s, **names):
        return {name: s[name] for name in names}

    grad = a["grad"]
    shares, norms = [None] * z.L, [None] * z.L
    chain = None
    for l in reversed(range(z.L)):
        s = c if l else first
        d = call(
            partial(feed_back_kernel, z, l),
            dict(
                place=place, mask=a["mask"], grad=grad, inner=c["inner"], outer=c["outer"], norm_gain=norm_gain,
                **some(s, act_rows=0, slope_rows=0, normed2=0, unit2=0, rstd2=0),
            ),
            dict(
                half_grad=kept(z.N, z.C), feed_small=arr(8, z.C), here=kept(z.parts // 2, 2 * z.units, z.C, dtype=BF16),
                away=kept(z.parts // 2, 2 * z.units, z.C, dtype=BF16), **token,
            ),
            dict(
                vec=kept(3, 8, z.C), inner_sums=kept(8, z.H), g_outer=kept(z.C, z.H), g_inner=kept(z.C, z.H),
                turned=kept(2, z.H, z.C, dtype=BF16),
            ),
            6, 4, smem, chain and chain.held(),
        )
        if chain:
            chain.step(d["token"])
        t = call(
            partial(token_back_kernel, z, l),
            dict(
                sizes=sizes, place=place, mask=a["mask"], half_grad=d["half_grad"], feed_small=d["feed_small"],
                perm=b["perm"], ewp=b["ewp"], **some(s, mixed=0, cat=0, share=0, pool=0, pooled=0, act=0, slope=0), **small,
            ),
            dict(
                mixed_grad=kept(z.N, z.I * z.C, dtype=BF16), scaled=kept(3 * z.C, z.I * z.C, dtype=BF16),
                push=kept(3, 8, z.C), here=kept(z.parts // 2, z.shared, z.C, dtype=BF16),
                away=kept(z.parts // 2, z.shared, z.C, dtype=BF16), **token,
            ),
            dict(
                vec=kept(2, 8, z.C), g_project=kept(z.C, z.C), g_mix=kept(z.I * z.C, 3 * z.C),
                rows=kept(z.parts * z.shared, z.C, dtype=BF16),
            ),
            4, 4, smem, chain and chain.held(),
        )
        parts = [d, t]
        if chain:
            chain.step(t["token"])
        elif l:
            parts += [dict(here=c["merge_here"], away=c["merge_away"])]
            chain = Chain(parts, hid, img)
        if not l:
            tail = Chain(parts, hid, img)
        e = call(
            partial(mix_back_kernel, z, l, l == 0),
            dict(
                mask=a["mask"], back=a["back"], norm_gain=norm_gain, half_grad=d["half_grad"],
                **some(t, mixed_grad=0, scaled=0, push=0), **some(s, unit1=0, rstd1=0),
            ),
            dict(state_grad=kept(z.N, z.C) if l else arr(z.N0, z.C), first_norm=arr(2, z.C), **token),
            dict(back_h=kept(z.long, z.C), back_w=kept(z.long, z.C), back_c=kept(z.long, z.C), vec=kept(2, 8, z.C)),
            5, 3, (), chain and chain.held(),
        )
        if chain:
            chain.step(e["token"])
        grad, norms[l] = e["state_grad"], e["first_norm"]
    images_grad = grad.reshape(z.side, z.side, z.I, z.C).transpose(2, 0, 1, 3)

    early = chain.finish()
    tail.step(e["token"])
    norm_rows = jnp.pad(jnp.concatenate(norms, axis=0), ((0, 16 - 2 * z.L), (0, 0))).astype(BF16)
    late_rows = tail.finish(norm_rows)
    feed = 2 * z.units
    cut = feed + z.shared
    feed_rows = jnp.concatenate([late_rows[:feed], early[:feed]], axis=0)
    have, norm_rows = late_rows[feed:cut], late_rows[cut:]
    merge = early[None, feed:]
    for bit in bits_of(hid)[::-1]:
        sent = jnp.concatenate([have, norm_rows], axis=0)
        got, merge_got = swap(sent, "hid", hid, bit), swap(merge, "hid", hid, bit)
        if bit > 1:
            have = jnp.concatenate([have, got[:-16]], axis=0)
            norm_rows = add(norm_rows, got[-16:], None)
            merge = jnp.concatenate([merge, merge_got], axis=0)
    g = call(
        partial(last_kernel, z),
        dict(place=place, have=sent, got=got, merge_have=merge, merge_got=merge_got, feed_rows=feed_rows),
        final_outputs(z),
        dict(rows=kept(z.L, z.parts * z.shared, z.C, dtype=BF16), merge_rows=kept(z.parts * z.merge, z.C, dtype=BF16)),
        5, 2, smem,
    )
    return (
        c["features"], images_grad, g["mix_weight"], g["mix_bias"], g["squeeze_weight"].transpose(0, 2, 1),
        g["squeeze_bias"], g["expand_weight"], g["expand_bias"], g["project_weight"], g["project_bias"], g["norm_gain"],
        g["norm_bias"], g["inner_weight"].transpose(0, 2, 1), g["inner_bias"], g["outer_weight"], g["outer_bias"],
        g["merge_weight"].T, g["merge_bias"].reshape(-1),
    )


def solution(mesh):
    maps = ("img", "hid")
    in_specs = (
        P(maps, None, None, None), P(maps, None), P(maps, None, None), P(), P(), P(), P(), P(), P(), P(), P(), P(), P(),
        P(None, None, "hid"), P(None, "hid"), P(None, "hid", None), P(), P(), P(),
    )
    out_specs = (
        P(maps, None, None), P(maps, None, None, None), P(), P(), P(), P(), P(), P(), P(), P(), P(), P(),
        P(None, None, "hid"), P(None, "hid"), P(None, "hid", None), P(), P(), P(),
    )
    return jax.shard_map(
        partial(per_device, mesh.shape["img"], mesh.shape["hid"]),
        mesh=mesh, in_specs=in_specs, out_specs=out_specs, check_vma=False,
    )
```

```python
from functools import partial

import jax
import jax.numpy as jnp
from jax import lax
from jax.experimental import pallas as pl
from jax.experimental.pallas import tpu as pltpu
from jax.sharding import PartitionSpec as P

F32 = jnp.float32
BF16 = jnp.bfloat16
GROUP = 8
MIB = 2**20


def dot(a, b, dims=(1, 0)):
    return lax.dot_general(a, b, (((dims[0],), (dims[1],)), ((), ())), preferred_element_type=F32)


def halves(v):
    high = v.astype(BF16)
    return high, (v - high.astype(F32)).astype(BF16)


def fine(a, b, dims=(1, 0)):
    high, low = halves(a)
    if b.dtype == BF16:
        return dot(high, b, dims) + dot(low, b, dims)
    b_high, b_low = halves(b)
    return dot(high, b_high, dims) + (dot(low, b_high, dims) + dot(high, b_low, dims))


def rows8(v):
    return v.reshape(-1, 8, v.shape[-1]).sum(axis=0)


def total(v):
    return v.sum(axis=0, keepdims=True)


def tile(v, rows):
    return jnp.broadcast_to(v[None], (rows // 8, 8, v.shape[-1])).reshape(rows, v.shape[-1])


def gelu_pair(x):
    cdf = 0.5 * lax.erf(x * 0.7071067811865476) + 0.5
    bell = jnp.exp2(x * x * (-0.5 * 1.4426950408889634))
    return x * cdf, cdf + x * bell * 0.3989422804014327


def norm_parts(v):
    centred = v - jnp.mean(v, axis=-1, keepdims=True)
    rstd = lax.rsqrt(jnp.mean(centred * centred, axis=-1, keepdims=True) + 1e-05)
    return centred * rstd, jnp.broadcast_to(rstd, v.shape)


def norm_back(grad, unit, rstd, gain):
    scaled = grad * gain
    first = jnp.mean(scaled, axis=-1, keepdims=True)
    second = jnp.mean(scaled * unit, axis=-1, keepdims=True)
    return rstd * (scaled - first - unit * second)


class Sizes:
    def __init__(self, images, side, channels, hidden, red, out, layers, parts):
        self.I, self.side, self.C, self.H, self.R, self.O, self.L = images, side, channels, hidden, red, out, layers
        self.parts, self.units = parts, hidden // parts
        self.W = side * images
        self.N0 = side * self.W
        self.N = -(-self.N0 // 384) * 384
        self.run_first = self.run_back = self.run_mix = self.N
        self.run_second = self.N // 7
        self.half = side // 2
        self.hp = -(-self.half // 8) * 8
        self.M = self.half * self.hp
        self.base = self.W
        self.tall = self.W * (2 * self.hp + 2)
        self.long = self.base + self.N + self.W
        self.at_project = 3 * channels
        self.at_expand = self.at_project + channels
        self.at_squeeze = self.at_expand + 3 * red
        self.at_small = self.at_squeeze + red
        self.shared = -(-(self.at_small + 16) // (16 * parts)) * 16
        self.merge = -(-(9 * out + 3) // (16 * parts)) * 16


class Refs:
    pass


def call(body, ins, outs, scratch, limit, micros, smem=(), after=(), far=()):
    waits = {f"after{k}": array for k, array in enumerate(after)}
    ins = dict(ins, **waits)
    vmem = pl.BlockSpec(memory_space=pltpu.VMEM)
    scalar, anywhere = pl.BlockSpec(memory_space=pltpu.SMEM), pl.BlockSpec(memory_space=pl.ANY)

    def place(name):
        return scalar if name in smem else anywhere if name in waits or name in far else vmem

    names = list(ins) + list(outs) + list(scratch)

    def kernel(*refs):
        r = Refs()
        for name, ref in zip(names, refs):
            setattr(r, name, ref)
        body(r)

    found = pl.pallas_call(
        kernel,
        out_shape=list(outs.values()),
        in_specs=[place(name) for name in ins],
        out_specs=[vmem] * len(outs),
        scratch_shapes=list(scratch.values()),
        compiler_params=pltpu.CompilerParams(vmem_limit_bytes=limit * MIB),
        cost_estimate=pl.CostEstimate(flops=int(micros * 1.15e9), bytes_accessed=0, transcendentals=0),
    )(*ins.values())
    return dict(zip(outs, found))


def arr(*shape, dtype=F32):
    return jax.ShapeDtypeStruct(shape, dtype)


def kept(*shape, dtype=F32):
    return pltpu.VMEM(shape, dtype)


def over(z, body, size):
    for at in range(0, z.N, size):
        body(slice(at, at + size), at)


def near(ref, start, off, size):
    return ref[start + off : start + off + size, :]


def parity(z, i):
    rows = lax.broadcasted_iota(jnp.int32, (8, z.C), 0)
    return jnp.where(rows % z.I == i, 1.0, 0.0)


def kinds(z, rows):
    return tile(lax.broadcasted_iota(jnp.int32, (8, z.C), 1) % 3, rows)


def weave(z, v):
    out = v[0:1] * parity(z, 0)
    for i in range(1, z.I):
        out += v[i : i + 1] * parity(z, i)
    return out


def split(z, v):
    rows = [total(v * parity(z, i)) for i in range(z.I)]
    return jnp.concatenate(rows + [jnp.zeros((GROUP - z.I, z.C), F32)], axis=0)


def front_kernel(z, r):
    rows = lax.broadcasted_iota(jnp.int32, (z.W, z.C), 0)
    lanes = lax.broadcasted_iota(jnp.int32, (z.W, z.C), 1) % 3
    image = rows % z.I
    col = rows // z.I
    high = jnp.zeros((z.W, z.C), jnp.int32)
    wide = jnp.zeros((z.W, z.C), jnp.int32)
    for i in range(z.I):
        high = jnp.where(image == i, r.sizes[i, 0], high)
        wide = jnp.where(image == i, r.sizes[i, 1], wide)
    inside = jnp.where(col < wide, 1.0, 0.0)
    first, last = col == 0, col == z.side - 1
    edge = jnp.where((first & (lanes == 2)) | (last & (lanes == 1)), 0.0, 1.0)
    back = jnp.where((last & (lanes == 2)) | (first & (lanes == 1)), 0.0, 1.0)

    def step(row, carry):
        at = pl.ds(pl.multiple_of(row * z.W, 8), z.W)
        r.mask[at, :] = jnp.where(high > row, inside, 0.0)
        return carry

    lax.fori_loop(0, z.side, step, 0)
    edge = jnp.concatenate([edge, edge], axis=0).astype(BF16)
    back = jnp.concatenate([back, back], axis=0).astype(BF16)

    def step2(row, carry):
        at = pl.ds(pl.multiple_of(row * 2 * z.W, 16), 2 * z.W)
        r.edge[at, :] = edge
        r.back[at, :] = back
        return carry

    lax.fori_loop(0, z.side // 2, step2, 0)
    pad = jnp.zeros((z.N - z.N0, z.C), F32)
    for ref in (r.mask, r.edge, r.back):
        ref[z.N0 :, :] = pad.astype(ref.dtype)
    pad = jnp.zeros((z.hp - z.half, z.O), F32)
    r.pgrad[z.M :, :] = jnp.zeros((8, 9 * z.C), F32)
    sums = jnp.zeros((8, z.O), F32)
    for i in range(z.I):
        for pair in range(z.half // 2):
            both = r.cotangent[i, :, 2 * pair * z.O : (2 * pair + 2) * z.O].astype(F32)
            both = jnp.concatenate([both[:, : z.O], pad, both[:, z.O :], pad], axis=0)
            at = i * z.M + 2 * pair * z.hp
            r.cot[at : at + 2 * z.hp, :] = both.astype(BF16)
            sums += rows8(both)
        step = z.M // 2
        for at in range(0, z.M, step):
            r.pgrad[at : at + step, :] = dot(r.cot[i * z.M + at : i * z.M + at + step, :], r.merge_weight[...])

        def part(dr, ds, b, down=0):
            k = 3 * dr + ds
            return r.pgrad[pl.ds(b * z.hp + down, z.hp), k * z.C : (k + 1) * z.C]

        for b in range(z.half):
            planes = [
                part(1, 1, b),
                part(2, 1, b) + part(0, 1, b, 1),
                part(1, 2, b),
                part(2, 2, b) + part(0, 2, b, 1),
            ]
            if b < z.half - 1:
                planes[2] += part(1, 0, b + 1)
                planes[3] += part(2, 0, b + 1) + part(0, 0, b + 1, 1)
            for plane, (down, right) in zip(planes, ((0, 0), (1, 0), (0, 1), (1, 1))):
                start = down * z.W + (2 * b + right) * z.I + i
                r.grad[pl.ds(start, z.hp, stride=2 * z.W), :] = plane
    r.merge_bias_sums[...] = sums
    r.token[...] = jnp.zeros_like(r.token)


def shift_phase(z, r, cat, size):
    r.sums[...] = jnp.zeros_like(r.sums)

    def body(rows, at):
        start = z.base + at
        kind = kinds(z, size)
        mid = near(r.normed, start, 0, size)
        high = jnp.where(kind == 2, near(r.normed, start, -z.W, size), near(r.normed, start, z.W, size))
        wide = jnp.where(kind == 2, near(r.normed, start, -z.I, size), near(r.normed, start, z.I, size))
        high = jnp.where(kind == 0, mid, high).astype(BF16)
        wide = jnp.where(kind == 0, mid, wide * r.edge[rows, :].astype(F32)).astype(BF16)
        mask = r.mask[rows, :]
        for j, piece in enumerate((high, wide, mid.astype(BF16))):
            cat[rows, j * z.C : (j + 1) * z.C] = piece
            r.sums[j] += rows8(piece.astype(F32) * mask)

    over(z, body, size)


def counts_of(z, r):
    rows = []
    for i in range(GROUP):
        count = (r.sizes[i, 0] * r.sizes[i, 1]).astype(F32) if i < z.I else 1.0
        rows.append(jnp.full((1, z.C), 1.0, F32) * count)
    return jnp.concatenate(rows, axis=0)


def weigh_phase(z, r, l, o):
    pooled = r.mix_bias[l, 0:1] + r.mix_bias[l, 1:2]
    counts = counts_of(z, r)
    for j in range(3):
        pool = split(z, r.sums[j])
        o.pool[j] = pool
        pooled = pooled + fine(pool, r.mix_weight[l, j]) / counts
    o.pooled[...] = pooled
    act, slope = gelu_pair(fine(pooled, r.squeeze_weight[l], (1, 1)) + r.squeeze_bias[l : l + 1])
    o.act[...] = act
    o.slope[...] = slope
    logits = fine(act, r.ewp[l]) + r.ebp[l : l + 1]
    parts = [logits[:, j * z.C : (j + 1) * z.C] for j in range(3)]
    top = jnp.maximum(jnp.maximum(parts[0], parts[1]), parts[2])
    parts = [jnp.exp(part - top) for part in parts]
    whole = parts[0] + parts[1] + parts[2]
    for j in range(3):
        o.share[j] = parts[j] / whole


def mix_phase(z, r, l, o, size):
    share = [weave(z, o.share[j]) for j in range(3)]
    bias = tile(r.mix_bias[l, 0:1] * share[0] + r.mix_bias[l, 1:2] * share[1], size)
    share = [tile(s, size) for s in share]
    gain, shift = r.norm_gain[l, 1:2], r.norm_bias[l, 1:2]

    def body(rows, at):
        mixed = bias
        for j in range(3):
            mixed = mixed + dot(o.cat[rows, j * z.C : (j + 1) * z.C], r.mix_weight[l, j]) * share[j]
        mixed = mixed.astype(BF16)
        o.mixed[rows, :] = mixed
        token = dot(mixed, r.project_weight[l]) + r.project_bias[l : l + 1]
        halfway = r.state[rows, :] + r.mask[rows, :] * token
        unit, rstd = norm_parts(halfway)
        o.unit2[rows, :] = unit.astype(BF16)
        o.rstd2[rows, :] = rstd.astype(BF16)
        o.normed2[rows, :] = (unit * gain + shift).astype(BF16)
        r.state[rows, :] = halfway

    over(z, body, size)


def norm_store(z, r, l, o, rows, at, state):
    unit, rstd = norm_parts(state)
    o.unit1[rows, :] = unit.astype(BF16)
    o.rstd1[rows, :] = rstd.astype(BF16)
    r.normed[z.base + at : z.base + at + rows.stop - rows.start, :] = unit * r.norm_gain[l, 0:1] + r.norm_bias[l, 0:1]


def clear_edges(z, ref):
    ref[: z.base, :] = jnp.zeros((z.base, z.C), F32)
    ref[z.base + z.N0 :, :] = jnp.zeros((ref.shape[0] - z.base - z.N0, z.C), F32)


def feed_phase(z, r, l, o, after):
    def body(rows, at):
        pre = dot(o.normed2[rows, :], r.inner[l], (1, 1)) + r.inner_bias[l : l + 1]
        act, slope = gelu_pair(pre)
        act = act.astype(BF16)
        o.act_rows[rows, :] = act
        o.slope_rows[rows, :] = slope.astype(BF16)
        out = dot(act, r.outer[l]) + r.outer_bias[l : l + 1]
        state = r.state[rows, :] + r.mask[rows, :] * out
        after(rows, at, state)

    over(z, body, z.run_second)


def saved_early(z):
    return dict(
        unit1=kept(z.N, z.C, dtype=BF16), rstd1=kept(z.N, z.C, dtype=BF16), cat=kept(z.N, 3 * z.C, dtype=BF16), mixed=kept(z.N, z.C, dtype=BF16),
        unit2=kept(z.N, z.C, dtype=BF16), rstd2=kept(z.N, z.C, dtype=BF16), normed2=kept(z.N, z.C, dtype=BF16), pool=kept(3, GROUP, z.C),
        pooled=kept(GROUP, z.C), act=kept(GROUP, z.R), slope=kept(GROUP, z.R), share=kept(3, GROUP, z.C),
    )


def saved_late(z):
    return dict(act_rows=kept(z.N, z.H, dtype=BF16), slope_rows=kept(z.N, z.H, dtype=BF16))


def first_kernel(z, r):
    spots = lax.broadcasted_iota(jnp.int32, (3 * z.C, 3 * z.C), 0)
    ends = lax.broadcasted_iota(jnp.int32, (3 * z.C, 3 * z.C), 1)
    kind = jnp.where(ends >= 2 * z.C, 2, jnp.where(ends >= z.C, 1, 0))
    r.perm[...] = jnp.where(spots == 3 * (ends - kind * z.C) + kind, 1.0, 0.0).astype(BF16)
    for l in range(z.L):
        r.ewp[l] = fine(r.expand_weight[l], r.perm[...])
    r.ebp[...] = fine(r.expand_bias[...], r.perm[...])

    def begin(rows, at):
        real = min(rows.stop, z.N0) - at
        state = r.images[at : at + real, :].astype(F32) * r.mask[at : at + real, :]
        if real < rows.stop - at:
            state = jnp.concatenate([state, jnp.zeros((rows.stop - at - real, z.C), F32)], axis=0)
        r.state[rows, :] = state
        norm_store(z, r, 0, r, rows, at, state)

    over(z, begin, z.run_first)
    clear_edges(z, r.normed)
    shift_phase(z, r, r.cat, z.run_first)
    weigh_phase(z, r, 0, r)
    mix_phase(z, r, 0, r, z.run_first)
    r.token[...] = jnp.zeros_like(r.token)


def exchange_order(n):
    bits = bits_of(n)
    return bits[:1] + bits[:0:-1]


def rank(n, e):
    return sum((n >> k + 1) * (e // bit % 2) for k, bit in enumerate(exchange_order(n)))


def put_blocks(z, me, rows, size, here, away, start=0):
    half = z.parts // 2
    for e in range(z.parts):
        at = rank(z.parts, e)
        block = rows[pl.ds(pl.multiple_of((me ^ e) * size, 16), size), :]
        if at < half:
            here[at, start : start + size, :] = block
        else:
            away[at - half, start : start + size, :] = block


def second_kernel(z, r):
    me = r.place[0]
    for k, e in enumerate(z.gathered):
        at = pl.multiple_of((me ^ e) * z.units, z.units)
        for l in range(z.L):
            r.inner[l, pl.ds(at, z.units), :] = r.gathered[k, 2 * l * z.units : (2 * l + 1) * z.units, :]
            r.outer[l, pl.ds(at, z.units), :] = r.gathered[k, (2 * l + 1) * z.units : (2 * l + 2) * z.units, :]
        at = 2 * z.L * z.units
        r.bias_rows[me ^ e] = r.gathered[k, at : at + 16, :].astype(F32)
    for l in range(z.L):
        r.inner_bias[l : l + 1] = jnp.concatenate([r.bias_rows[h, l : l + 1, : z.units] for h in range(z.parts)], axis=1)
    early, late = [Refs() for _ in range(z.L)], [Refs() for _ in range(z.L)]
    for l in range(z.L):
        early[l].normed2 = r.normed2_0 if l == 0 else r.normed2
        early[l].act_rows = r.act_rows_0 if l == 0 else r.act_rows
        early[l].slope_rows = r.slope_rows_0 if l == 0 else r.slope_rows

    def then_norm(rows, at, state):
        r.state[rows, :] = state
        norm_store(z, r, 1, r, rows, at, state)

    r.state[...] = r.state_in[...]
    feed_phase(z, r, 0, early[0], then_norm)
    clear_edges(z, r.normed)
    shift_phase(z, r, r.cat, z.run_second)
    weigh_phase(z, r, 1, r)
    mix_phase(z, r, 1, r, z.run_second)

    def then_keep(rows, at, state):
        r.normed[z.base + at : z.base + at + rows.stop - rows.start, :] = state

    feed_phase(z, r, 1, early[1], then_keep)
    for i in range(z.I):
        for pair in range(z.half // 2):
            at = i * z.M + 2 * pair * z.hp
            for k in range(9):
                dr, ds = divmod(k, 3)
                two = []
                for b in (2 * pair, 2 * pair + 1):
                    col = 2 * b + ds - 1
                    if col < 0:
                        two.append(jnp.zeros((z.hp, z.C), F32))
                    else:
                        two.append(r.normed[pl.ds(dr * z.W + col * z.I + i, z.hp, stride=2 * z.W), :])
                r.patch[at : at + 2 * z.hp, k * z.C : (k + 1) * z.C] = jnp.concatenate(two, axis=0).astype(BF16)
    for k in range(9):
        grad = dot(r.cot[...], r.patch[:, k * z.C : (k + 1) * z.C], (0, 0))
        r.merge_rows[k * z.O : (k + 1) * z.O, :] = grad.astype(BF16)
    bias = total(r.merge_bias_sums[...])
    rest = z.O - 2 * z.C
    rows = [bias[:, : z.C], bias[:, z.C : 2 * z.C]]
    rows += [jnp.concatenate([bias[:, 2 * z.C :], jnp.zeros((1, z.C - rest), F32)], axis=1)]
    rows += [jnp.zeros((z.parts * z.merge - 9 * z.O - 3, z.C), F32)]
    r.merge_rows[9 * z.O :, :] = jnp.concatenate(rows, axis=0).astype(BF16)
    put_blocks(z, me, r.merge_rows, z.merge, r.merge_here, r.merge_away)


def features_kernel(z, r):
    r.merged[...] = dot(r.patch[...], r.merge_weight[...], (1, 1)) + r.merge_bias[...]
    r.token[...] = jnp.zeros_like(r.token)
    for i in range(z.I):
        for pair in range(z.half // 2):
            at = i * z.M + 2 * pair * z.hp
            wide = [r.merged[at : at + z.half, :], r.merged[at + z.hp : at + z.hp + z.half, :]]
            wide = jnp.concatenate(wide, axis=1).astype(BF16)
            r.features[i, :, 2 * pair * z.O : (2 * pair + 2) * z.O] = wide


def feed_back_kernel(z, l, r):
    gain = r.norm_gain[l, 1:2]
    for ref in (r.vec, r.inner_sums, r.g_outer, r.g_inner):
        ref[...] = jnp.zeros_like(ref)

    def body(rows, at):
        mask = r.mask[rows, :]
        grad = r.grad[rows, :]
        out = (grad * mask).astype(BF16)
        r.vec[0] += rows8(out.astype(F32))
        pre = (dot(out, r.outer[l], (1, 1)) * r.slope_rows[rows, :].astype(F32)).astype(BF16)
        r.inner_sums[...] += rows8(pre.astype(F32))
        r.g_outer[...] += dot(out, r.act_rows[rows, :], (0, 0))
        r.g_inner[...] += dot(r.normed2[rows, :], pre, (0, 0))
        normed_grad = dot(pre, r.inner[l])
        unit = r.unit2[rows, :].astype(F32)
        r.vec[1] += rows8(normed_grad * unit)
        r.vec[2] += rows8(normed_grad)
        r.half_grad[rows, :] = grad + norm_back(normed_grad, unit, r.rstd2[rows, :].astype(F32), gain)

    over(z, body, z.run_back)
    inner = total(r.inner_sums[...])
    small = [total(r.vec[k]) for k in range(3)]
    small += [inner[:, k * z.C : (k + 1) * z.C] for k in range(z.H // z.C)]
    small += [jnp.zeros((1, z.C), F32)]
    r.feed_small[...] = jnp.concatenate(small, axis=0)
    r.turned[0] = r.g_inner[...].T.astype(BF16)
    r.turned[1] = r.g_outer[...].T.astype(BF16)
    for k in range(2):
        put_blocks(z, r.place[0], r.turned.at[k], z.units, r.here, r.away, k * z.units)
    r.token[...] = jnp.zeros_like(r.token)


def token_back_kernel(z, l, r):
    for ref in (r.vec, r.g_project, r.g_mix):
        ref[...] = jnp.zeros_like(ref)
    even, odd = tile(parity(z, 0), z.run_back), tile(parity(z, 1), z.run_back)

    def body(rows, at):
        token = (r.half_grad[rows, :] * r.mask[rows, :]).astype(BF16)
        r.vec[0] += rows8(token.astype(F32))
        r.g_project[...] += dot(r.mixed[rows, :], token, (0, 0))
        mixed_grad = dot(token, r.project_weight[l], (1, 1))
        r.vec[1] += rows8(mixed_grad)
        both = jnp.concatenate([(mixed_grad * even).astype(BF16), (mixed_grad * odd).astype(BF16)], axis=1)
        r.mixed_grad[rows, :] = both
        r.g_mix[...] += dot(both, r.cat[rows, :], (0, 0))

    over(z, body, z.run_back)
    counts = counts_of(z, r)
    zeros = jnp.zeros((GROUP - z.I, z.C), F32)
    summed = split(z, r.vec[1])
    share = [r.share[j] for j in range(3)]
    mix, dp = [], []
    for j in range(3):
        weight = r.mix_weight[l, j].astype(F32)
        rows = []
        found = 0.0
        for i in range(z.I):
            block = r.g_mix[i * z.C : (i + 1) * z.C, j * z.C : (j + 1) * z.C].T
            rows.append(total(weight * block))
            found = found + block * share[j][i : i + 1]
            scaled = weight * share[j][i : i + 1]
            r.scaled[j * z.C : (j + 1) * z.C, i * z.C : (i + 1) * z.C] = scaled.astype(BF16)
        mix.append(found)
        dp.append(jnp.concatenate(rows + [zeros], axis=0))
    for j in range(2):
        dp[j] += summed * r.mix_bias[l, j : j + 1]
    even = dp[0] * share[0] + dp[1] * share[1] + dp[2] * share[2]
    dz = jnp.concatenate([share[j] * (dp[j] - even) for j in range(3)], axis=1)
    act, slope, pooled = r.act[...], r.slope[...], r.pooled[...]
    expand = fine(fine(act, dz, (0, 0)), r.perm[...], (1, 1))
    expand_bias = total(fine(dz, r.perm[...], (1, 1)))
    dact = fine(dz, r.ewp[l], (1, 1)) * slope
    squeeze = fine(dact, pooled, (0, 0))
    dpool = fine(dact, r.squeeze_weight[l])
    push = dpool / counts
    for j in range(3):
        mix[j] += fine(r.pool[j], push, (0, 0))
        r.push[j] = weave(z, fine(push, r.mix_weight[l, j], (1, 1)))
    for j in range(3):
        r.rows[j * z.C : (j + 1) * z.C, :] = mix[j].astype(BF16)
    r.rows[z.at_project : z.at_expand, :] = r.g_project[...].astype(BF16)
    for j in range(3):
        at = z.at_expand + j * z.R
        r.rows[at : at + z.R, :] = expand[:, j * z.C : (j + 1) * z.C].astype(BF16)
    r.rows[z.at_squeeze : z.at_small, :] = squeeze.astype(BF16)
    small = [total(share[j] * summed + dpool) for j in range(2)]
    small += [total(r.vec[0]), r.feed_small[: 3 + z.H // z.C, :]]
    small += [expand_bias[:, j * z.C : (j + 1) * z.C] for j in range(3)]
    small += [jnp.concatenate([total(dact), jnp.zeros((1, z.C - z.R), F32)], axis=1)]
    used = sum(row.shape[0] for row in small)
    small += [jnp.zeros((z.parts * z.shared - z.at_small - used, z.C), F32)]
    r.rows[z.at_small :, :] = jnp.concatenate(small, axis=0).astype(BF16)
    put_blocks(z, r.place[0], r.rows, z.shared, r.here, r.away)
    r.token[...] = jnp.zeros_like(r.token)


def mix_back_kernel(z, l, last, r):
    for ref in (r.back_h, r.back_w):
        clear_edges(z, ref)
    gain = r.norm_gain[l, 0:1]
    size = z.run_mix
    push = [tile(r.push[j], size) for j in range(3)]

    def spread(rows, at):
        mask = r.mask[rows, :]
        parts = dot(r.mixed_grad[rows, :], r.scaled[...], (1, 1))
        for j, ref in enumerate((r.back_h, r.back_w, r.back_c)):
            ref[z.base + at : z.base + at + size, :] = parts[:, j * z.C : (j + 1) * z.C] + mask * push[j]

    over(z, spread, size)
    r.vec[...] = jnp.zeros_like(r.vec)

    def body(rows, at):
        start = z.base + at
        kind = kinds(z, size)
        high = jnp.where(kind == 2, near(r.back_h, start, z.W, size), near(r.back_h, start, -z.W, size))
        wide = jnp.where(kind == 2, near(r.back_w, start, z.I, size), near(r.back_w, start, -z.I, size))
        high = jnp.where(kind == 0, near(r.back_h, start, 0, size), high)
        wide = jnp.where(kind == 0, near(r.back_w, start, 0, size), wide * r.back[rows, :].astype(F32))
        grad = high + wide + near(r.back_c, start, 0, size)
        unit = r.unit1[rows, :].astype(F32)
        r.vec[0] += rows8(grad * unit)
        r.vec[1] += rows8(grad)
        grad = r.half_grad[rows, :] + norm_back(grad, unit, r.rstd1[rows, :].astype(F32), gain)
        if last:
            real = min(rows.stop, z.N0) - at
            r.state_grad[at : at + real, :] = (grad * r.mask[rows, :])[:real]
        else:
            r.state_grad[rows, :] = grad

    over(z, body, size)
    stray = r.back_h[z.base + z.N0 - z.W : z.base + z.N0, :]
    r.vec[1] -= rows8(jnp.where(kinds(z, z.W) == 1, stray, 0.0))
    r.first_norm[...] = jnp.concatenate([total(r.vec[0]), total(r.vec[1])], axis=0)
    r.token[...] = jnp.zeros_like(r.token)


def final_outputs(z):
    return dict(
        mix_weight=arr(z.L, 3, z.C, z.C), mix_bias=arr(z.L, 2, z.C), squeeze_weight=arr(z.L, z.R, z.C),
        squeeze_bias=arr(z.L, z.R), expand_weight=arr(z.L, z.R, 3 * z.C), expand_bias=arr(z.L, 3 * z.C),
        project_weight=arr(z.L, z.C, z.C), project_bias=arr(z.L, z.C), norm_gain=arr(z.L, 2, z.C),
        norm_bias=arr(z.L, 2, z.C), inner_weight=arr(z.L, z.units, z.C), inner_bias=arr(z.L, z.units),
        outer_weight=arr(z.L, z.units, z.C), outer_bias=arr(z.L, z.C), merge_weight=arr(z.O, 9 * z.C),
        merge_bias=arr(1, z.O),
    )


def last_kernel(z, r):
    me = r.place[0]
    half = z.parts // 2
    size = z.L * z.shared
    for at in range(z.parts):
        k = at % half
        have, merge = (r.have, r.merge_have) if at < half else (r.got, r.merge_got)
        rows = pl.ds(pl.multiple_of((me ^ z.found[0][at]) * z.shared, 16), z.shared)
        for l in range(z.L):
            r.rows[l, rows, :] = have[k * size + l * z.shared : k * size + (l + 1) * z.shared, :]
        rows = pl.ds(pl.multiple_of((me ^ z.found[1][at]) * z.merge, 16), z.merge)
        r.merge_rows[rows, :] = merge[k]
    norms = r.have[half * size :, :].astype(F32) + r.got[half * size :, :].astype(F32)
    for l in range(z.L):
        rows = r.rows.at[l]

        def get(at, count):
            return rows[at : at + count, :].astype(F32)

        for j in range(3):
            r.mix_weight[l, j] = get(j * z.C, z.C)
            r.expand_weight[l, :, j * z.C : (j + 1) * z.C] = get(z.at_expand + j * z.R, z.R)
        r.project_weight[l] = get(z.at_project, z.C)
        r.squeeze_weight[l] = get(z.at_squeeze, z.R)
        small = get(z.at_small, 16)
        r.mix_bias[l] = small[0:2]
        r.project_bias[l : l + 1] = small[2:3]
        r.outer_bias[l : l + 1] = small[3:4]
        r.norm_gain[l] = jnp.concatenate([norms[2 * l : 2 * l + 1], small[4:5]], axis=0)
        r.norm_bias[l] = jnp.concatenate([norms[2 * l + 1 : 2 * l + 2], small[5:6]], axis=0)
        at = 6
        inner = jnp.zeros((1, z.units), F32)
        for k in range(z.H // z.C):
            for c in range(0, z.C, z.units):
                mine = jnp.where(me == (k * z.C + c) // z.units, 1.0, 0.0)
                inner = inner + small[at : at + 1, c : c + z.units] * mine
            at += 1
        r.inner_bias[l : l + 1] = inner
        for j in range(3):
            r.expand_bias[l : l + 1, j * z.C : (j + 1) * z.C] = small[at : at + 1]
            at += 1
        r.squeeze_bias[l : l + 1] = small[at : at + 1, : z.R]
        feed = r.feed_rows[2 * l * z.units : 2 * (l + 1) * z.units, :].astype(F32)
        r.inner_weight[l] = feed[: z.units]
        r.outer_weight[l] = feed[z.units :]
    for k in range(9):
        r.merge_weight[:, k * z.C : (k + 1) * z.C] = r.merge_rows[k * z.O : (k + 1) * z.O, :].astype(F32)
    small = r.merge_rows[9 * z.O : 9 * z.O + 16, :].astype(F32)
    r.merge_bias[:, : z.C] = small[0:1]
    r.merge_bias[:, z.C : 2 * z.C] = small[1:2]
    r.merge_bias[:, 2 * z.C :] = small[2:3, : z.O - 2 * z.C]


def pack_kernel(z, r):
    u = z.units
    copies = [pltpu.make_async_copy(r.inner_bias, r.bias, r.sem.at[2 * z.L])]
    for l in range(z.L):
        for k, ref in enumerate((r.inner_weight, r.outer_weight)):
            at = (2 * l + k) * u
            copies.append(pltpu.make_async_copy(ref.at[l], r.block.at[at : at + u], r.sem.at[2 * l + k]))
    for copy in copies:
        copy.start()
    for copy in copies:
        copy.wait()
    bias = r.bias[...].astype(F32)
    if u < z.C:
        bias = jnp.concatenate([bias, jnp.zeros((z.L, z.C - u), F32)], axis=1)
    bias = jnp.concatenate([bias, jnp.zeros((16 - z.L, z.C), F32)], axis=0)
    r.block[2 * z.L * u :, :] = bias.astype(BF16)


def swap(x, axis, n, bit):
    return lax.ppermute(x, axis, [(a, a ^ bit) for a in range(n)])


def bits_of(n):
    return [1 << k for k in range(n.bit_length() - 1)]


def add(here, got, token):
    out = here.astype(F32) + got.astype(F32)
    if token is not None:
        out = out + token[0]
    return out.astype(BF16)


def take(tokens):
    return tokens.pop(0) if tokens else None


class Chain:
    def __init__(self, parts, hid):
        self.here = jnp.concatenate([part["here"] for part in parts], axis=1)
        self.away = jnp.concatenate([part["away"] for part in parts], axis=1)
        self.left = [("hid", hid, bit) for bit in exchange_order(hid)]

    def step(self, token=None):
        axis, n, bit = self.left.pop(0)
        x = add(self.here, swap(self.away, axis, n, bit), token)
        if axis == "img":
            self.here = self.away = x
            return
        half = x.shape[0] // 2
        self.here, self.away = (x[:half], x[half:]) if half else (x[0], None)

    def halve(self, token):
        while self.left:
            self.step(token)
        return self.here

    def widen(self, rows, img):
        self.here = self.away = rows
        self.left = [("img", img, bit) for bit in bits_of(img)]


def per_device(
    img, hid, images, sizes, cotangent, mix_weight, mix_bias, squeeze_weight, squeeze_bias, expand_weight, expand_bias,
    project_weight, project_bias, norm_gain, norm_bias, inner_weight, inner_bias, outer_weight, outer_bias,
    merge_weight, merge_bias,
):
    z = Sizes(
        images.shape[0], images.shape[1], images.shape[3], inner_weight.shape[2] * hid, squeeze_weight.shape[2],
        merge_weight.shape[1], mix_weight.shape[0], hid,
    )
    place = lax.axis_index("hid").reshape(1)
    flat = images.transpose(1, 2, 0, 3).reshape(z.N0, z.C)
    merge_t = merge_weight.T
    squeeze_t = squeeze_weight.transpose(0, 2, 1)
    far = [pltpu.with_memory_space_constraint(v, pltpu.HBM) for v in (inner_weight.transpose(0, 2, 1), outer_weight, inner_bias)]
    block = call(
        partial(pack_kernel, z),
        dict(place=place, inner_weight=far[0], outer_weight=far[1], inner_bias=far[2]),
        dict(block=kept(2 * z.L * z.units + 16, z.C, dtype=BF16)),
        dict(bias=kept(z.L, z.units, dtype=BF16), sem=pltpu.SemaphoreType.DMA((2 * z.L + 1,))),
        2, 1, dict(place=0), far=dict(inner_weight=0, outer_weight=0, inner_bias=0),
    )
    block = block["block"]
    smem = dict(sizes=0, place=0)
    small = dict(
        mix_weight=mix_weight, mix_bias=mix_bias, squeeze_weight=squeeze_t, squeeze_bias=squeeze_bias,
        project_weight=project_weight, project_bias=project_bias, norm_gain=norm_gain, norm_bias=norm_bias,
    )
    token = dict(token=arr(1, z.C))
    a = call(
        partial(front_kernel, z),
        dict(sizes=sizes, place=place, cotangent=cotangent, merge_weight=merge_t),
        dict(
            mask=kept(z.N, z.C), edge=kept(z.N, z.C, dtype=BF16), back=kept(z.N, z.C, dtype=BF16), cot=kept(z.I * z.M, z.O, dtype=BF16),
            grad=kept(z.tall, z.C), merge_bias_sums=kept(8, z.O), **token,
        ),
        dict(pgrad=kept(z.M + 8, 9 * z.C)),
        4, 3, smem,
    )
    order = bits_of(hid)[1:] + [1]

    def widen(have, bit, token):
        got = swap(have, "hid", hid, bit)
        return jnp.concatenate([have, got if token is None else got + token.astype(BF16)], axis=0)

    z.gathered = [0]
    for bit in order:
        z.gathered = z.gathered + [e ^ bit for e in z.gathered]
    have = widen(block[None], order[0], a["token"])
    b = call(
        partial(first_kernel, z),
        dict(
            images=flat, sizes=sizes, mask=a["mask"], edge=a["edge"], expand_weight=expand_weight, expand_bias=expand_bias,
            **small,
        ),
        dict(
            state=kept(z.N, z.C), perm=kept(3 * z.C, 3 * z.C, dtype=BF16), ewp=kept(z.L, z.R, 3 * z.C),
            ebp=kept(z.L, 3 * z.C), **saved_early(z), **token,
        ),
        dict(normed=kept(z.long, z.C), sums=kept(3, 8, z.C)),
        5, 5, smem, [have],
    )
    for bit in order[1:]:
        have = widen(have, bit, b["token"] if bit == order[1] else None)
    late = saved_late(z)
    c = call(
        partial(second_kernel, z),
        dict(
            sizes=sizes, mask=a["mask"], edge=a["edge"], state_in=b["state"], normed2_0=b["normed2"], gathered=have, place=place,
            ewp=b["ewp"], ebp=b["ebp"], outer_bias=outer_bias, cot=a["cot"], merge_bias_sums=a["merge_bias_sums"], **small,
        ),
        dict(
            patch=kept(z.I * z.M, 9 * z.C, dtype=BF16),
            merge_here=kept(z.parts // 2, z.merge, z.C, dtype=BF16), merge_away=kept(z.parts // 2, z.merge, z.C, dtype=BF16),
            inner=kept(z.L, z.H, z.C, dtype=BF16), outer=kept(z.L, z.H, z.C, dtype=BF16),
            act_rows_0=late["act_rows"], slope_rows_0=late["slope_rows"], **saved_early(z), **late,
        ),
        dict(
            state=kept(z.N, z.C), normed=kept(z.tall, z.C), sums=kept(3, 8, z.C), inner_bias=kept(z.L, z.H), bias_rows=kept(z.parts, 16, z.C),
            merge_rows=kept(z.parts * z.merge, z.C, dtype=BF16),
        ),
        11, 16, smem,
    )
    first = dict(b, act_rows=c["act_rows_0"], slope_rows=c["slope_rows_0"])

    def some(s, **names):
        return {name: s[name] for name in names}

    grad = a["grad"]
    norms, chain = [None] * z.L, None
    merge = Chain([dict(here=c["merge_here"], away=c["merge_away"])], hid)
    for l in reversed(range(z.L)):
        s = c if l else first
        d = call(
            partial(feed_back_kernel, z, l),
            dict(
                place=place, mask=a["mask"], grad=grad, inner=c["inner"], outer=c["outer"], norm_gain=norm_gain,
                **some(s, act_rows=0, slope_rows=0, normed2=0, unit2=0, rstd2=0),
            ),
            dict(
                half_grad=kept(z.N, z.C), feed_small=arr(8, z.C), here=kept(z.parts // 2, 2 * z.units, z.C, dtype=BF16),
                away=kept(z.parts // 2, 2 * z.units, z.C, dtype=BF16), **token,
            ),
            dict(
                vec=kept(3, 8, z.C), inner_sums=kept(8, z.H), g_outer=kept(z.C, z.H), g_inner=kept(z.C, z.H),
                turned=kept(2, z.H, z.C, dtype=BF16),
            ),
            6, 2, smem, [merge.here] + ([chain.here] if chain else []),
        )
        (chain or merge).step(d["token"])
        t = call(
            partial(token_back_kernel, z, l),
            dict(
                sizes=sizes, place=place, mask=a["mask"], half_grad=d["half_grad"], feed_small=d["feed_small"],
                perm=b["perm"], ewp=b["ewp"], **some(s, mixed=0, cat=0, share=0, pool=0, pooled=0, act=0, slope=0), **small,
            ),
            dict(
                mixed_grad=kept(z.N, z.I * z.C, dtype=BF16), scaled=kept(3 * z.C, z.I * z.C, dtype=BF16),
                push=kept(3, 8, z.C), here=kept(z.parts // 2, z.shared, z.C, dtype=BF16),
                away=kept(z.parts // 2, z.shared, z.C, dtype=BF16), **token,
            ),
            dict(
                vec=kept(2, 8, z.C), g_project=kept(z.C, z.C), g_mix=kept(z.I * z.C, 3 * z.C),
                rows=kept(z.parts * z.shared, z.C, dtype=BF16),
            ),
            4, 1, smem, [(chain or merge).here],
        )
        own = Chain([d, t], hid)
        if chain:
            rows = jnp.concatenate([chain.halve(t["token"]), merge.halve(t["token"])], axis=0)
            chain.widen(rows, img)
        held = [own.here] + ([chain.here] if chain else [])
        e = call(
            partial(mix_back_kernel, z, l, l == 0),
            dict(
                mask=a["mask"], back=a["back"], norm_gain=norm_gain, half_grad=d["half_grad"],
                **some(t, mixed_grad=0, scaled=0, push=0), **some(s, unit1=0, rstd1=0),
            ),
            dict(state_grad=kept(z.N, z.C) if l else arr(z.N0, z.C), first_norm=arr(2, z.C), **token),
            dict(back_h=kept(z.long, z.C), back_w=kept(z.long, z.C), back_c=kept(z.long, z.C), vec=kept(2, 8, z.C)),
            5, 0.05, (), held,
        )
        own.step(e["token"])
        (chain or merge).step(e["token"])
        chain, last = chain or own, own
        grad, norms[l] = e["state_grad"], e["first_norm"]
    images_grad = grad.reshape(z.side, z.side, z.I, z.C).transpose(2, 0, 1, 3)

    f = call(
        partial(features_kernel, z),
        dict(patch=c["patch"], merge_weight=merge_t, merge_bias=merge_bias.reshape(1, -1)),
        dict(features=arr(z.I, z.half, z.half * z.O, dtype=BF16), **token), dict(merged=kept(z.I * z.M, z.O)), 6, 2, (), [last.here],
    )
    norm_rows = jnp.pad(jnp.concatenate(norms, axis=0), ((0, 16 - 2 * z.L), (0, 0))).astype(BF16)
    last.widen(jnp.concatenate([last.halve(None), norm_rows], axis=0), img)
    shown = f["token"]
    while chain.left or last.left:
        for each in (chain, last):
            if each.left:
                each.step(shown if each is last else None)
        shown = None
    feed, cut = 2 * z.units, 2 * z.units + z.shared
    feed_rows = jnp.concatenate([last.here[:feed], chain.here[:feed]], axis=0)
    have = jnp.concatenate([last.here[feed:cut], chain.here[feed:cut]], axis=0)
    norm_rows, merge = last.here[cut:], chain.here[None, cut:]
    bits = bits_of(hid)
    orders = bits[::-1], bits[1:] + bits[:1]
    z.found = [[0], [0]]
    for step, (bit, merge_bit) in enumerate(zip(*orders)):
        sent = jnp.concatenate([have, norm_rows], axis=0)
        got, merge_got = swap(sent, "hid", hid, bit), swap(merge, "hid", hid, merge_bit)
        z.found = [found + [e ^ b for e in found] for found, b in zip(z.found, (bit, merge_bit))]
        if step < len(bits) - 1:
            have = jnp.concatenate([have, got[:-16]], axis=0)
            norm_rows = add(norm_rows, got[-16:], None)
            merge = jnp.concatenate([merge, merge_got], axis=0)
    g = call(
        partial(last_kernel, z),
        dict(place=place, have=sent, got=got, merge_have=merge, merge_got=merge_got, feed_rows=feed_rows),
        final_outputs(z),
        dict(rows=kept(z.L, z.parts * z.shared, z.C, dtype=BF16), merge_rows=kept(z.parts * z.merge, z.C, dtype=BF16)),
        5, 2, smem,
    )
    return (
        f["features"], images_grad, g["mix_weight"], g["mix_bias"], g["squeeze_weight"].transpose(0, 2, 1),
        g["squeeze_bias"], g["expand_weight"], g["expand_bias"], g["project_weight"], g["project_bias"], g["norm_gain"],
        g["norm_bias"], g["inner_weight"].transpose(0, 2, 1), g["inner_bias"], g["outer_weight"], g["outer_bias"],
        g["merge_weight"].T, g["merge_bias"].reshape(-1),
    )


def solution(mesh):
    maps = ("img", "hid")
    in_specs = (
        P(maps, None, None, None), P(maps, None), P(maps, None, None), P(), P(), P(), P(), P(), P(), P(), P(), P(), P(),
        P(None, None, "hid"), P(None, "hid"), P(None, "hid", None), P(), P(), P(),
    )
    out_specs = (
        P(maps, None, None), P(maps, None, None, None), P(), P(), P(), P(), P(), P(), P(), P(), P(), P(),
        P(None, None, "hid"), P(None, "hid"), P(None, "hid", None), P(), P(), P(),
    )
    return jax.shard_map(
        partial(per_device, mesh.shape["img"], mesh.shape["hid"]),
        mesh=mesh, in_specs=in_specs, out_specs=out_specs, check_vma=False,
    )
```

```python
from functools import partial

import jax
import jax.numpy as jnp
from jax import lax
from jax.experimental import pallas as pl
from jax.experimental.pallas import tpu as pltpu
from jax.sharding import PartitionSpec as P

F32 = jnp.float32
BF16 = jnp.bfloat16
GROUP = 8
MIB = 2**20


def dot(a, b, dims=(1, 0)):
    return lax.dot_general(a, b, (((dims[0],), (dims[1],)), ((), ())), preferred_element_type=F32)


def halves(v):
    high = v.astype(BF16)
    return high, (v - high.astype(F32)).astype(BF16)


def fine(a, b, dims=(1, 0)):
    high, low = halves(a)
    if dims == (0, 0):
        b_high, b_low = halves(b)
        return dot(jnp.concatenate([high, low, high], axis=0), jnp.concatenate([b_high, b_high, b_low], axis=0), dims)
    rows = a.shape[0]
    both = jnp.concatenate([high, low], axis=0)
    if b.dtype == BF16:
        out = dot(both, b, dims)
        return out[:rows] + out[rows:]
    b_high, b_low = halves(b)
    out = dot(both, b_high, dims)
    return out[:rows] + (out[rows:] + dot(high, b_low, dims))


def rows8(v):
    return v.reshape(-1, 8, v.shape[-1]).sum(axis=0)


def total(v):
    return v.sum(axis=0, keepdims=True)


def tile(v, rows):
    return jnp.broadcast_to(v[None], (rows // 8, 8, v.shape[-1])).reshape(rows, v.shape[-1])


def gelu_pair(x):
    cdf = 0.5 * lax.erf(x * 0.7071067811865476) + 0.5
    bell = jnp.exp2(x * x * (-0.5 * 1.4426950408889634))
    return x * cdf, cdf + x * bell * 0.3989422804014327


def norm_parts(v):
    centred = v - jnp.mean(v, axis=-1, keepdims=True)
    rstd = lax.rsqrt(jnp.mean(centred * centred, axis=-1, keepdims=True) + 1e-05)
    return centred * rstd, jnp.broadcast_to(rstd, v.shape)


def norm_back(grad, unit, rstd, gain):
    scaled = grad * gain
    first = jnp.mean(scaled, axis=-1, keepdims=True)
    second = jnp.mean(scaled * unit, axis=-1, keepdims=True)
    return rstd * (scaled - first - unit * second)


class Sizes:
    def __init__(self, images, side, channels, hidden, red, out, layers, parts):
        self.I, self.side, self.C, self.H, self.R, self.O, self.L = images, side, channels, hidden, red, out, layers
        self.parts, self.units = parts, hidden // parts
        self.W = side * images
        self.N0 = side * self.W
        self.N = -(-self.N0 // 384) * 384
        self.run_first = self.run_back = self.run_mix = self.N
        self.run_second = self.N // 7
        self.half = side // 2
        self.hp = -(-self.half // 8) * 8
        self.M = self.half * self.hp
        self.base = self.W
        self.tall = self.W * (2 * self.hp + 2)
        self.long = self.base + self.N + self.W
        self.at_project = 3 * channels
        self.at_expand = self.at_project + channels
        self.at_squeeze = self.at_expand + 3 * red
        self.at_small = self.at_squeeze + red
        self.shared = -(-(self.at_small + 16) // (16 * parts)) * 16
        self.merge = -(-(9 * out + 3) // (16 * parts)) * 16


class Refs:
    pass


def call(body, ins, outs, scratch, limit, micros, smem=(), after=(), far=()):
    waits = {f"after{k}": array for k, array in enumerate(after)}
    ins = dict(ins, **waits)
    vmem = pl.BlockSpec(memory_space=pltpu.VMEM)
    scalar, anywhere = pl.BlockSpec(memory_space=pltpu.SMEM), pl.BlockSpec(memory_space=pl.ANY)

    def place(name):
        return scalar if name in smem else anywhere if name in waits or name in far else vmem

    names = list(ins) + list(outs) + list(scratch)

    def kernel(*refs):
        r = Refs()
        for name, ref in zip(names, refs):
            setattr(r, name, ref)
        body(r)

    found = pl.pallas_call(
        kernel,
        out_shape=list(outs.values()),
        in_specs=[place(name) for name in ins],
        out_specs=[vmem] * len(outs),
        scratch_shapes=list(scratch.values()),
        compiler_params=pltpu.CompilerParams(vmem_limit_bytes=limit * MIB),
        cost_estimate=pl.CostEstimate(flops=int(micros * 1.15e9), bytes_accessed=0, transcendentals=0),
    )(*ins.values())
    return dict(zip(outs, found))


def arr(*shape, dtype=F32):
    return jax.ShapeDtypeStruct(shape, dtype)


def kept(*shape, dtype=F32):
    return pltpu.VMEM(shape, dtype)


def over(z, body, size):
    for at in range(0, z.N, size):
        body(slice(at, at + size), at)


def near(ref, start, off, size):
    return ref[start + off : start + off + size, :]


def parity(z, i):
    rows = lax.broadcasted_iota(jnp.int32, (8, z.C), 0)
    return jnp.where(rows % z.I == i, 1.0, 0.0)


def kinds(z, rows):
    return tile(lax.broadcasted_iota(jnp.int32, (8, z.C), 1) % 3, rows)


def weave(z, v):
    out = v[0:1] * parity(z, 0)
    for i in range(1, z.I):
        out += v[i : i + 1] * parity(z, i)
    return out


def split(z, v):
    rows = [total(v * parity(z, i)) for i in range(z.I)]
    return jnp.concatenate(rows + [jnp.zeros((GROUP - z.I, z.C), F32)], axis=0)


def front_kernel(z, r):
    rows = lax.broadcasted_iota(jnp.int32, (z.W, z.C), 0)
    lanes = lax.broadcasted_iota(jnp.int32, (z.W, z.C), 1) % 3
    image = rows % z.I
    col = rows // z.I
    high = jnp.zeros((z.W, z.C), jnp.int32)
    wide = jnp.zeros((z.W, z.C), jnp.int32)
    for i in range(z.I):
        high = jnp.where(image == i, r.sizes[i, 0], high)
        wide = jnp.where(image == i, r.sizes[i, 1], wide)
    inside = jnp.where(col < wide, 1.0, 0.0)
    first, last = col == 0, col == z.side - 1
    edge = jnp.where((first & (lanes == 2)) | (last & (lanes == 1)), 0.0, 1.0)
    back = jnp.where((last & (lanes == 2)) | (first & (lanes == 1)), 0.0, 1.0)

    def step(row, carry):
        at = pl.ds(pl.multiple_of(row * z.W, 8), z.W)
        r.mask[at, :] = jnp.where(high > row, inside, 0.0)
        return carry

    lax.fori_loop(0, z.side, step, 0)
    edge = jnp.concatenate([edge, edge], axis=0).astype(BF16)
    back = jnp.concatenate([back, back], axis=0).astype(BF16)

    def step2(row, carry):
        at = pl.ds(pl.multiple_of(row * 2 * z.W, 16), 2 * z.W)
        r.edge[at, :] = edge
        r.back[at, :] = back
        return carry

    lax.fori_loop(0, z.side // 2, step2, 0)
    pad = jnp.zeros((z.N - z.N0, z.C), F32)
    for ref in (r.mask, r.edge, r.back):
        ref[z.N0 :, :] = pad.astype(ref.dtype)
    pad = jnp.zeros((z.hp - z.half, z.O), F32)
    r.pgrad[z.M :, :] = jnp.zeros((8, 9 * z.C), F32)
    sums = jnp.zeros((8, z.O), F32)
    for i in range(z.I):
        for pair in range(z.half // 2):
            both = r.cotangent[i, :, 2 * pair * z.O : (2 * pair + 2) * z.O].astype(F32)
            both = jnp.concatenate([both[:, : z.O], pad, both[:, z.O :], pad], axis=0)
            at = i * z.M + 2 * pair * z.hp
            r.cot[at : at + 2 * z.hp, :] = both.astype(BF16)
            sums += rows8(both)
        step = z.M // 2
        for at in range(0, z.M, step):
            r.pgrad[at : at + step, :] = dot(r.cot[i * z.M + at : i * z.M + at + step, :], r.merge_weight[...])

        def part(dr, ds, b, down=0):
            k = 3 * dr + ds
            return r.pgrad[pl.ds(b * z.hp + down, z.hp), k * z.C : (k + 1) * z.C]

        for b in range(z.half):
            planes = [
                part(1, 1, b),
                part(2, 1, b) + part(0, 1, b, 1),
                part(1, 2, b),
                part(2, 2, b) + part(0, 2, b, 1),
            ]
            if b < z.half - 1:
                planes[2] += part(1, 0, b + 1)
                planes[3] += part(2, 0, b + 1) + part(0, 0, b + 1, 1)
            for plane, (down, right) in zip(planes, ((0, 0), (1, 0), (0, 1), (1, 1))):
                start = down * z.W + (2 * b + right) * z.I + i
                r.grad[pl.ds(start, z.hp, stride=2 * z.W), :] = plane
    r.merge_bias_sums[...] = sums
    r.token[...] = jnp.zeros_like(r.token)


def shift_phase(z, r, cat, size):
    r.sums[...] = jnp.zeros_like(r.sums)

    def body(rows, at):
        start = z.base + at
        kind = kinds(z, size)
        mid = near(r.normed, start, 0, size)
        high = jnp.where(kind == 2, near(r.normed, start, -z.W, size), near(r.normed, start, z.W, size))
        wide = jnp.where(kind == 2, near(r.normed, start, -z.I, size), near(r.normed, start, z.I, size))
        high = jnp.where(kind == 0, mid, high)
        wide = jnp.where(kind == 0, mid, wide * r.edge[rows, :].astype(F32))
        mask = r.mask[rows, :]
        for j, piece in enumerate((high, wide, mid)):
            cat[rows, j * z.C : (j + 1) * z.C] = piece.astype(BF16)
            r.sums[j] += rows8(piece * mask)

    over(z, body, size)


def counts_of(z, r):
    rows = []
    for i in range(GROUP):
        count = (r.sizes[i, 0] * r.sizes[i, 1]).astype(F32) if i < z.I else 1.0
        rows.append(jnp.full((1, z.C), 1.0, F32) * count)
    return jnp.concatenate(rows, axis=0)


def weigh_phase(z, r, l, o):
    pooled = r.mix_bias[l, 0:1] + r.mix_bias[l, 1:2]
    counts = counts_of(z, r)
    for j in range(3):
        pool = split(z, r.sums[j])
        o.pool[j] = pool
        pooled = pooled + fine(pool, r.mix_weight[l, j]) / counts
    o.pooled[...] = pooled
    act, slope = gelu_pair(fine(pooled, r.squeeze_weight[l], (1, 1)) + r.squeeze_bias[l : l + 1])
    o.act[...] = act
    o.slope[...] = slope
    logits = fine(act, r.ewp[l]) + r.ebp[l : l + 1]
    parts = [logits[:, j * z.C : (j + 1) * z.C] for j in range(3)]
    top = jnp.maximum(jnp.maximum(parts[0], parts[1]), parts[2])
    parts = [jnp.exp(part - top) for part in parts]
    whole = parts[0] + parts[1] + parts[2]
    for j in range(3):
        o.share[j] = parts[j] / whole


def mix_phase(z, r, l, o, size):
    share = [weave(z, o.share[j]) for j in range(3)]
    bias = tile(r.mix_bias[l, 0:1] * share[0] + r.mix_bias[l, 1:2] * share[1], size)
    share = [tile(s, size) for s in share]
    gain, shift = r.norm_gain[l, 1:2], r.norm_bias[l, 1:2]

    def body(rows, at):
        mixed = bias
        for j in range(3):
            mixed = mixed + dot(o.cat[rows, j * z.C : (j + 1) * z.C], r.mix_weight[l, j]) * share[j]
        mixed = mixed.astype(BF16)
        o.mixed[rows, :] = mixed
        token = dot(mixed, r.project_weight[l]) + r.project_bias[l : l + 1]
        halfway = r.state[rows, :] + r.mask[rows, :] * token
        unit, rstd = norm_parts(halfway)
        o.unit2[rows, :] = unit.astype(BF16)
        o.rstd2[rows, :] = rstd.astype(BF16)
        o.normed2[rows, :] = (unit * gain + shift).astype(BF16)
        r.state[rows, :] = halfway

    over(z, body, size)


def norm_store(z, r, l, o, rows, at, state):
    unit, rstd = norm_parts(state)
    o.unit1[rows, :] = unit.astype(BF16)
    o.rstd1[rows, :] = rstd.astype(BF16)
    r.normed[z.base + at : z.base + at + rows.stop - rows.start, :] = unit * r.norm_gain[l, 0:1] + r.norm_bias[l, 0:1]


def clear_edges(z, ref):
    ref[: z.base, :] = jnp.zeros((z.base, z.C), F32)
    ref[z.base + z.N0 :, :] = jnp.zeros((ref.shape[0] - z.base - z.N0, z.C), F32)


def feed_phase(z, r, l, o, source, after):
    def body(rows, at):
        pre = dot(o.normed2[rows, :], r.inner[l], (1, 1)) + r.inner_bias[l : l + 1]
        act, slope = gelu_pair(pre)
        act = act.astype(BF16)
        o.act_rows[rows, :] = act
        o.slope_rows[rows, :] = slope.astype(BF16)
        out = dot(act, r.outer[l]) + r.outer_bias[l : l + 1]
        state = source[rows, :] + r.mask[rows, :] * out
        after(rows, at, state)

    over(z, body, z.run_second)


def saved_early(z):
    return dict(
        unit1=kept(z.N, z.C, dtype=BF16), rstd1=kept(z.N, z.C, dtype=BF16), cat=kept(z.N, 3 * z.C, dtype=BF16), mixed=kept(z.N, z.C, dtype=BF16),
        unit2=kept(z.N, z.C, dtype=BF16), rstd2=kept(z.N, z.C, dtype=BF16), normed2=kept(z.N, z.C, dtype=BF16), pool=kept(3, GROUP, z.C),
        pooled=kept(GROUP, z.C), act=kept(GROUP, z.R), slope=kept(GROUP, z.R), share=kept(3, GROUP, z.C),
    )


def saved_late(z):
    return dict(act_rows=kept(z.N, z.H, dtype=BF16), slope_rows=kept(z.N, z.H, dtype=BF16))


def first_kernel(z, r):
    spots = lax.broadcasted_iota(jnp.int32, (3 * z.C, 3 * z.C), 0)
    ends = lax.broadcasted_iota(jnp.int32, (3 * z.C, 3 * z.C), 1)
    kind = jnp.where(ends >= 2 * z.C, 2, jnp.where(ends >= z.C, 1, 0))
    r.perm[...] = jnp.where(spots == 3 * (ends - kind * z.C) + kind, 1.0, 0.0).astype(BF16)
    blank = jnp.zeros((8 - z.L, 3 * z.C), F32)
    rows = [r.expand_weight[l] for l in range(z.L)] + [r.expand_bias[...], blank]
    rows = fine(jnp.concatenate(rows, axis=0), r.perm[...])
    for l in range(z.L):
        r.ewp[l] = rows[l * z.R : (l + 1) * z.R]
    r.ebp[...] = rows[z.L * z.R : z.L * z.R + z.L]

    def begin(rows, at):
        real = min(rows.stop, z.N0) - at
        state = r.images[at : at + real, :].astype(F32) * r.mask[at : at + real, :]
        if real < rows.stop - at:
            state = jnp.concatenate([state, jnp.zeros((rows.stop - at - real, z.C), F32)], axis=0)
        r.state[rows, :] = state
        norm_store(z, r, 0, r, rows, at, state)

    over(z, begin, z.run_first)
    clear_edges(z, r.normed)
    shift_phase(z, r, r.cat, z.run_first)
    weigh_phase(z, r, 0, r)
    mix_phase(z, r, 0, r, z.run_first)
    r.token[...] = jnp.zeros_like(r.token)


def exchange_order(n):
    bits = bits_of(n)
    return bits[:1] + bits[:0:-1]


def rank(n, e):
    return sum((n >> k + 1) * (e // bit % 2) for k, bit in enumerate(exchange_order(n)))


def put_blocks(z, me, rows, size, here, away, start=0):
    half = z.parts // 2
    for e in range(z.parts):
        at = rank(z.parts, e)
        block = rows[pl.ds(pl.multiple_of((me ^ e) * size, 16), size), :]
        if at < half:
            here[at, start : start + size, :] = block
        else:
            away[at - half, start : start + size, :] = block


def second_kernel(z, r):
    me = r.place[0]
    for k, e in enumerate(z.gathered):
        at = pl.multiple_of((me ^ e) * z.units, z.units)
        for l in range(z.L):
            r.inner[l, pl.ds(at, z.units), :] = r.gathered[k, 2 * l * z.units : (2 * l + 1) * z.units, :]
            r.outer[l, pl.ds(at, z.units), :] = r.gathered[k, (2 * l + 1) * z.units : (2 * l + 2) * z.units, :]
        at = 2 * z.L * z.units
        r.bias_rows[me ^ e] = r.gathered[k, at : at + 16, :].astype(F32)
    for l in range(z.L):
        r.inner_bias[l : l + 1] = jnp.concatenate([r.bias_rows[h, l : l + 1, : z.units] for h in range(z.parts)], axis=1)
    early, late = [Refs() for _ in range(z.L)], [Refs() for _ in range(z.L)]
    for l in range(z.L):
        early[l].normed2 = r.normed2_0 if l == 0 else r.normed2
        early[l].act_rows = r.act_rows_0 if l == 0 else r.act_rows
        early[l].slope_rows = r.slope_rows_0 if l == 0 else r.slope_rows

    def then_norm(rows, at, state):
        r.state[rows, :] = state
        norm_store(z, r, 1, r, rows, at, state)

    feed_phase(z, r, 0, early[0], r.state_in, then_norm)
    clear_edges(z, r.normed)
    shift_phase(z, r, r.cat, z.run_second)
    weigh_phase(z, r, 1, r)
    mix_phase(z, r, 1, r, z.run_second)

    def then_keep(rows, at, state):
        r.normed[z.base + at : z.base + at + rows.stop - rows.start, :] = state

    feed_phase(z, r, 1, early[1], r.state, then_keep)
    for i in range(z.I):
        for pair in range(z.half // 2):
            at = i * z.M + 2 * pair * z.hp
            for k in range(9):
                dr, ds = divmod(k, 3)
                two = []
                for b in (2 * pair, 2 * pair + 1):
                    col = 2 * b + ds - 1
                    if col < 0:
                        two.append(jnp.zeros((z.hp, z.C), F32))
                    else:
                        two.append(r.normed[pl.ds(dr * z.W + col * z.I + i, z.hp, stride=2 * z.W), :])
                r.patch[at : at + 2 * z.hp, k * z.C : (k + 1) * z.C] = jnp.concatenate(two, axis=0).astype(BF16)
    for k in range(9):
        grad = dot(r.cot[...], r.patch[:, k * z.C : (k + 1) * z.C], (0, 0))
        r.merge_rows[k * z.O : (k + 1) * z.O, :] = grad.astype(BF16)
    bias = total(r.merge_bias_sums[...])
    rest = z.O - 2 * z.C
    rows = [bias[:, : z.C], bias[:, z.C : 2 * z.C]]
    rows += [jnp.concatenate([bias[:, 2 * z.C :], jnp.zeros((1, z.C - rest), F32)], axis=1)]
    rows += [jnp.zeros((z.parts * z.merge - 9 * z.O - 3, z.C), F32)]
    r.merge_rows[9 * z.O :, :] = jnp.concatenate(rows, axis=0).astype(BF16)
    put_blocks(z, me, r.merge_rows, z.merge, r.merge_here, r.merge_away)


def features_kernel(z, r):
    r.merged[...] = dot(r.patch[...], r.merge_weight[...], (1, 1)) + r.merge_bias[...]
    r.token[...] = jnp.zeros_like(r.token)
    for i in range(z.I):
        for pair in range(z.half // 2):
            at = i * z.M + 2 * pair * z.hp
            wide = [r.merged[at : at + z.half, :], r.merged[at + z.hp : at + z.hp + z.half, :]]
            wide = jnp.concatenate(wide, axis=1).astype(BF16)
            r.features[i, :, 2 * pair * z.O : (2 * pair + 2) * z.O] = wide


def feed_back_kernel(z, l, r):
    gain = r.norm_gain[l, 1:2]
    for ref in (r.vec, r.inner_sums, r.g_outer, r.g_inner):
        ref[...] = jnp.zeros_like(ref)

    def body(rows, at):
        mask = r.mask[rows, :]
        grad = r.grad[rows, :]
        out = grad * mask
        r.vec[0] += rows8(out)
        out = out.astype(BF16)
        pre = dot(out, r.outer[l], (1, 1)) * r.slope_rows[rows, :].astype(F32)
        r.inner_sums[...] += rows8(pre)
        pre = pre.astype(BF16)
        r.g_outer[...] += dot(out, r.act_rows[rows, :], (0, 0))
        r.g_inner[...] += dot(r.normed2[rows, :], pre, (0, 0))
        normed_grad = dot(pre, r.inner[l])
        unit = r.unit2[rows, :].astype(F32)
        r.vec[1] += rows8(normed_grad * unit)
        r.vec[2] += rows8(normed_grad)
        r.half_grad[rows, :] = grad + norm_back(normed_grad, unit, r.rstd2[rows, :].astype(F32), gain)

    over(z, body, z.run_back)
    inner = total(r.inner_sums[...])
    small = [total(r.vec[k]) for k in range(3)]
    small += [inner[:, k * z.C : (k + 1) * z.C] for k in range(z.H // z.C)]
    small += [jnp.zeros((1, z.C), F32)]
    r.feed_small[...] = jnp.concatenate(small, axis=0)
    r.turned[0] = r.g_inner[...].T.astype(BF16)
    r.turned[1] = r.g_outer[...].T.astype(BF16)
    for k in range(2):
        put_blocks(z, r.place[0], r.turned.at[k], z.units, r.here, r.away, k * z.units)
    r.token[...] = jnp.zeros_like(r.token)


def token_back_kernel(z, l, r):
    for ref in (r.vec, r.g_project, r.g_mix):
        ref[...] = jnp.zeros_like(ref)
    even, odd = tile(parity(z, 0), z.run_back), tile(parity(z, 1), z.run_back)

    def body(rows, at):
        token = r.half_grad[rows, :] * r.mask[rows, :]
        r.vec[0] += rows8(token)
        token = token.astype(BF16)
        r.g_project[...] += dot(r.mixed[rows, :], token, (0, 0))
        mixed_grad = dot(token, r.project_weight[l], (1, 1))
        r.vec[1] += rows8(mixed_grad)
        both = jnp.concatenate([(mixed_grad * even).astype(BF16), (mixed_grad * odd).astype(BF16)], axis=1)
        r.mixed_grad[rows, :] = both
        r.g_mix[...] += dot(both, r.cat[rows, :], (0, 0))

    over(z, body, z.run_back)
    counts = counts_of(z, r)
    zeros = jnp.zeros((GROUP - z.I, z.C), F32)
    summed = split(z, r.vec[1])
    share = [r.share[j] for j in range(3)]
    mix, dp = [], []
    for j in range(3):
        weight = r.mix_weight[l, j].astype(F32)
        rows = []
        found = 0.0
        for i in range(z.I):
            block = r.g_mix[i * z.C : (i + 1) * z.C, j * z.C : (j + 1) * z.C].T
            rows.append(total(weight * block))
            found = found + block * share[j][i : i + 1]
            scaled = weight * share[j][i : i + 1]
            r.scaled[j * z.C : (j + 1) * z.C, i * z.C : (i + 1) * z.C] = scaled.astype(BF16)
        mix.append(found)
        dp.append(jnp.concatenate(rows + [zeros], axis=0))
    for j in range(2):
        dp[j] += summed * r.mix_bias[l, j : j + 1]
    even = dp[0] * share[0] + dp[1] * share[1] + dp[2] * share[2]
    dz = jnp.concatenate([share[j] * (dp[j] - even) for j in range(3)], axis=1)
    act, slope, pooled = r.act[...], r.slope[...], r.pooled[...]
    expand = fine(jnp.concatenate([fine(act, dz, (0, 0)), dz], axis=0), r.perm[...], (1, 1))
    expand, expand_bias = expand[: z.R], total(expand[z.R :])
    dact = fine(dz, r.ewp[l], (1, 1)) * slope
    squeeze = fine(dact, pooled, (0, 0))
    dpool = fine(dact, r.squeeze_weight[l])
    push = dpool / counts
    for j in range(3):
        mix[j] += fine(r.pool[j], push, (0, 0))
        r.push[j] = weave(z, fine(push, r.mix_weight[l, j], (1, 1)))
    for j in range(3):
        r.rows[j * z.C : (j + 1) * z.C, :] = mix[j].astype(BF16)
    r.rows[z.at_project : z.at_expand, :] = r.g_project[...].astype(BF16)
    for j in range(3):
        at = z.at_expand + j * z.R
        r.rows[at : at + z.R, :] = expand[:, j * z.C : (j + 1) * z.C].astype(BF16)
    r.rows[z.at_squeeze : z.at_small, :] = squeeze.astype(BF16)
    small = [total(share[j] * summed + dpool) for j in range(2)]
    small += [total(r.vec[0]), r.feed_small[: 3 + z.H // z.C, :]]
    small += [expand_bias[:, j * z.C : (j + 1) * z.C] for j in range(3)]
    small += [jnp.concatenate([total(dact), jnp.zeros((1, z.C - z.R), F32)], axis=1)]
    used = sum(row.shape[0] for row in small)
    small += [jnp.zeros((z.parts * z.shared - z.at_small - used, z.C), F32)]
    r.rows[z.at_small :, :] = jnp.concatenate(small, axis=0).astype(BF16)
    put_blocks(z, r.place[0], r.rows, z.shared, r.here, r.away)
    r.token[...] = jnp.zeros_like(r.token)


def mix_back_kernel(z, l, last, r):
    for ref in (r.back_h, r.back_w):
        clear_edges(z, ref)
    gain = r.norm_gain[l, 0:1]
    size = z.run_mix
    push = [tile(r.push[j], size) for j in range(3)]

    def spread(rows, at):
        mask = r.mask[rows, :]
        parts = dot(r.mixed_grad[rows, :], r.scaled[...], (1, 1))
        for j, ref in enumerate((r.back_h, r.back_w, r.back_c)):
            ref[z.base + at : z.base + at + size, :] = parts[:, j * z.C : (j + 1) * z.C] + mask * push[j]

    over(z, spread, size)
    r.vec[...] = jnp.zeros_like(r.vec)

    def body(rows, at):
        start = z.base + at
        kind = kinds(z, size)
        high = jnp.where(kind == 2, near(r.back_h, start, z.W, size), near(r.back_h, start, -z.W, size))
        wide = jnp.where(kind == 2, near(r.back_w, start, z.I, size), near(r.back_w, start, -z.I, size))
        high = jnp.where(kind == 0, near(r.back_h, start, 0, size), high)
        wide = jnp.where(kind == 0, near(r.back_w, start, 0, size), wide * r.back[rows, :].astype(F32))
        grad = high + wide + near(r.back_c, start, 0, size)
        unit = r.unit1[rows, :].astype(F32)
        r.vec[0] += rows8(grad * unit)
        r.vec[1] += rows8(grad)
        grad = r.half_grad[rows, :] + norm_back(grad, unit, r.rstd1[rows, :].astype(F32), gain)
        if last:
            real = min(rows.stop, z.N0) - at
            r.state_grad[at : at + real, :] = (grad * r.mask[rows, :])[:real]
        else:
            r.state_grad[rows, :] = grad

    over(z, body, size)
    stray = r.back_h[z.base + z.N0 - z.W : z.base + z.N0, :]
    r.vec[1] -= rows8(jnp.where(kinds(z, z.W) == 1, stray, 0.0))
    r.first_norm[...] = jnp.concatenate([total(r.vec[0]), total(r.vec[1])], axis=0)
    r.token[...] = jnp.zeros_like(r.token)


def final_outputs(z):
    return dict(
        mix_weight=arr(z.L, 3, z.C, z.C), mix_bias=arr(z.L, 2, z.C), squeeze_weight=arr(z.L, z.R, z.C),
        squeeze_bias=arr(z.L, z.R), expand_weight=arr(z.L, z.R, 3 * z.C), expand_bias=arr(z.L, 3 * z.C),
        project_weight=arr(z.L, z.C, z.C), project_bias=arr(z.L, z.C), norm_gain=arr(z.L, 2, z.C),
        norm_bias=arr(z.L, 2, z.C), inner_weight=arr(z.L, z.units, z.C), inner_bias=arr(z.L, z.units),
        outer_weight=arr(z.L, z.units, z.C), outer_bias=arr(z.L, z.C), merge_weight=arr(z.O, 9 * z.C),
        merge_bias=arr(z.O),
    )


def last_kernel(z, r):
    me = r.place[0]
    half = z.parts // 2
    size = z.shared
    for at in range(z.parts):
        k = at % half
        have, merge = (r.have, r.merge_have) if at < half else (r.got, r.merge_got)
        rows = pl.ds(pl.multiple_of((me ^ z.found[at]) * z.shared, 16), z.shared)
        r.rows[0, rows, :] = have[k * size : (k + 1) * size, :]
        r.rows[1, rows, :] = merge[k, :size, :]
        rows = pl.ds(pl.multiple_of((me ^ z.found[at]) * z.merge, 16), z.merge)
        r.merge_rows[rows, :] = merge[k, size:, :]
    norms = r.have[half * size :, :].astype(F32) + r.got[half * size :, :].astype(F32)
    for l in range(z.L):
        rows = r.rows.at[l]

        def get(at, count):
            return rows[at : at + count, :].astype(F32)

        for j in range(3):
            r.mix_weight[l, j] = get(j * z.C, z.C)
            r.expand_weight[l, :, j * z.C : (j + 1) * z.C] = get(z.at_expand + j * z.R, z.R)
        r.project_weight[l] = get(z.at_project, z.C)
        r.squeeze_weight[l] = get(z.at_squeeze, z.R)
        small = get(z.at_small, 16)
        r.mix_bias[l] = small[0:2]
        r.project_bias[l : l + 1] = small[2:3]
        r.outer_bias[l : l + 1] = small[3:4]
        r.norm_gain[l] = jnp.concatenate([norms[2 * l : 2 * l + 1], small[4:5]], axis=0)
        r.norm_bias[l] = jnp.concatenate([norms[2 * l + 1 : 2 * l + 2], small[5:6]], axis=0)
        at = 6
        inner = jnp.zeros((1, z.units), F32)
        for k in range(z.H // z.C):
            for c in range(0, z.C, z.units):
                mine = jnp.where(me == (k * z.C + c) // z.units, 1.0, 0.0)
                inner = inner + small[at : at + 1, c : c + z.units] * mine
            at += 1
        r.inner_bias[l : l + 1] = inner
        for j in range(3):
            r.expand_bias[l : l + 1, j * z.C : (j + 1) * z.C] = small[at : at + 1]
            at += 1
        r.squeeze_bias[l : l + 1] = small[at : at + 1, : z.R]
        feed = r.feed_rows[2 * l * z.units : 2 * (l + 1) * z.units, :].astype(F32)
        r.inner_weight[l] = feed[: z.units]
        r.outer_weight[l] = feed[z.units :]
    for k in range(9):
        r.merge_weight[:, k * z.C : (k + 1) * z.C] = r.merge_rows[k * z.O : (k + 1) * z.O, :].astype(F32)
    small = r.merge_rows[9 * z.O : 9 * z.O + 16, :].astype(F32)
    r.merge_bias[: z.C] = small[0]
    r.merge_bias[z.C : 2 * z.C] = small[1]
    r.merge_bias[2 * z.C :] = small[2, : z.O - 2 * z.C]


def pack_kernel(z, r):
    u = z.units
    copies = [pltpu.make_async_copy(r.inner_bias, r.bias, r.sem.at[2 * z.L])]
    for l in range(z.L):
        for k, ref in enumerate((r.inner_weight, r.outer_weight)):
            at = (2 * l + k) * u
            copies.append(pltpu.make_async_copy(ref.at[l], r.block.at[at : at + u], r.sem.at[2 * l + k]))
    for copy in copies:
        copy.start()
    for copy in copies:
        copy.wait()
    bias = r.bias[...].astype(F32)
    if u < z.C:
        bias = jnp.concatenate([bias, jnp.zeros((z.L, z.C - u), F32)], axis=1)
    bias = jnp.concatenate([bias, jnp.zeros((16 - z.L, z.C), F32)], axis=0)
    r.block[2 * z.L * u :, :] = bias.astype(BF16)


def swap(x, axis, n, bit):
    return lax.ppermute(x, axis, [(a, a ^ bit) for a in range(n)])


def bits_of(n):
    return [1 << k for k in range(n.bit_length() - 1)]


def add(here, got, token):
    out = here.astype(F32) + got.astype(F32)
    if token is not None:
        out = out + token[0]
    return out.astype(BF16)


def take(tokens):
    return tokens.pop(0) if tokens else None


class Chain:
    def __init__(self, parts, hid):
        self.here = jnp.concatenate([part["here"] for part in parts], axis=1)
        self.away = jnp.concatenate([part["away"] for part in parts], axis=1)
        self.left = [("hid", hid, bit) for bit in exchange_order(hid)]

    def step(self, token=None, tie=None):
        axis, n, bit = self.left.pop(0)
        got = swap(self.away, axis, n, bit)
        if tie is not None:
            got, tie = lax.optimization_barrier((got, tie))
        x = add(self.here, got, token)
        if axis == "img":
            self.here = self.away = x
            return tie
        half = x.shape[0] // 2
        self.here, self.away = (x[:half], x[half:]) if half else (x[0], None)
        return tie

    def halve(self, token):
        while self.left:
            self.step(token)
        return self.here

    def widen(self, rows, img):
        self.here = self.away = rows
        self.left = [("img", img, bit) for bit in bits_of(img)]


def per_device(
    img, hid, images, sizes, cotangent, mix_weight, mix_bias, squeeze_weight, squeeze_bias, expand_weight, expand_bias,
    project_weight, project_bias, norm_gain, norm_bias, inner_weight, inner_bias, outer_weight, outer_bias,
    merge_weight, merge_bias,
):
    z = Sizes(
        images.shape[0], images.shape[1], images.shape[3], inner_weight.shape[2] * hid, squeeze_weight.shape[2],
        merge_weight.shape[1], mix_weight.shape[0], hid,
    )
    place = lax.axis_index("hid").reshape(1)
    flat = images.transpose(1, 2, 0, 3).reshape(z.N0, z.C)
    merge_t = merge_weight.T
    squeeze_t = squeeze_weight.transpose(0, 2, 1)
    far = [pltpu.with_memory_space_constraint(v, pltpu.HBM) for v in (inner_weight.transpose(0, 2, 1), outer_weight, inner_bias)]
    block = call(
        partial(pack_kernel, z),
        dict(place=place, inner_weight=far[0], outer_weight=far[1], inner_bias=far[2]),
        dict(block=kept(2 * z.L * z.units + 16, z.C, dtype=BF16)),
        dict(bias=kept(z.L, z.units, dtype=BF16), sem=pltpu.SemaphoreType.DMA((2 * z.L + 1,))),
        2, 1, dict(place=0), far=dict(inner_weight=0, outer_weight=0, inner_bias=0),
    )
    block = block["block"]
    smem = dict(sizes=0, place=0)
    small = dict(
        mix_weight=mix_weight, mix_bias=mix_bias, squeeze_weight=squeeze_t, squeeze_bias=squeeze_bias,
        project_weight=project_weight, project_bias=project_bias, norm_gain=norm_gain, norm_bias=norm_bias,
    )
    token = dict(token=arr(1, z.C))
    a = call(
        partial(front_kernel, z),
        dict(sizes=sizes, place=place, cotangent=cotangent, merge_weight=merge_t),
        dict(
            mask=kept(z.N, z.C), edge=kept(z.N, z.C, dtype=BF16), back=kept(z.N, z.C, dtype=BF16), cot=kept(z.I * z.M, z.O, dtype=BF16),
            grad=kept(z.tall, z.C), merge_bias_sums=kept(8, z.O), **token,
        ),
        dict(pgrad=kept(z.M + 8, 9 * z.C)),
        4, 3, smem,
    )
    order = bits_of(hid)[1:] + [1]

    def widen(have, bit, token):
        got = swap(have, "hid", hid, bit)
        return jnp.concatenate([have, got if token is None else got + token.astype(BF16)], axis=0)

    z.gathered = [0]
    for bit in order:
        z.gathered = z.gathered + [e ^ bit for e in z.gathered]
    have = widen(block[None], order[0], a["token"])
    b = call(
        partial(first_kernel, z),
        dict(
            images=flat, sizes=sizes, mask=a["mask"], edge=a["edge"], expand_weight=expand_weight, expand_bias=expand_bias,
            **small,
        ),
        dict(
            state=kept(z.N, z.C), perm=kept(3 * z.C, 3 * z.C, dtype=BF16), ewp=kept(z.L, z.R, 3 * z.C),
            ebp=kept(z.L, 3 * z.C), **saved_early(z), **token,
        ),
        dict(normed=kept(z.long, z.C), sums=kept(3, 8, z.C)),
        5, 5, smem, [have],
    )
    for bit in order[1:]:
        have = widen(have, bit, b["token"] if bit == order[1] else None)
    late = saved_late(z)
    c = call(
        partial(second_kernel, z),
        dict(
            sizes=sizes, mask=a["mask"], edge=a["edge"], state_in=b["state"], normed2_0=b["normed2"], gathered=have, place=place,
            ewp=b["ewp"], ebp=b["ebp"], outer_bias=outer_bias, cot=a["cot"], merge_bias_sums=a["merge_bias_sums"], **small,
        ),
        dict(
            patch=kept(z.I * z.M, 9 * z.C, dtype=BF16),
            merge_here=kept(z.parts // 2, z.merge, z.C, dtype=BF16), merge_away=kept(z.parts // 2, z.merge, z.C, dtype=BF16),
            inner=kept(z.L, z.H, z.C, dtype=BF16), outer=kept(z.L, z.H, z.C, dtype=BF16),
            act_rows_0=late["act_rows"], slope_rows_0=late["slope_rows"], **saved_early(z), **late,
        ),
        dict(
            state=kept(z.N, z.C), normed=kept(z.tall, z.C), sums=kept(3, 8, z.C), inner_bias=kept(z.L, z.H), bias_rows=kept(z.parts, 16, z.C),
            merge_rows=kept(z.parts * z.merge, z.C, dtype=BF16),
        ),
        11, 16, smem,
    )
    first = dict(b, act_rows=c["act_rows_0"], slope_rows=c["slope_rows_0"])

    def some(s, **names):
        return {name: s[name] for name in names}

    grad = a["grad"]
    norms, chain = [None] * z.L, None
    merge = Chain([dict(here=c["merge_here"], away=c["merge_away"])], hid)
    for l in reversed(range(z.L)):
        s = c if l else first
        d = call(
            partial(feed_back_kernel, z, l),
            dict(
                place=place, mask=a["mask"], grad=grad, inner=c["inner"], outer=c["outer"], norm_gain=norm_gain,
                **some(s, act_rows=0, slope_rows=0, normed2=0, unit2=0, rstd2=0),
            ),
            dict(
                half_grad=kept(z.N, z.C), feed_small=arr(8, z.C), here=kept(z.parts // 2, 2 * z.units, z.C, dtype=BF16),
                away=kept(z.parts // 2, 2 * z.units, z.C, dtype=BF16), **token,
            ),
            dict(
                vec=kept(3, 8, z.C), inner_sums=kept(8, z.H), g_outer=kept(z.C, z.H), g_inner=kept(z.C, z.H),
                turned=kept(2, z.H, z.C, dtype=BF16),
            ),
            6, 2, smem, [merge.here] + ([chain.here] if chain else []),
        )
        (chain or merge).step(d["token"])
        t = call(
            partial(token_back_kernel, z, l),
            dict(
                sizes=sizes, place=place, mask=a["mask"], half_grad=d["half_grad"], feed_small=d["feed_small"],
                perm=b["perm"], ewp=b["ewp"], **some(s, mixed=0, cat=0, share=0, pool=0, pooled=0, act=0, slope=0), **small,
            ),
            dict(
                mixed_grad=kept(z.N, z.I * z.C, dtype=BF16), scaled=kept(3 * z.C, z.I * z.C, dtype=BF16),
                push=kept(3, 8, z.C), here=kept(z.parts // 2, z.shared, z.C, dtype=BF16),
                away=kept(z.parts // 2, z.shared, z.C, dtype=BF16), **token,
            ),
            dict(
                vec=kept(2, 8, z.C), g_project=kept(z.C, z.C), g_mix=kept(z.I * z.C, 3 * z.C),
                rows=kept(z.parts * z.shared, z.C, dtype=BF16),
            ),
            4, 1, smem, [(chain or merge).here],
        )
        own = Chain([d, t], hid)
        if chain:
            rows = jnp.concatenate([chain.halve(t["token"]), merge.halve(t["token"])], axis=0)
            chain.widen(rows, img)
        if chain:
            own.step()
        held = [own.here] + ([chain.here] if chain else [])
        e = call(
            partial(mix_back_kernel, z, l, l == 0),
            dict(
                mask=a["mask"], back=a["back"], norm_gain=norm_gain, half_grad=d["half_grad"],
                **some(t, mixed_grad=0, scaled=0, push=0), **some(s, unit1=0, rstd1=0),
            ),
            dict(state_grad=kept(z.N, z.C) if l else arr(z.N0, z.C), first_norm=arr(2, z.C), **token),
            dict(back_h=kept(z.long, z.C), back_w=kept(z.long, z.C), back_c=kept(z.long, z.C), vec=kept(2, 8, z.C)),
            5, 0.05, (), held,
        )
        own.step(e["token"])
        if chain:
            chain.step(None, own.here)
        else:
            merge.step(e["token"])
        chain, last = chain or own, own
        grad, norms[l] = e["state_grad"], e["first_norm"]
    images_grad = grad.reshape(z.side, z.side, z.I, z.C).transpose(2, 0, 1, 3)

    f = call(
        partial(features_kernel, z),
        dict(patch=c["patch"], merge_weight=merge_t, merge_bias=merge_bias.reshape(1, -1)),
        dict(features=arr(z.I, z.half, z.half * z.O, dtype=BF16), **token), dict(merged=kept(z.I * z.M, z.O)), 6, 2, (), [last.here],
    )
    norm_rows = jnp.pad(jnp.concatenate(norms, axis=0), ((0, 16 - 2 * z.L), (0, 0))).astype(BF16)
    last.widen(jnp.concatenate([last.halve(f["token"]), norm_rows], axis=0), img)
    while chain.left:
        chain.step(None, last.here)
    feed, cut = 2 * z.units, 2 * z.units + z.shared
    merge = chain.here[None, feed:]
    bits = bits_of(hid)
    bits = bits[1:] + bits[:1]

    def widen_merge(merge, bit):
        return jnp.concatenate([merge, swap(merge, "hid", hid, bit)], axis=0)

    merge = widen_merge(merge, bits[0])
    while len(last.left) > 1:
        last.step()
    last.step(None, merge)
    feed_rows = jnp.concatenate([last.here[:feed], chain.here[:feed]], axis=0)
    have = last.here[feed:cut]
    norm_rows = last.here[cut:]
    z.found = [0]
    for step, bit in enumerate(bits):
        sent = jnp.concatenate([have, norm_rows], axis=0)
        got = swap(sent, "hid", hid, bit)
        z.found = z.found + [e ^ bit for e in z.found]
        if step + 2 < len(bits):
            merge = widen_merge(merge, bits[step + 1])
            got, _ = lax.optimization_barrier((got, merge))
        elif step + 2 == len(bits):
            merge_got = swap(merge, "hid", hid, bits[-1])
        if step + 1 < len(bits):
            have = jnp.concatenate([have, got[:-16]], axis=0)
            norm_rows = add(norm_rows, got[-16:], None)
    g = call(
        partial(last_kernel, z),
        dict(place=place, have=sent, got=got, merge_have=merge, merge_got=merge_got, feed_rows=feed_rows),
        final_outputs(z),
        dict(rows=kept(z.L, z.parts * z.shared, z.C, dtype=BF16), merge_rows=kept(z.parts * z.merge, z.C, dtype=BF16)),
        5, 2, smem,
    )
    return (
        f["features"], images_grad, g["mix_weight"], g["mix_bias"], g["squeeze_weight"].transpose(0, 2, 1),
        g["squeeze_bias"], g["expand_weight"], g["expand_bias"], g["project_weight"], g["project_bias"], g["norm_gain"],
        g["norm_bias"], g["inner_weight"].transpose(0, 2, 1), g["inner_bias"], g["outer_weight"], g["outer_bias"],
        g["merge_weight"].T, g["merge_bias"],
    )


def solution(mesh):
    maps = ("img", "hid")
    in_specs = (
        P(maps, None, None, None), P(maps, None), P(maps, None, None), P(), P(), P(), P(), P(), P(), P(), P(), P(), P(),
        P(None, None, "hid"), P(None, "hid"), P(None, "hid", None), P(), P(), P(),
    )
    out_specs = (
        P(maps, None, None), P(maps, None, None, None), P(), P(), P(), P(), P(), P(), P(), P(), P(), P(),
        P(None, None, "hid"), P(None, "hid"), P(None, "hid", None), P(), P(), P(),
    )
    return jax.shard_map(
        partial(per_device, mesh.shape["img"], mesh.shape["hid"]),
        mesh=mesh, in_specs=in_specs, out_specs=out_specs, check_vma=False,
    )
```

```python
from functools import partial

import jax
import jax.numpy as jnp
from jax import lax
from jax.experimental import pallas as pl
from jax.experimental.pallas import tpu as pltpu
from jax.sharding import PartitionSpec as P

F32 = jnp.float32
BF16 = jnp.bfloat16
GROUP = 8
MIB = 2**20


def dot(a, b, dims=(1, 0)):
    return lax.dot_general(a, b, (((dims[0],), (dims[1],)), ((), ())), preferred_element_type=F32)


def halves(v):
    high = v.astype(BF16)
    return high, (v - high.astype(F32)).astype(BF16)


def fine(a, b, dims=(1, 0)):
    high, low = halves(a)
    if dims == (0, 0):
        b_high, b_low = halves(b)
        return dot(jnp.concatenate([high, low, high], axis=0), jnp.concatenate([b_high, b_high, b_low], axis=0), dims)
    rows = a.shape[0]
    both = jnp.concatenate([high, low], axis=0)
    if b.dtype == BF16:
        out = dot(both, b, dims)
        return out[:rows] + out[rows:]
    b_high, b_low = halves(b)
    out = dot(both, b_high, dims)
    return out[:rows] + (out[rows:] + dot(high, b_low, dims))


def rows8(v):
    return v.reshape(-1, 8, v.shape[-1]).sum(axis=0)


def total(v):
    return v.sum(axis=0, keepdims=True)


def tile(v, rows):
    return jnp.broadcast_to(v[None], (rows // 8, 8, v.shape[-1])).reshape(rows, v.shape[-1])


def gelu_pair(x):
    cdf = 0.5 * lax.erf(x * 0.7071067811865476) + 0.5
    bell = jnp.exp2(x * x * (-0.5 * 1.4426950408889634))
    return x * cdf, cdf + x * bell * 0.3989422804014327


def norm_parts(v):
    centred = v - jnp.mean(v, axis=-1, keepdims=True)
    rstd = lax.rsqrt(jnp.mean(centred * centred, axis=-1, keepdims=True) + 1e-05)
    return centred * rstd, jnp.broadcast_to(rstd, v.shape)


def norm_back(grad, unit, rstd, gain):
    scaled = grad * gain
    first = jnp.mean(scaled, axis=-1, keepdims=True)
    second = jnp.mean(scaled * unit, axis=-1, keepdims=True)
    return rstd * (scaled - first - unit * second)


class Sizes:
    def __init__(self, images, side, channels, hidden, red, out, layers, parts):
        self.I, self.side, self.C, self.H, self.R, self.O, self.L = images, side, channels, hidden, red, out, layers
        self.parts, self.units = parts, hidden // parts
        self.W = side * images
        self.N0 = side * self.W
        self.N = -(-self.N0 // 384) * 384
        self.run_first = self.run_back = self.run_mix = self.N
        self.run_second = self.N // 7
        self.half = side // 2
        self.hp = -(-self.half // 8) * 8
        self.M = self.half * self.hp
        self.base = self.W
        self.tall = self.W * (2 * self.hp + 2)
        self.long = self.base + self.N + self.W
        self.at_project = 3 * channels
        self.at_expand = self.at_project + channels
        self.at_squeeze = self.at_expand + 3 * red
        self.at_small = self.at_squeeze + red
        self.shared = -(-(self.at_small + 16) // (16 * parts)) * 16
        self.merge = -(-(9 * out + 3) // (16 * parts)) * 16


class Refs:
    pass


def call(body, ins, outs, scratch, limit, micros, smem=(), after=(), far=()):
    waits = {f"after{k}": array for k, array in enumerate(after)}
    ins = dict(ins, **waits)
    vmem = pl.BlockSpec(memory_space=pltpu.VMEM)
    scalar, anywhere = pl.BlockSpec(memory_space=pltpu.SMEM), pl.BlockSpec(memory_space=pl.ANY)

    def place(name):
        return scalar if name in smem else anywhere if name in waits or name in far else vmem

    names = list(ins) + list(outs) + list(scratch)

    def kernel(*refs):
        r = Refs()
        for name, ref in zip(names, refs):
            setattr(r, name, ref)
        body(r)

    found = pl.pallas_call(
        kernel,
        out_shape=list(outs.values()),
        in_specs=[place(name) for name in ins],
        out_specs=[vmem] * len(outs),
        scratch_shapes=list(scratch.values()),
        compiler_params=pltpu.CompilerParams(vmem_limit_bytes=limit * MIB),
        cost_estimate=pl.CostEstimate(flops=int(micros * 1.15e9), bytes_accessed=0, transcendentals=0),
    )(*ins.values())
    return dict(zip(outs, found))


def arr(*shape, dtype=F32):
    return jax.ShapeDtypeStruct(shape, dtype)


def kept(*shape, dtype=F32):
    return pltpu.VMEM(shape, dtype)


def over(z, body, size):
    for at in range(0, z.N, size):
        body(slice(at, at + size), at)


def near(ref, start, off, size):
    return ref[start + off : start + off + size, :]


def parity(z, i):
    rows = lax.broadcasted_iota(jnp.int32, (8, z.C), 0)
    return jnp.where(rows % z.I == i, 1.0, 0.0)


def kinds(z, rows):
    return tile(lax.broadcasted_iota(jnp.int32, (8, z.C), 1) % 3, rows)


def weave(z, v):
    out = v[0:1] * parity(z, 0)
    for i in range(1, z.I):
        out += v[i : i + 1] * parity(z, i)
    return out


def split(z, v):
    rows = [total(v * parity(z, i)) for i in range(z.I)]
    return jnp.concatenate(rows + [jnp.zeros((GROUP - z.I, z.C), F32)], axis=0)


def front_kernel(z, r):
    rows = lax.broadcasted_iota(jnp.int32, (z.W, z.C), 0)
    lanes = lax.broadcasted_iota(jnp.int32, (z.W, z.C), 1) % 3
    image = rows % z.I
    col = rows // z.I
    high = jnp.zeros((z.W, z.C), jnp.int32)
    wide = jnp.zeros((z.W, z.C), jnp.int32)
    for i in range(z.I):
        high = jnp.where(image == i, r.sizes[i, 0], high)
        wide = jnp.where(image == i, r.sizes[i, 1], wide)
    inside = jnp.where(col < wide, 1.0, 0.0)
    first, last = col == 0, col == z.side - 1
    edge = jnp.where((first & (lanes == 2)) | (last & (lanes == 1)), 0.0, 1.0)
    back = jnp.where((last & (lanes == 2)) | (first & (lanes == 1)), 0.0, 1.0)

    def step(row, carry):
        at = pl.ds(pl.multiple_of(row * z.W, 8), z.W)
        r.mask[at, :] = jnp.where(high > row, inside, 0.0)
        return carry

    lax.fori_loop(0, z.side, step, 0)
    edge = jnp.concatenate([edge, edge], axis=0).astype(BF16)
    back = jnp.concatenate([back, back], axis=0).astype(BF16)

    def step2(row, carry):
        at = pl.ds(pl.multiple_of(row * 2 * z.W, 16), 2 * z.W)
        r.edge[at, :] = edge
        r.back[at, :] = back
        return carry

    lax.fori_loop(0, z.side // 2, step2, 0)
    pad = jnp.zeros((z.N - z.N0, z.C), F32)
    for ref in (r.mask, r.edge, r.back):
        ref[z.N0 :, :] = pad.astype(ref.dtype)
    pad = jnp.zeros((z.hp - z.half, z.O), F32)
    r.pgrad[z.M :, :] = jnp.zeros((8, 9 * z.C), F32)
    sums = jnp.zeros((8, z.O), F32)
    for i in range(z.I):
        for pair in range(z.half // 2):
            both = r.cotangent[i, :, 2 * pair * z.O : (2 * pair + 2) * z.O].astype(F32)
            both = jnp.concatenate([both[:, : z.O], pad, both[:, z.O :], pad], axis=0)
            at = i * z.M + 2 * pair * z.hp
            r.cot[at : at + 2 * z.hp, :] = both.astype(BF16)
            sums += rows8(both)
        step = z.M // 2
        for at in range(0, z.M, step):
            r.pgrad[at : at + step, :] = dot(r.cot[i * z.M + at : i * z.M + at + step, :], r.merge_weight[...])

        def part(dr, ds, b, down=0):
            k = 3 * dr + ds
            return r.pgrad[pl.ds(b * z.hp + down, z.hp), k * z.C : (k + 1) * z.C]

        for b in range(z.half):
            planes = [
                part(1, 1, b),
                part(2, 1, b) + part(0, 1, b, 1),
                part(1, 2, b),
                part(2, 2, b) + part(0, 2, b, 1),
            ]
            if b < z.half - 1:
                planes[2] += part(1, 0, b + 1)
                planes[3] += part(2, 0, b + 1) + part(0, 0, b + 1, 1)
            for plane, (down, right) in zip(planes, ((0, 0), (1, 0), (0, 1), (1, 1))):
                start = down * z.W + (2 * b + right) * z.I + i
                r.grad[pl.ds(start, z.hp, stride=2 * z.W), :] = plane
    r.merge_bias_sums[...] = sums
    r.token[...] = jnp.zeros_like(r.token)


def shift_phase(z, r, cat, size):
    r.sums[...] = jnp.zeros_like(r.sums)

    def body(rows, at):
        start = z.base + at
        kind = kinds(z, size)
        mid = near(r.normed, start, 0, size)
        high = jnp.where(kind == 2, near(r.normed, start, -z.W, size), near(r.normed, start, z.W, size))
        wide = jnp.where(kind == 2, near(r.normed, start, -z.I, size), near(r.normed, start, z.I, size))
        high = jnp.where(kind == 0, mid, high)
        wide = jnp.where(kind == 0, mid, wide * r.edge[rows, :].astype(F32))
        mask = r.mask[rows, :]
        for j, piece in enumerate((high, wide, mid)):
            cat[rows, j * z.C : (j + 1) * z.C] = piece.astype(BF16)
            r.sums[j] += rows8(piece * mask)

    over(z, body, size)


def counts_of(z, r):
    rows = []
    for i in range(GROUP):
        count = (r.sizes[i, 0] * r.sizes[i, 1]).astype(F32) if i < z.I else 1.0
        rows.append(jnp.full((1, z.C), 1.0, F32) * count)
    return jnp.concatenate(rows, axis=0)


def weigh_phase(z, r, l, o):
    pooled = r.mix_bias[l, 0:1] + r.mix_bias[l, 1:2]
    counts = counts_of(z, r)
    for j in range(3):
        pool = split(z, r.sums[j])
        o.pool[j] = pool
        pooled = pooled + fine(pool, r.mix_weight[l, j]) / counts
    o.pooled[...] = pooled
    act, slope = gelu_pair(fine(pooled, r.squeeze_weight[l], (1, 1)) + r.squeeze_bias[l : l + 1])
    o.act[...] = act
    o.slope[...] = slope
    logits = fine(act, r.ewp[l]) + r.ebp[l : l + 1]
    parts = [logits[:, j * z.C : (j + 1) * z.C] for j in range(3)]
    top = jnp.maximum(jnp.maximum(parts[0], parts[1]), parts[2])
    parts = [jnp.exp(part - top) for part in parts]
    whole = parts[0] + parts[1] + parts[2]
    for j in range(3):
        o.share[j] = parts[j] / whole


def mix_phase(z, r, l, o, size):
    share = [weave(z, o.share[j]) for j in range(3)]
    bias = tile(r.mix_bias[l, 0:1] * share[0] + r.mix_bias[l, 1:2] * share[1], size)
    share = [tile(s, size) for s in share]
    gain, shift = r.norm_gain[l, 1:2], r.norm_bias[l, 1:2]

    def body(rows, at):
        mixed = bias
        for j in range(3):
            mixed = mixed + dot(o.cat[rows, j * z.C : (j + 1) * z.C], r.mix_weight[l, j]) * share[j]
        mixed = mixed.astype(BF16)
        o.mixed[rows, :] = mixed
        token = dot(mixed, r.project_weight[l]) + r.project_bias[l : l + 1]
        halfway = r.state[rows, :] + r.mask[rows, :] * token
        unit, rstd = norm_parts(halfway)
        o.unit2[rows, :] = unit.astype(BF16)
        o.rstd2[rows, :] = rstd.astype(BF16)
        o.normed2[rows, :] = (unit * gain + shift).astype(BF16)
        r.state[rows, :] = halfway

    over(z, body, size)


def norm_store(z, r, l, o, rows, at, state):
    unit, rstd = norm_parts(state)
    o.unit1[rows, :] = unit.astype(BF16)
    o.rstd1[rows, :] = rstd.astype(BF16)
    r.normed[z.base + at : z.base + at + rows.stop - rows.start, :] = unit * r.norm_gain[l, 0:1] + r.norm_bias[l, 0:1]


def clear_edges(z, ref):
    ref[: z.base, :] = jnp.zeros((z.base, z.C), F32)
    ref[z.base + z.N0 :, :] = jnp.zeros((ref.shape[0] - z.base - z.N0, z.C), F32)


def unit_bias(z, blocks, l, which):
    at = 2 * z.L * z.units + l
    return jnp.concatenate([blocks[k, at : at + 1, : z.units].astype(F32) for k in which], axis=1)


def feed_some(o, rows, inner, bias, outer):
    act, slope = gelu_pair(dot(o.normed2[rows, :], inner, (1, 1)) + bias)
    act = act.astype(BF16)
    o.act_rows[rows, :] = act
    o.slope_rows[rows, :] = slope.astype(BF16)
    return dot(act, outer)


def half_kernel(z, r):
    which, u = range(z.parts // 2), z.units
    inner = jnp.concatenate([r.gathered[k, :u, :] for k in which], axis=0)
    outer = jnp.concatenate([r.gathered[k, u : 2 * u, :] for k in which], axis=0)
    bias = unit_bias(z, r.gathered, 0, which)

    def body(rows, at):
        r.partial[rows, :] = feed_some(r, rows, inner, bias, outer) + r.outer_bias[0:1]

    over(z, body, z.run_second)
    r.token[...] = jnp.zeros_like(r.token)


def feed_phase(z, r, l, o, source, after):
    first = 0 if l else z.H // 2

    def body(rows, at):
        out = feed_some(o, rows, r.inner[l, first:, :], r.inner_bias[l : l + 1, first:], r.outer[l, first:, :])
        out = out + (r.outer_bias[l : l + 1] if l else r.partial[rows, :])
        state = source[rows, :] + r.mask[rows, :] * out
        after(rows, at, state)

    over(z, body, z.run_second)


def saved_early(z):
    return dict(
        unit1=kept(z.N, z.C, dtype=BF16), rstd1=kept(z.N, z.C, dtype=BF16), cat=kept(z.N, 3 * z.C, dtype=BF16), mixed=kept(z.N, z.C, dtype=BF16),
        unit2=kept(z.N, z.C, dtype=BF16), rstd2=kept(z.N, z.C, dtype=BF16), normed2=kept(z.N, z.C, dtype=BF16), pool=kept(3, GROUP, z.C),
        pooled=kept(GROUP, z.C), act=kept(GROUP, z.R), slope=kept(GROUP, z.R), share=kept(3, GROUP, z.C),
    )


def saved_late(z):
    return dict(act_rows=kept(z.N, z.H, dtype=BF16), slope_rows=kept(z.N, z.H, dtype=BF16))


def first_kernel(z, r):
    spots = lax.broadcasted_iota(jnp.int32, (3 * z.C, 3 * z.C), 0)
    ends = lax.broadcasted_iota(jnp.int32, (3 * z.C, 3 * z.C), 1)
    kind = jnp.where(ends >= 2 * z.C, 2, jnp.where(ends >= z.C, 1, 0))
    r.perm[...] = jnp.where(spots == 3 * (ends - kind * z.C) + kind, 1.0, 0.0).astype(BF16)
    blank = jnp.zeros((8 - z.L, 3 * z.C), F32)
    rows = [r.expand_weight[l] for l in range(z.L)] + [r.expand_bias[...], blank]
    rows = fine(jnp.concatenate(rows, axis=0), r.perm[...])
    for l in range(z.L):
        r.ewp[l] = rows[l * z.R : (l + 1) * z.R]
    r.ebp[...] = rows[z.L * z.R : z.L * z.R + z.L]

    def begin(rows, at):
        real = min(rows.stop, z.N0) - at
        state = r.images[at : at + real, :].astype(F32) * r.mask[at : at + real, :]
        if real < rows.stop - at:
            state = jnp.concatenate([state, jnp.zeros((rows.stop - at - real, z.C), F32)], axis=0)
        r.state[rows, :] = state
        norm_store(z, r, 0, r, rows, at, state)

    over(z, begin, z.run_first)
    clear_edges(z, r.normed)
    shift_phase(z, r, r.cat, z.run_first)
    weigh_phase(z, r, 0, r)
    mix_phase(z, r, 0, r, z.run_first)
    r.token[...] = jnp.zeros_like(r.token)


def exchange_order(n):
    bits = bits_of(n)
    return bits[:1] + bits[:0:-1]


def rank(n, e):
    return sum((n >> k + 1) * (e // bit % 2) for k, bit in enumerate(exchange_order(n)))


def put_blocks(z, me, rows, size, here, away):
    for e in range(z.parts):
        put_block(z, e, rows[pl.ds(pl.multiple_of((me ^ e) * size, 16), size), :], here, away)


def put_block(z, e, block, here, away, start=0):
    at, half, stop = rank(z.parts, e), z.parts // 2, start + block.shape[0]
    if at < half:
        here[at, start:stop, :] = block
    else:
        away[at - half, start:stop, :] = block


def second_kernel(z, r):
    me = r.place[0]
    for k in range(z.parts):
        at = k * z.units
        for l in range(z.L):
            r.inner[l, at : at + z.units, :] = r.gathered[k, 2 * l * z.units : (2 * l + 1) * z.units, :]
            r.outer[l, at : at + z.units, :] = r.gathered[k, (2 * l + 1) * z.units : (2 * l + 2) * z.units, :]
    for l in range(z.L):
        r.inner_bias[l : l + 1] = unit_bias(z, r.gathered, l, range(z.parts))
    early, late = [Refs() for _ in range(z.L)], [Refs() for _ in range(z.L)]
    for l in range(z.L):
        early[l].normed2 = r.normed2_0 if l == 0 else r.normed2
        early[l].act_rows = r.act_rows_0 if l == 0 else r.act_rows
        early[l].slope_rows = r.slope_rows_0 if l == 0 else r.slope_rows

    def then_norm(rows, at, state):
        r.state[rows, :] = state
        norm_store(z, r, 1, r, rows, at, state)

    feed_phase(z, r, 0, early[0], r.state_in, then_norm)
    clear_edges(z, r.normed)
    shift_phase(z, r, r.cat, z.run_second)
    weigh_phase(z, r, 1, r)
    mix_phase(z, r, 1, r, z.run_second)

    def then_keep(rows, at, state):
        r.normed[z.base + at : z.base + at + rows.stop - rows.start, :] = state

    feed_phase(z, r, 1, early[1], r.state, then_keep)
    for i in range(z.I):
        for pair in range(z.half // 2):
            at = i * z.M + 2 * pair * z.hp
            for k in range(9):
                dr, ds = divmod(k, 3)
                two = []
                for b in (2 * pair, 2 * pair + 1):
                    col = 2 * b + ds - 1
                    if col < 0:
                        two.append(jnp.zeros((z.hp, z.C), F32))
                    else:
                        two.append(r.normed[pl.ds(dr * z.W + col * z.I + i, z.hp, stride=2 * z.W), :])
                r.patch[at : at + 2 * z.hp, k * z.C : (k + 1) * z.C] = jnp.concatenate(two, axis=0).astype(BF16)
    for k in range(9):
        grad = dot(r.cot[...], r.patch[:, k * z.C : (k + 1) * z.C], (0, 0))
        r.merge_rows[k * z.O : (k + 1) * z.O, :] = grad.astype(BF16)
    bias = total(r.merge_bias_sums[...])
    rest = z.O - 2 * z.C
    rows = [bias[:, : z.C], bias[:, z.C : 2 * z.C]]
    rows += [jnp.concatenate([bias[:, 2 * z.C :], jnp.zeros((1, z.C - rest), F32)], axis=1)]
    rows += [jnp.zeros((z.parts * z.merge - 9 * z.O - 3, z.C), F32)]
    r.merge_rows[9 * z.O :, :] = jnp.concatenate(rows, axis=0).astype(BF16)
    put_blocks(z, me, r.merge_rows, z.merge, r.merge_here, r.merge_away)


def features_kernel(z, r):
    r.merged[...] = dot(r.patch[...], r.merge_weight[...], (1, 1)) + r.merge_bias[...]
    r.token[...] = jnp.zeros_like(r.token)
    for i in range(z.I):
        for pair in range(z.half // 2):
            at = i * z.M + 2 * pair * z.hp
            wide = [r.merged[at : at + z.half, :], r.merged[at + z.hp : at + z.hp + z.half, :]]
            wide = jnp.concatenate(wide, axis=1).astype(BF16)
            r.features[i, :, 2 * pair * z.O : (2 * pair + 2) * z.O] = wide


def feed_back_kernel(z, l, r):
    gain = r.norm_gain[l, 1:2]
    for ref in (r.vec, r.inner_sums, r.g_outer, r.g_inner):
        ref[...] = jnp.zeros_like(ref)

    def units(late, early, rows):
        return late[rows, :] if l else jnp.concatenate([early[rows, :], late[rows, :]], axis=1)

    def body(rows, at):
        mask = r.mask[rows, :]
        grad = r.grad[rows, :]
        slope = units(r.slope_rows, None if l else r.slope_before, rows)
        act = units(r.act_rows, None if l else r.act_before, rows)
        out = grad * mask
        r.vec[0] += rows8(out)
        out = out.astype(BF16)
        pre = dot(out, r.outer[l], (1, 1)) * slope.astype(F32)
        r.inner_sums[...] += rows8(pre)
        pre = pre.astype(BF16)
        r.g_outer[...] += dot(out, act, (0, 0))
        r.g_inner[...] += dot(r.normed2[rows, :], pre, (0, 0))
        normed_grad = dot(pre, r.inner[l])
        unit = r.unit2[rows, :].astype(F32)
        r.vec[1] += rows8(normed_grad * unit)
        r.vec[2] += rows8(normed_grad)
        r.half_grad[rows, :] = grad + norm_back(normed_grad, unit, r.rstd2[rows, :].astype(F32), gain)

    over(z, body, z.run_back)
    inner, me = total(r.inner_sums[...]), r.place[0]
    for k, e in enumerate(z.gathered):
        r.unit_sums[me ^ e] = inner[:, k * z.units : (k + 1) * z.units]
    inner = jnp.concatenate([r.unit_sums[k] for k in range(z.parts)], axis=1)
    small = [total(r.vec[k]) for k in range(3)]
    small += [inner[:, k * z.C : (k + 1) * z.C] for k in range(z.H // z.C)]
    small += [jnp.zeros((1, z.C), F32)]
    r.feed_small[...] = jnp.concatenate(small, axis=0)
    r.turned[0] = r.g_inner[...].T.astype(BF16)
    r.turned[1] = r.g_outer[...].T.astype(BF16)
    for k in range(2):
        for spot, e in enumerate(z.gathered):
            block = r.turned[k, spot * z.units : (spot + 1) * z.units, :]
            put_block(z, e, block, r.here, r.away, k * z.units)
    r.token[...] = jnp.zeros_like(r.token)


def token_back_kernel(z, l, r):
    for ref in (r.vec, r.g_project, r.g_mix):
        ref[...] = jnp.zeros_like(ref)
    even, odd = tile(parity(z, 0), z.run_back), tile(parity(z, 1), z.run_back)

    def body(rows, at):
        token = r.half_grad[rows, :] * r.mask[rows, :]
        r.vec[0] += rows8(token)
        token = token.astype(BF16)
        r.g_project[...] += dot(r.mixed[rows, :], token, (0, 0))
        mixed_grad = dot(token, r.project_weight[l], (1, 1))
        r.vec[1] += rows8(mixed_grad)
        both = jnp.concatenate([(mixed_grad * even).astype(BF16), (mixed_grad * odd).astype(BF16)], axis=1)
        r.mixed_grad[rows, :] = both
        r.g_mix[...] += dot(both, r.cat[rows, :], (0, 0))

    over(z, body, z.run_back)
    counts = counts_of(z, r)
    zeros = jnp.zeros((GROUP - z.I, z.C), F32)
    summed = split(z, r.vec[1])
    share = [r.share[j] for j in range(3)]
    mix, dp = [], []
    for j in range(3):
        weight = r.mix_weight[l, j].astype(F32)
        rows = []
        found = 0.0
        for i in range(z.I):
            block = r.g_mix[i * z.C : (i + 1) * z.C, j * z.C : (j + 1) * z.C].T
            rows.append(total(weight * block))
            found = found + block * share[j][i : i + 1]
            scaled = weight * share[j][i : i + 1]
            r.scaled[j * z.C : (j + 1) * z.C, i * z.C : (i + 1) * z.C] = scaled.astype(BF16)
        mix.append(found)
        dp.append(jnp.concatenate(rows + [zeros], axis=0))
    for j in range(2):
        dp[j] += summed * r.mix_bias[l, j : j + 1]
    even = dp[0] * share[0] + dp[1] * share[1] + dp[2] * share[2]
    dz = jnp.concatenate([share[j] * (dp[j] - even) for j in range(3)], axis=1)
    act, slope, pooled = r.act[...], r.slope[...], r.pooled[...]
    expand = fine(jnp.concatenate([fine(act, dz, (0, 0)), dz], axis=0), r.perm[...], (1, 1))
    expand, expand_bias = expand[: z.R], total(expand[z.R :])
    dact = fine(dz, r.ewp[l], (1, 1)) * slope
    squeeze = fine(dact, pooled, (0, 0))
    dpool = fine(dact, r.squeeze_weight[l])
    push = dpool / counts
    for j in range(3):
        mix[j] += fine(r.pool[j], push, (0, 0))
        r.push[j] = weave(z, fine(push, r.mix_weight[l, j], (1, 1)))
    for j in range(3):
        r.rows[j * z.C : (j + 1) * z.C, :] = mix[j].astype(BF16)
    r.rows[z.at_project : z.at_expand, :] = r.g_project[...].astype(BF16)
    for j in range(3):
        at = z.at_expand + j * z.R
        r.rows[at : at + z.R, :] = expand[:, j * z.C : (j + 1) * z.C].astype(BF16)
    r.rows[z.at_squeeze : z.at_small, :] = squeeze.astype(BF16)
    small = [total(share[j] * summed + dpool) for j in range(2)]
    small += [total(r.vec[0]), r.feed_small[: 3 + z.H // z.C, :]]
    small += [expand_bias[:, j * z.C : (j + 1) * z.C] for j in range(3)]
    small += [jnp.concatenate([total(dact), jnp.zeros((1, z.C - z.R), F32)], axis=1)]
    used = sum(row.shape[0] for row in small)
    small += [jnp.zeros((z.parts * z.shared - z.at_small - used, z.C), F32)]
    r.rows[z.at_small :, :] = jnp.concatenate(small, axis=0).astype(BF16)
    put_blocks(z, r.place[0], r.rows, z.shared, r.here, r.away)
    r.token[...] = jnp.zeros_like(r.token)


def mix_back_kernel(z, l, last, r):
    for ref in (r.back_h, r.back_w):
        clear_edges(z, ref)
    gain = r.norm_gain[l, 0:1]
    size = z.run_mix
    push = [tile(r.push[j], size) for j in range(3)]

    def spread(rows, at):
        mask = r.mask[rows, :]
        parts = dot(r.mixed_grad[rows, :], r.scaled[...], (1, 1))
        for j, ref in enumerate((r.back_h, r.back_w, r.back_c)):
            ref[z.base + at : z.base + at + size, :] = parts[:, j * z.C : (j + 1) * z.C] + mask * push[j]

    over(z, spread, size)
    r.vec[...] = jnp.zeros_like(r.vec)

    def body(rows, at):
        start = z.base + at
        kind = kinds(z, size)
        high = jnp.where(kind == 2, near(r.back_h, start, z.W, size), near(r.back_h, start, -z.W, size))
        wide = jnp.where(kind == 2, near(r.back_w, start, z.I, size), near(r.back_w, start, -z.I, size))
        high = jnp.where(kind == 0, near(r.back_h, start, 0, size), high)
        wide = jnp.where(kind == 0, near(r.back_w, start, 0, size), wide * r.back[rows, :].astype(F32))
        grad = high + wide + near(r.back_c, start, 0, size)
        unit = r.unit1[rows, :].astype(F32)
        r.vec[0] += rows8(grad * unit)
        r.vec[1] += rows8(grad)
        grad = r.half_grad[rows, :] + norm_back(grad, unit, r.rstd1[rows, :].astype(F32), gain)
        if last:
            real = min(rows.stop, z.N0) - at
            r.state_grad[at : at + real, :] = (grad * r.mask[rows, :])[:real]
        else:
            r.state_grad[rows, :] = grad

    over(z, body, size)
    stray = r.back_h[z.base + z.N0 - z.W : z.base + z.N0, :]
    r.vec[1] -= rows8(jnp.where(kinds(z, z.W) == 1, stray, 0.0))
    r.first_norm[...] = jnp.concatenate([total(r.vec[0]), total(r.vec[1])], axis=0)
    r.token[...] = jnp.zeros_like(r.token)


def final_outputs(z):
    return dict(
        mix_weight=arr(z.L, 3, z.C, z.C), mix_bias=arr(z.L, 2, z.C), squeeze_weight=arr(z.L, z.R, z.C),
        squeeze_bias=arr(z.L, z.R), expand_weight=arr(z.L, z.R, 3 * z.C), expand_bias=arr(z.L, 3 * z.C),
        project_weight=arr(z.L, z.C, z.C), project_bias=arr(z.L, z.C), norm_gain=arr(z.L, 2, z.C),
        norm_bias=arr(z.L, 2, z.C), inner_weight=arr(z.L, z.units, z.C), inner_bias=arr(z.L, z.units),
        outer_weight=arr(z.L, z.units, z.C), outer_bias=arr(z.L, z.C), merge_weight=arr(z.O, 9 * z.C),
        merge_bias=arr(z.O),
    )


def last_kernel(z, r):
    me = r.place[0]
    half = z.parts // 2
    size = z.shared
    for at in range(z.parts):
        k = at % half
        have, merge = (r.have, r.merge_have) if at < half else (r.got, r.merge_got)
        rows = pl.ds(pl.multiple_of((me ^ z.found[at]) * z.shared, 16), z.shared)
        r.rows[0, rows, :] = have[k * size : (k + 1) * size, :]
        r.rows[1, rows, :] = merge[k, :size, :]
        rows = pl.ds(pl.multiple_of((me ^ z.found[at]) * z.merge, 16), z.merge)
        r.merge_rows[rows, :] = merge[k, size:, :]
    norms = r.have[half * size :, :].astype(F32) + r.got[half * size :, :].astype(F32)
    for l in range(z.L):
        rows = r.rows.at[l]

        def get(at, count):
            return rows[at : at + count, :].astype(F32)

        for j in range(3):
            r.mix_weight[l, j] = get(j * z.C, z.C)
            r.expand_weight[l, :, j * z.C : (j + 1) * z.C] = get(z.at_expand + j * z.R, z.R)
        r.project_weight[l] = get(z.at_project, z.C)
        r.squeeze_weight[l] = get(z.at_squeeze, z.R)
        small = get(z.at_small, 16)
        r.mix_bias[l] = small[0:2]
        r.project_bias[l : l + 1] = small[2:3]
        r.outer_bias[l : l + 1] = small[3:4]
        r.norm_gain[l] = jnp.concatenate([norms[2 * l : 2 * l + 1], small[4:5]], axis=0)
        r.norm_bias[l] = jnp.concatenate([norms[2 * l + 1 : 2 * l + 2], small[5:6]], axis=0)
        at = 6
        inner = jnp.zeros((1, z.units), F32)
        for k in range(z.H // z.C):
            for c in range(0, z.C, z.units):
                mine = jnp.where(me == (k * z.C + c) // z.units, 1.0, 0.0)
                inner = inner + small[at : at + 1, c : c + z.units] * mine
            at += 1
        r.inner_bias[l : l + 1] = inner
        for j in range(3):
            r.expand_bias[l : l + 1, j * z.C : (j + 1) * z.C] = small[at : at + 1]
            at += 1
        r.squeeze_bias[l : l + 1] = small[at : at + 1, : z.R]
        feed = r.feed_rows[2 * l * z.units : 2 * (l + 1) * z.units, :].astype(F32)
        r.inner_weight[l] = feed[: z.units]
        r.outer_weight[l] = feed[z.units :]
    for k in range(9):
        r.merge_weight[:, k * z.C : (k + 1) * z.C] = r.merge_rows[k * z.O : (k + 1) * z.O, :].astype(F32)
    small = r.merge_rows[9 * z.O : 9 * z.O + 16, :].astype(F32)
    r.merge_bias[: z.C] = small[0]
    r.merge_bias[z.C : 2 * z.C] = small[1]
    r.merge_bias[2 * z.C :] = small[2, : z.O - 2 * z.C]


def pack_kernel(z, r):
    u = z.units
    copies = [pltpu.make_async_copy(r.inner_bias, r.bias, r.sem.at[2 * z.L])]
    for l in range(z.L):
        for k, ref in enumerate((r.inner_weight, r.outer_weight)):
            at = (2 * l + k) * u
            copies.append(pltpu.make_async_copy(ref.at[l], r.block.at[at : at + u], r.sem.at[2 * l + k]))
    for copy in copies:
        copy.start()
    for copy in copies:
        copy.wait()
    bias = r.bias[...].astype(F32)
    if u < z.C:
        bias = jnp.concatenate([bias, jnp.zeros((z.L, z.C - u), F32)], axis=1)
    bias = jnp.concatenate([bias, jnp.zeros((16 - z.L, z.C), F32)], axis=0)
    r.block[2 * z.L * u :, :] = bias.astype(BF16)


def swap(x, axis, n, bit):
    return lax.ppermute(x, axis, [(a, a ^ bit) for a in range(n)])


def bits_of(n):
    return [1 << k for k in range(n.bit_length() - 1)]


def add(here, got, token):
    out = here.astype(F32) + got.astype(F32)
    if token is not None:
        out = out + token[0]
    return out.astype(BF16)


def take(tokens):
    return tokens.pop(0) if tokens else None


class Chain:
    def __init__(self, parts, hid):
        self.here = jnp.concatenate([part["here"] for part in parts], axis=1)
        self.away = jnp.concatenate([part["away"] for part in parts], axis=1)
        self.left = [("hid", hid, bit) for bit in exchange_order(hid)]

    def step(self, token=None, tie=None):
        axis, n, bit = self.left.pop(0)
        got = swap(self.away, axis, n, bit)
        if tie is not None:
            got, tie = lax.optimization_barrier((got, tie))
        x = add(self.here, got, token)
        if axis == "img":
            self.here = self.away = x
            return tie
        half = x.shape[0] // 2
        self.here, self.away = (x[:half], x[half:]) if half else (x[0], None)
        return tie

    def halve(self, token):
        while self.left:
            self.step(token)
        return self.here

    def widen(self, rows, img):
        self.here = self.away = rows
        self.left = [("img", img, bit) for bit in bits_of(img)]


def per_device(
    img, hid, images, sizes, cotangent, mix_weight, mix_bias, squeeze_weight, squeeze_bias, expand_weight, expand_bias,
    project_weight, project_bias, norm_gain, norm_bias, inner_weight, inner_bias, outer_weight, outer_bias,
    merge_weight, merge_bias,
):
    z = Sizes(
        images.shape[0], images.shape[1], images.shape[3], inner_weight.shape[2] * hid, squeeze_weight.shape[2],
        merge_weight.shape[1], mix_weight.shape[0], hid,
    )
    place = lax.axis_index("hid").reshape(1)
    flat = images.transpose(1, 2, 0, 3).reshape(z.N0, z.C)
    merge_t = merge_weight.T
    squeeze_t = squeeze_weight.transpose(0, 2, 1)
    far = [pltpu.with_memory_space_constraint(v, pltpu.HBM) for v in (inner_weight.transpose(0, 2, 1), outer_weight, inner_bias)]
    block = call(
        partial(pack_kernel, z),
        dict(place=place, inner_weight=far[0], outer_weight=far[1], inner_bias=far[2]),
        dict(block=kept(2 * z.L * z.units + 16, z.C, dtype=BF16)),
        dict(bias=kept(z.L, z.units, dtype=BF16), sem=pltpu.SemaphoreType.DMA((2 * z.L + 1,))),
        2, 1, dict(place=0), far=dict(inner_weight=0, outer_weight=0, inner_bias=0),
    )
    block = block["block"]
    smem = dict(sizes=0, place=0)
    small = dict(
        mix_weight=mix_weight, mix_bias=mix_bias, squeeze_weight=squeeze_t, squeeze_bias=squeeze_bias,
        project_weight=project_weight, project_bias=project_bias, norm_gain=norm_gain, norm_bias=norm_bias,
    )
    token = dict(token=arr(1, z.C))
    a = call(
        partial(front_kernel, z),
        dict(sizes=sizes, place=place, cotangent=cotangent, merge_weight=merge_t),
        dict(
            mask=kept(z.N, z.C), edge=kept(z.N, z.C, dtype=BF16), back=kept(z.N, z.C, dtype=BF16), cot=kept(z.I * z.M, z.O, dtype=BF16),
            grad=kept(z.tall, z.C), merge_bias_sums=kept(8, z.O), **token,
        ),
        dict(pgrad=kept(z.M + 8, 9 * z.C)),
        4, 3, smem,
    )
    order = bits_of(hid)[1:] + [1]

    def widen(have, bit, token):
        got = swap(have, "hid", hid, bit)
        return jnp.concatenate([have, got if token is None else got + token.astype(BF16)], axis=0)

    z.gathered = [0]
    for bit in order:
        z.gathered = z.gathered + [e ^ bit for e in z.gathered]
    have = widen(block[None], order[0], a["token"])
    b = call(
        partial(first_kernel, z),
        dict(
            images=flat, sizes=sizes, mask=a["mask"], edge=a["edge"], expand_weight=expand_weight, expand_bias=expand_bias,
            **small,
        ),
        dict(
            state=kept(z.N, z.C), perm=kept(3 * z.C, 3 * z.C, dtype=BF16), ewp=kept(z.L, z.R, 3 * z.C),
            ebp=kept(z.L, 3 * z.C), **saved_early(z), **token,
        ),
        dict(normed=kept(z.long, z.C), sums=kept(3, 8, z.C)),
        5, 5, smem, [have],
    )
    for bit in order[1:-1]:
        have = widen(have, bit, b["token"] if bit == order[1] else None)
    late, some_units = saved_late(z), kept(z.N, z.H // 2, dtype=BF16)
    h = call(
        partial(half_kernel, z),
        dict(gathered=have, normed2=b["normed2"], outer_bias=outer_bias),
        dict(partial=kept(z.N, z.C), act_rows=some_units, slope_rows=some_units, **token), {}, 4, 2,
    )
    have = widen(have, order[-1], h["token"])
    c = call(
        partial(second_kernel, z),
        dict(
            sizes=sizes, mask=a["mask"], edge=a["edge"], state_in=b["state"], normed2_0=b["normed2"], gathered=have,
            partial=h["partial"], place=place,
            ewp=b["ewp"], ebp=b["ebp"], outer_bias=outer_bias, cot=a["cot"], merge_bias_sums=a["merge_bias_sums"], **small,
        ),
        dict(
            patch=kept(z.I * z.M, 9 * z.C, dtype=BF16),
            merge_here=kept(z.parts // 2, z.merge, z.C, dtype=BF16), merge_away=kept(z.parts // 2, z.merge, z.C, dtype=BF16),
            inner=kept(z.L, z.H, z.C, dtype=BF16), outer=kept(z.L, z.H, z.C, dtype=BF16),
            act_rows_0=some_units, slope_rows_0=some_units, **saved_early(z), **late,
        ),
        dict(
            state=kept(z.N, z.C), normed=kept(z.tall, z.C), sums=kept(3, 8, z.C), inner_bias=kept(z.L, z.H),
            merge_rows=kept(z.parts * z.merge, z.C, dtype=BF16),
        ),
        11, 16, smem,
    )
    first = dict(b, act_rows=c["act_rows_0"], slope_rows=c["slope_rows_0"])
    before = dict(act_before=h["act_rows"], slope_before=h["slope_rows"])

    def some(s, **names):
        return {name: s[name] for name in names}

    grad = a["grad"]
    norms, chain = [None] * z.L, None
    merge = Chain([dict(here=c["merge_here"], away=c["merge_away"])], hid)
    for l in reversed(range(z.L)):
        s = c if l else first
        d = call(
            partial(feed_back_kernel, z, l),
            dict(
                place=place, mask=a["mask"], grad=grad, inner=c["inner"], outer=c["outer"], norm_gain=norm_gain,
                **some(s, act_rows=0, slope_rows=0, normed2=0, unit2=0, rstd2=0), **({} if l else before),
            ),
            dict(
                half_grad=kept(z.N, z.C), feed_small=arr(8, z.C), here=kept(z.parts // 2, 2 * z.units, z.C, dtype=BF16),
                away=kept(z.parts // 2, 2 * z.units, z.C, dtype=BF16), **token,
            ),
            dict(
                vec=kept(3, 8, z.C), inner_sums=kept(8, z.H), g_outer=kept(z.C, z.H), g_inner=kept(z.C, z.H),
                turned=kept(2, z.H, z.C, dtype=BF16), unit_sums=kept(z.parts, 1, z.units),
            ),
            6, 2, smem, [merge.here] + ([chain.here] if chain else []),
        )
        (chain or merge).step(d["token"])
        t = call(
            partial(token_back_kernel, z, l),
            dict(
                sizes=sizes, place=place, mask=a["mask"], half_grad=d["half_grad"], feed_small=d["feed_small"],
                perm=b["perm"], ewp=b["ewp"], **some(s, mixed=0, cat=0, share=0, pool=0, pooled=0, act=0, slope=0), **small,
            ),
            dict(
                mixed_grad=kept(z.N, z.I * z.C, dtype=BF16), scaled=kept(3 * z.C, z.I * z.C, dtype=BF16),
                push=kept(3, 8, z.C), here=kept(z.parts // 2, z.shared, z.C, dtype=BF16),
                away=kept(z.parts // 2, z.shared, z.C, dtype=BF16), **token,
            ),
            dict(
                vec=kept(2, 8, z.C), g_project=kept(z.C, z.C), g_mix=kept(z.I * z.C, 3 * z.C),
                rows=kept(z.parts * z.shared, z.C, dtype=BF16),
            ),
            4, 1, smem, [(chain or merge).here],
        )
        own = Chain([d, t], hid)
        if chain:
            rows = jnp.concatenate([chain.halve(t["token"]), merge.halve(t["token"])], axis=0)
            chain.widen(rows, img)
        if chain:
            own.step()
        held = [own.here] + ([chain.here] if chain else [])
        e = call(
            partial(mix_back_kernel, z, l, l == 0),
            dict(
                mask=a["mask"], back=a["back"], norm_gain=norm_gain, half_grad=d["half_grad"],
                **some(t, mixed_grad=0, scaled=0, push=0), **some(s, unit1=0, rstd1=0),
            ),
            dict(state_grad=kept(z.N, z.C) if l else arr(z.N0, z.C), first_norm=arr(2, z.C), **token),
            dict(back_h=kept(z.long, z.C), back_w=kept(z.long, z.C), back_c=kept(z.long, z.C), vec=kept(2, 8, z.C)),
            5, 0.05, (), held,
        )
        own.step(e["token"])
        if chain:
            chain.step(None, own.here)
        else:
            merge.step(e["token"])
        chain, last = chain or own, own
        grad, norms[l] = e["state_grad"], e["first_norm"]
    images_grad = grad.reshape(z.side, z.side, z.I, z.C).transpose(2, 0, 1, 3)

    f = call(
        partial(features_kernel, z),
        dict(patch=c["patch"], merge_weight=merge_t, merge_bias=merge_bias.reshape(1, -1)),
        dict(features=arr(z.I, z.half, z.half * z.O, dtype=BF16), **token), dict(merged=kept(z.I * z.M, z.O)), 6, 2, (), [last.here],
    )
    norm_rows = jnp.pad(jnp.concatenate(norms, axis=0), ((0, 16 - 2 * z.L), (0, 0))).astype(BF16)
    last.widen(jnp.concatenate([last.halve(f["token"]), norm_rows], axis=0), img)
    while chain.left:
        chain.step(None, last.here)
    feed, cut = 2 * z.units, 2 * z.units + z.shared
    merge = chain.here[None, feed:]
    bits = bits_of(hid)
    bits = bits[1:] + bits[:1]

    def widen_merge(merge, bit):
        return jnp.concatenate([merge, swap(merge, "hid", hid, bit)], axis=0)

    merge = widen_merge(merge, bits[0])
    while len(last.left) > 1:
        last.step()
    last.step(None, merge)
    feed_rows = jnp.concatenate([last.here[:feed], chain.here[:feed]], axis=0)
    have = last.here[feed:cut]
    norm_rows = last.here[cut:]
    z.found = [0]
    for step, bit in enumerate(bits):
        sent = jnp.concatenate([have, norm_rows], axis=0)
        got = swap(sent, "hid", hid, bit)
        z.found = z.found + [e ^ bit for e in z.found]
        if step + 2 < len(bits):
            merge = widen_merge(merge, bits[step + 1])
            got, _ = lax.optimization_barrier((got, merge))
        elif step + 2 == len(bits):
            merge_got = swap(merge, "hid", hid, bits[-1])
        if step + 1 < len(bits):
            have = jnp.concatenate([have, got[:-16]], axis=0)
            norm_rows = add(norm_rows, got[-16:], None)
    g = call(
        partial(last_kernel, z),
        dict(place=place, have=sent, got=got, merge_have=merge, merge_got=merge_got, feed_rows=feed_rows),
        final_outputs(z),
        dict(rows=kept(z.L, z.parts * z.shared, z.C, dtype=BF16), merge_rows=kept(z.parts * z.merge, z.C, dtype=BF16)),
        5, 2, smem,
    )
    return (
        f["features"], images_grad, g["mix_weight"], g["mix_bias"], g["squeeze_weight"].transpose(0, 2, 1),
        g["squeeze_bias"], g["expand_weight"], g["expand_bias"], g["project_weight"], g["project_bias"], g["norm_gain"],
        g["norm_bias"], g["inner_weight"].transpose(0, 2, 1), g["inner_bias"], g["outer_weight"], g["outer_bias"],
        g["merge_weight"].T, g["merge_bias"],
    )


def solution(mesh):
    maps = ("img", "hid")
    in_specs = (
        P(maps, None, None, None), P(maps, None), P(maps, None, None), P(), P(), P(), P(), P(), P(), P(), P(), P(), P(),
        P(None, None, "hid"), P(None, "hid"), P(None, "hid", None), P(), P(), P(),
    )
    out_specs = (
        P(maps, None, None), P(maps, None, None, None), P(), P(), P(), P(), P(), P(), P(), P(), P(), P(),
        P(None, None, "hid"), P(None, "hid"), P(None, "hid", None), P(), P(), P(),
    )
    return jax.shard_map(
        partial(per_device, mesh.shape["img"], mesh.shape["hid"]),
        mesh=mesh, in_specs=in_specs, out_specs=out_specs, check_vma=False,
    )
```

```python
from functools import partial

import jax
import jax.numpy as jnp
from jax import lax
from jax.experimental import pallas as pl
from jax.experimental.pallas import tpu as pltpu
from jax.sharding import PartitionSpec as P

F32 = jnp.float32
BF16 = jnp.bfloat16
GROUP = 8
MIB = 2**20


def dot(a, b, dims=(1, 0)):
    return lax.dot_general(a, b, (((dims[0],), (dims[1],)), ((), ())), preferred_element_type=F32)


def halves(v):
    high = v.astype(BF16)
    return high, (v - high.astype(F32)).astype(BF16)


def fine(a, b, dims=(1, 0)):
    high, low = halves(a)
    if dims == (0, 0):
        b_high, b_low = halves(b)
        return dot(jnp.concatenate([high, low, high], axis=0), jnp.concatenate([b_high, b_high, b_low], axis=0), dims)
    rows = a.shape[0]
    both = jnp.concatenate([high, low], axis=0)
    if b.dtype == BF16:
        out = dot(both, b, dims)
        return out[:rows] + out[rows:]
    b_high, b_low = halves(b)
    out = dot(both, b_high, dims)
    return out[:rows] + (out[rows:] + dot(high, b_low, dims))


def rows8(v):
    return v.reshape(-1, 8, v.shape[-1]).sum(axis=0)


def total(v):
    return v.sum(axis=0, keepdims=True)


def tile(v, rows):
    return jnp.broadcast_to(v[None], (rows // 8, 8, v.shape[-1])).reshape(rows, v.shape[-1])


def gelu_pair(x):
    cdf = 0.5 * lax.erf(x * 0.7071067811865476) + 0.5
    bell = jnp.exp2(x * x * (-0.5 * 1.4426950408889634))
    return x * cdf, cdf + x * bell * 0.3989422804014327


def norm_parts(v):
    centred = v - jnp.mean(v, axis=-1, keepdims=True)
    rstd = lax.rsqrt(jnp.mean(centred * centred, axis=-1, keepdims=True) + 1e-05)
    return centred * rstd, jnp.broadcast_to(rstd, v.shape)


def norm_back(grad, unit, rstd, gain):
    scaled = grad * gain
    first = jnp.mean(scaled, axis=-1, keepdims=True)
    second = jnp.mean(scaled * unit, axis=-1, keepdims=True)
    return rstd * (scaled - first - unit * second)


class Sizes:
    def __init__(self, images, side, channels, hidden, red, out, layers, parts):
        self.I, self.side, self.C, self.H, self.R, self.O, self.L = images, side, channels, hidden, red, out, layers
        self.parts, self.units = parts, hidden // parts
        self.W = side * images
        self.N0 = side * self.W
        self.N = -(-self.N0 // 432) * 432
        self.run_first = self.run_back = self.run_mix = self.N
        self.run_second = self.N // 6
        self.half = side // 2
        self.hp = -(-self.half // 8) * 8
        self.M = self.half * self.hp
        self.base = self.W
        self.tall = self.W * (2 * self.hp + 2)
        self.long = self.base + self.N + self.W
        self.at_project = 3 * channels
        self.at_expand = self.at_project + channels
        self.at_squeeze = self.at_expand + 3 * red
        self.at_small = self.at_squeeze + red
        self.shared = -(-(self.at_small + 16) // (16 * parts)) * 16
        self.merge = -(-(9 * out + 3) // (16 * parts)) * 16


class Refs:
    pass


def call(body, ins, outs, scratch, limit, micros, smem=(), after=(), far=()):
    waits = {f"after{k}": array for k, array in enumerate(after)}
    ins = dict(ins, **waits)
    vmem = pl.BlockSpec(memory_space=pltpu.VMEM)
    scalar, anywhere = pl.BlockSpec(memory_space=pltpu.SMEM), pl.BlockSpec(memory_space=pl.ANY)

    def place(name):
        return scalar if name in smem else anywhere if name in waits or name in far else vmem

    names = list(ins) + list(outs) + list(scratch)

    def kernel(*refs):
        r = Refs()
        for name, ref in zip(names, refs):
            setattr(r, name, ref)
        body(r)

    found = pl.pallas_call(
        kernel,
        out_shape=list(outs.values()),
        in_specs=[place(name) for name in ins],
        out_specs=[vmem] * len(outs),
        scratch_shapes=list(scratch.values()),
        compiler_params=pltpu.CompilerParams(vmem_limit_bytes=limit * MIB),
        cost_estimate=pl.CostEstimate(flops=int(micros * 1.15e9), bytes_accessed=0, transcendentals=0),
    )(*ins.values())
    return dict(zip(outs, found))


def arr(*shape, dtype=F32):
    return jax.ShapeDtypeStruct(shape, dtype)


def kept(*shape, dtype=F32):
    return pltpu.VMEM(shape, dtype)


def over(z, body, size):
    for at in range(0, z.N, size):
        body(slice(at, at + size), at)


def near(ref, start, off, size):
    return ref[start + off : start + off + size, :]


def parity(z, i):
    rows = lax.broadcasted_iota(jnp.int32, (8, z.C), 0)
    return jnp.where(rows % z.I == i, 1.0, 0.0)


def kinds(z, rows):
    return tile(lax.broadcasted_iota(jnp.int32, (8, z.C), 1) % 3, rows)


def weave(z, v):
    out = v[0:1] * parity(z, 0)
    for i in range(1, z.I):
        out += v[i : i + 1] * parity(z, i)
    return out


def split(z, v):
    rows = [total(v * parity(z, i)) for i in range(z.I)]
    return jnp.concatenate(rows + [jnp.zeros((GROUP - z.I, z.C), F32)], axis=0)


def front_kernel(z, r):
    rows = lax.broadcasted_iota(jnp.int32, (z.W, z.C), 0)
    lanes = lax.broadcasted_iota(jnp.int32, (z.W, z.C), 1) % 3
    image = rows % z.I
    col = rows // z.I
    high = jnp.zeros((z.W, z.C), jnp.int32)
    wide = jnp.zeros((z.W, z.C), jnp.int32)
    for i in range(z.I):
        high = jnp.where(image == i, r.sizes[i, 0], high)
        wide = jnp.where(image == i, r.sizes[i, 1], wide)
    inside = jnp.where(col < wide, 1.0, 0.0)
    first, last = col == 0, col == z.side - 1
    edge = jnp.where((first & (lanes == 2)) | (last & (lanes == 1)), 0.0, 1.0)
    back = jnp.where((last & (lanes == 2)) | (first & (lanes == 1)), 0.0, 1.0)

    def step(row, carry):
        at = pl.ds(pl.multiple_of(row * z.W, 8), z.W)
        r.mask[at, :] = jnp.where(high > row, inside, 0.0)
        return carry

    lax.fori_loop(0, z.side, step, 0)
    edge = jnp.concatenate([edge, edge], axis=0).astype(BF16)
    back = jnp.concatenate([back, back], axis=0).astype(BF16)

    def step2(row, carry):
        at = pl.ds(pl.multiple_of(row * 2 * z.W, 16), 2 * z.W)
        r.edge[at, :] = edge
        r.back[at, :] = back
        return carry

    lax.fori_loop(0, z.side // 2, step2, 0)
    if z.N > z.N0:
        pad = jnp.zeros((z.N - z.N0, z.C), F32)
        for ref in (r.mask, r.edge, r.back):
            ref[z.N0 :, :] = pad.astype(ref.dtype)
    pad = jnp.zeros((z.hp - z.half, z.O), F32)
    r.pgrad[z.M :, :] = jnp.zeros((8, 9 * z.C), F32)
    sums = jnp.zeros((8, z.O), F32)
    for i in range(z.I):
        for pair in range(z.half // 2):
            both = r.cotangent[i, :, 2 * pair * z.O : (2 * pair + 2) * z.O].astype(F32)
            both = jnp.concatenate([both[:, : z.O], pad, both[:, z.O :], pad], axis=0)
            at = i * z.M + 2 * pair * z.hp
            r.cot[at : at + 2 * z.hp, :] = both.astype(BF16)
            sums += rows8(both)
        step = z.M // 2
        for at in range(0, z.M, step):
            r.pgrad[at : at + step, :] = dot(r.cot[i * z.M + at : i * z.M + at + step, :], r.merge_weight[...])

        def part(dr, ds, b, down=0):
            k = 3 * dr + ds
            return r.pgrad[pl.ds(b * z.hp + down, z.hp), k * z.C : (k + 1) * z.C]

        for b in range(z.half):
            planes = [
                part(1, 1, b),
                part(2, 1, b) + part(0, 1, b, 1),
                part(1, 2, b),
                part(2, 2, b) + part(0, 2, b, 1),
            ]
            if b < z.half - 1:
                planes[2] += part(1, 0, b + 1)
                planes[3] += part(2, 0, b + 1) + part(0, 0, b + 1, 1)
            for plane, (down, right) in zip(planes, ((0, 0), (1, 0), (0, 1), (1, 1))):
                start = down * z.W + (2 * b + right) * z.I + i
                r.grad[pl.ds(start, z.hp, stride=2 * z.W), :] = plane
    r.merge_bias_sums[...] = sums
    r.token[...] = jnp.zeros_like(r.token)


def shift_phase(z, r, cat, size):
    r.sums[...] = jnp.zeros_like(r.sums)

    def body(rows, at):
        start = z.base + at
        kind = kinds(z, size)
        mid = near(r.normed, start, 0, size)
        high = jnp.where(kind == 2, near(r.normed, start, -z.W, size), near(r.normed, start, z.W, size))
        wide = jnp.where(kind == 2, near(r.normed, start, -z.I, size), near(r.normed, start, z.I, size))
        high = jnp.where(kind == 0, mid, high)
        wide = jnp.where(kind == 0, mid, wide * r.edge[rows, :].astype(F32))
        mask = r.mask[rows, :]
        for j, piece in enumerate((high, wide, mid)):
            cat[rows, j * z.C : (j + 1) * z.C] = piece.astype(BF16)
            r.sums[j] += rows8(piece * mask)

    over(z, body, size)


def counts_of(z, r):
    rows = []
    for i in range(GROUP):
        count = (r.sizes[i, 0] * r.sizes[i, 1]).astype(F32) if i < z.I else 1.0
        rows.append(jnp.full((1, z.C), 1.0, F32) * count)
    return jnp.concatenate(rows, axis=0)


def weigh_phase(z, r, l, o):
    pooled = r.mix_bias[l, 0:1] + r.mix_bias[l, 1:2]
    counts = counts_of(z, r)
    for j in range(3):
        pool = split(z, r.sums[j])
        o.pool[j] = pool
        pooled = pooled + fine(pool, r.mix_weight[l, j]) / counts
    o.pooled[...] = pooled
    act, slope = gelu_pair(fine(pooled, r.squeeze_weight[l], (1, 1)) + r.squeeze_bias[l : l + 1])
    o.act[...] = act
    o.slope[...] = slope
    logits = fine(act, r.ewp[l]) + r.ebp[l : l + 1]
    parts = [logits[:, j * z.C : (j + 1) * z.C] for j in range(3)]
    top = jnp.maximum(jnp.maximum(parts[0], parts[1]), parts[2])
    parts = [jnp.exp(part - top) for part in parts]
    whole = parts[0] + parts[1] + parts[2]
    for j in range(3):
        o.share[j] = parts[j] / whole


def mix_phase(z, r, l, o, size):
    share = [weave(z, o.share[j]) for j in range(3)]
    bias = tile(r.mix_bias[l, 0:1] * share[0] + r.mix_bias[l, 1:2] * share[1], size)
    share = [tile(s, size) for s in share]
    gain, shift = r.norm_gain[l, 1:2], r.norm_bias[l, 1:2]

    def body(rows, at):
        mixed = bias
        for j in range(3):
            mixed = mixed + dot(o.cat[rows, j * z.C : (j + 1) * z.C], r.mix_weight[l, j]) * share[j]
        mixed = mixed.astype(BF16)
        o.mixed[rows, :] = mixed
        token = dot(mixed, r.project_weight[l]) + r.project_bias[l : l + 1]
        halfway = r.state[rows, :] + r.mask[rows, :] * token
        unit, rstd = norm_parts(halfway)
        o.unit2[rows, :] = unit.astype(BF16)
        o.rstd2[rows, :] = rstd.astype(BF16)
        o.normed2[rows, :] = (unit * gain + shift).astype(BF16)
        r.state[rows, :] = halfway

    over(z, body, size)


def norm_store(z, r, l, o, rows, at, state):
    unit, rstd = norm_parts(state)
    o.unit1[rows, :] = unit.astype(BF16)
    o.rstd1[rows, :] = rstd.astype(BF16)
    r.normed[z.base + at : z.base + at + rows.stop - rows.start, :] = unit * r.norm_gain[l, 0:1] + r.norm_bias[l, 0:1]


def clear_edges(z, ref):
    ref[: z.base, :] = jnp.zeros((z.base, z.C), F32)
    ref[z.base + z.N0 :, :] = jnp.zeros((ref.shape[0] - z.base - z.N0, z.C), F32)


def unit_bias(z, blocks, l, which):
    at = 2 * z.L * z.units + l
    return jnp.concatenate([blocks[k, at : at + 1, : z.units].astype(F32) for k in which], axis=1)


def feed_some(o, rows, inner, bias, outer):
    act, slope = gelu_pair(dot(o.normed2[rows, :], inner, (1, 1)) + bias)
    act = act.astype(BF16)
    o.act_rows[rows, :] = act
    o.slope_rows[rows, :] = slope.astype(BF16)
    return dot(act, outer)


def half_kernel(z, r):
    which, u = range(z.parts // 2), z.units
    inner = jnp.concatenate([r.gathered[k, :u, :] for k in which], axis=0)
    outer = jnp.concatenate([r.gathered[k, u : 2 * u, :] for k in which], axis=0)
    bias = unit_bias(z, r.gathered, 0, which)

    def body(rows, at):
        r.partial[rows, :] = feed_some(r, rows, inner, bias, outer) + r.outer_bias[0:1]

    over(z, body, z.run_second)
    r.token[...] = jnp.zeros_like(r.token)


def feed_phase(z, r, l, o, source, after):
    first = 0 if l else z.H // 2

    def body(rows, at):
        out = feed_some(o, rows, r.inner[l, first:, :], r.inner_bias[l : l + 1, first:], r.outer[l, first:, :])
        out = out + (r.outer_bias[l : l + 1] if l else r.partial[rows, :])
        state = source[rows, :] + r.mask[rows, :] * out
        after(rows, at, state)

    over(z, body, z.run_second)


def saved_early(z):
    return dict(
        unit1=kept(z.N, z.C, dtype=BF16), rstd1=kept(z.N, z.C, dtype=BF16), cat=kept(z.N, 3 * z.C, dtype=BF16), mixed=kept(z.N, z.C, dtype=BF16),
        unit2=kept(z.N, z.C, dtype=BF16), rstd2=kept(z.N, z.C, dtype=BF16), normed2=kept(z.N, z.C, dtype=BF16), pool=kept(3, GROUP, z.C),
        pooled=kept(GROUP, z.C), act=kept(GROUP, z.R), slope=kept(GROUP, z.R), share=kept(3, GROUP, z.C),
    )


def saved_late(z):
    return dict(act_rows=kept(z.N, z.H, dtype=BF16), slope_rows=kept(z.N, z.H, dtype=BF16))


def first_kernel(z, r):
    spots = lax.broadcasted_iota(jnp.int32, (3 * z.C, 3 * z.C), 0)
    ends = lax.broadcasted_iota(jnp.int32, (3 * z.C, 3 * z.C), 1)
    kind = jnp.where(ends >= 2 * z.C, 2, jnp.where(ends >= z.C, 1, 0))
    r.perm[...] = jnp.where(spots == 3 * (ends - kind * z.C) + kind, 1.0, 0.0).astype(BF16)
    blank = jnp.zeros((8 - z.L, 3 * z.C), F32)
    rows = [r.expand_weight[l] for l in range(z.L)] + [r.expand_bias[...], blank]
    rows = fine(jnp.concatenate(rows, axis=0), r.perm[...])
    for l in range(z.L):
        r.ewp[l] = rows[l * z.R : (l + 1) * z.R]
    r.ebp[...] = rows[z.L * z.R : z.L * z.R + z.L]

    def begin(rows, at):
        real = min(rows.stop, z.N0) - at
        state = r.images[at : at + real, :].astype(F32) * r.mask[at : at + real, :]
        if real < rows.stop - at:
            state = jnp.concatenate([state, jnp.zeros((rows.stop - at - real, z.C), F32)], axis=0)
        r.state[rows, :] = state
        norm_store(z, r, 0, r, rows, at, state)

    over(z, begin, z.run_first)
    clear_edges(z, r.normed)
    shift_phase(z, r, r.cat, z.run_first)
    weigh_phase(z, r, 0, r)
    mix_phase(z, r, 0, r, z.run_first)
    r.token[...] = jnp.zeros_like(r.token)


def exchange_order(n):
    bits = bits_of(n)
    return bits[:1] + bits[:0:-1]


def rank(n, e):
    return sum((n >> k + 1) * (e // bit % 2) for k, bit in enumerate(exchange_order(n)))


def put_blocks(z, me, rows, size, here, away):
    for e in range(z.parts):
        put_block(z, e, rows[pl.ds(pl.multiple_of((me ^ e) * size, 16), size), :], here, away)


def put_block(z, e, block, here, away, start=0):
    at, half, stop = rank(z.parts, e), z.parts // 2, start + block.shape[0]
    if at < half:
        here[at, start:stop, :] = block
    else:
        away[at - half, start:stop, :] = block


def second_kernel(z, r):
    me = r.place[0]
    for k in range(z.parts):
        at = k * z.units
        for l in range(z.L):
            r.inner[l, at : at + z.units, :] = r.gathered[k, 2 * l * z.units : (2 * l + 1) * z.units, :]
            r.outer[l, at : at + z.units, :] = r.gathered[k, (2 * l + 1) * z.units : (2 * l + 2) * z.units, :]
    for l in range(z.L):
        r.inner_bias[l : l + 1] = unit_bias(z, r.gathered, l, range(z.parts))
    early, late = [Refs() for _ in range(z.L)], [Refs() for _ in range(z.L)]
    for l in range(z.L):
        early[l].normed2 = r.normed2_0 if l == 0 else r.normed2
        early[l].act_rows = r.act_rows_0 if l == 0 else r.act_rows
        early[l].slope_rows = r.slope_rows_0 if l == 0 else r.slope_rows

    def then_norm(rows, at, state):
        r.state[rows, :] = state
        norm_store(z, r, 1, r, rows, at, state)

    feed_phase(z, r, 0, early[0], r.state_in, then_norm)
    clear_edges(z, r.normed)
    shift_phase(z, r, r.cat, z.run_second)
    weigh_phase(z, r, 1, r)
    mix_phase(z, r, 1, r, z.run_second)

    def then_keep(rows, at, state):
        r.normed[z.base + at : z.base + at + rows.stop - rows.start, :] = state

    feed_phase(z, r, 1, early[1], r.state, then_keep)
    for i in range(z.I):
        for pair in range(z.half // 2):
            at = i * z.M + 2 * pair * z.hp
            for k in range(9):
                dr, ds = divmod(k, 3)
                two = []
                for b in (2 * pair, 2 * pair + 1):
                    col = 2 * b + ds - 1
                    if col < 0:
                        two.append(jnp.zeros((z.hp, z.C), F32))
                    else:
                        two.append(r.normed[pl.ds(dr * z.W + col * z.I + i, z.hp, stride=2 * z.W), :])
                r.patch[at : at + 2 * z.hp, k * z.C : (k + 1) * z.C] = jnp.concatenate(two, axis=0).astype(BF16)
    for k in range(9):
        grad = dot(r.cot[...], r.patch[:, k * z.C : (k + 1) * z.C], (0, 0))
        r.merge_rows[k * z.O : (k + 1) * z.O, :] = grad.astype(BF16)
    bias = total(r.merge_bias_sums[...])
    rest = z.O - 2 * z.C
    rows = [bias[:, : z.C], bias[:, z.C : 2 * z.C]]
    rows += [jnp.concatenate([bias[:, 2 * z.C :], jnp.zeros((1, z.C - rest), F32)], axis=1)]
    rows += [jnp.zeros((z.parts * z.merge - 9 * z.O - 3, z.C), F32)]
    r.merge_rows[9 * z.O :, :] = jnp.concatenate(rows, axis=0).astype(BF16)
    put_blocks(z, me, r.merge_rows, z.merge, r.merge_here, r.merge_away)


def features_kernel(z, r):
    r.merged[...] = dot(r.patch[...], r.merge_weight[...], (1, 1)) + r.merge_bias[...]
    r.token[...] = jnp.zeros_like(r.token)
    for i in range(z.I):
        for pair in range(z.half // 2):
            at = i * z.M + 2 * pair * z.hp
            wide = [r.merged[at : at + z.half, :], r.merged[at + z.hp : at + z.hp + z.half, :]]
            wide = jnp.concatenate(wide, axis=1).astype(BF16)
            r.features[i, :, 2 * pair * z.O : (2 * pair + 2) * z.O] = wide


def feed_back_kernel(z, l, r):
    gain = r.norm_gain[l, 1:2]
    for ref in (r.vec, r.inner_sums, r.g_outer, r.g_inner):
        ref[...] = jnp.zeros_like(ref)

    def units(late, early, rows):
        return late[rows, :] if l else jnp.concatenate([early[rows, :], late[rows, :]], axis=1)

    def body(rows, at):
        mask = r.mask[rows, :]
        grad = r.grad[rows, :]
        slope = units(r.slope_rows, None if l else r.slope_before, rows)
        act = units(r.act_rows, None if l else r.act_before, rows)
        out = grad * mask
        r.vec[0] += rows8(out)
        out = out.astype(BF16)
        pre = dot(out, r.outer[l], (1, 1)) * slope.astype(F32)
        r.inner_sums[...] += rows8(pre)
        pre = pre.astype(BF16)
        r.g_outer[...] += dot(out, act, (0, 0))
        r.g_inner[...] += dot(r.normed2[rows, :], pre, (0, 0))
        normed_grad = dot(pre, r.inner[l])
        unit = r.unit2[rows, :].astype(F32)
        r.vec[1] += rows8(normed_grad * unit)
        r.vec[2] += rows8(normed_grad)
        r.half_grad[rows, :] = grad + norm_back(normed_grad, unit, r.rstd2[rows, :].astype(F32), gain)

    over(z, body, z.run_back)
    inner, me = total(r.inner_sums[...]), r.place[0]
    for k, e in enumerate(z.gathered):
        r.unit_sums[me ^ e] = inner[:, k * z.units : (k + 1) * z.units]
    inner = jnp.concatenate([r.unit_sums[k] for k in range(z.parts)], axis=1)
    small = [total(r.vec[k]) for k in range(3)]
    small += [inner[:, k * z.C : (k + 1) * z.C] for k in range(z.H // z.C)]
    small += [jnp.zeros((1, z.C), F32)]
    r.feed_small[...] = jnp.concatenate(small, axis=0)
    r.turned[0] = r.g_inner[...].T.astype(BF16)
    r.turned[1] = r.g_outer[...].T.astype(BF16)
    for k in range(2):
        for spot, e in enumerate(z.gathered):
            block = r.turned[k, spot * z.units : (spot + 1) * z.units, :]
            put_block(z, e, block, r.here, r.away, k * z.units)
    r.token[...] = jnp.zeros_like(r.token)


def token_back_kernel(z, l, r):
    for ref in (r.vec, r.g_project, r.g_mix):
        ref[...] = jnp.zeros_like(ref)
    even, odd = tile(parity(z, 0), z.run_back), tile(parity(z, 1), z.run_back)

    def body(rows, at):
        token = r.half_grad[rows, :] * r.mask[rows, :]
        r.vec[0] += rows8(token)
        token = token.astype(BF16)
        r.g_project[...] += dot(r.mixed[rows, :], token, (0, 0))
        mixed_grad = dot(token, r.project_weight[l], (1, 1))
        r.vec[1] += rows8(mixed_grad)
        both = jnp.concatenate([(mixed_grad * even).astype(BF16), (mixed_grad * odd).astype(BF16)], axis=1)
        r.mixed_grad[rows, :] = both
        r.g_mix[...] += dot(both, r.cat[rows, :], (0, 0))

    over(z, body, z.run_back)
    counts = counts_of(z, r)
    zeros = jnp.zeros((GROUP - z.I, z.C), F32)
    summed = split(z, r.vec[1])
    share = [r.share[j] for j in range(3)]
    mix, dp = [], []
    for j in range(3):
        weight = r.mix_weight[l, j].astype(F32)
        rows = []
        found = 0.0
        for i in range(z.I):
            block = r.g_mix[i * z.C : (i + 1) * z.C, j * z.C : (j + 1) * z.C].T
            rows.append(total(weight * block))
            found = found + block * share[j][i : i + 1]
            scaled = weight * share[j][i : i + 1]
            r.scaled[j * z.C : (j + 1) * z.C, i * z.C : (i + 1) * z.C] = scaled.astype(BF16)
        mix.append(found)
        dp.append(jnp.concatenate(rows + [zeros], axis=0))
    for j in range(2):
        dp[j] += summed * r.mix_bias[l, j : j + 1]
    even = dp[0] * share[0] + dp[1] * share[1] + dp[2] * share[2]
    dz = jnp.concatenate([share[j] * (dp[j] - even) for j in range(3)], axis=1)
    act, slope, pooled = r.act[...], r.slope[...], r.pooled[...]
    expand = fine(jnp.concatenate([fine(act, dz, (0, 0)), dz], axis=0), r.perm[...], (1, 1))
    expand, expand_bias = expand[: z.R], total(expand[z.R :])
    dact = fine(dz, r.ewp[l], (1, 1)) * slope
    squeeze = fine(dact, pooled, (0, 0))
    dpool = fine(dact, r.squeeze_weight[l])
    push = dpool / counts
    for j in range(3):
        mix[j] += fine(r.pool[j], push, (0, 0))
        r.push[j] = weave(z, fine(push, r.mix_weight[l, j], (1, 1)))
    for j in range(3):
        r.rows[j * z.C : (j + 1) * z.C, :] = mix[j].astype(BF16)
    r.rows[z.at_project : z.at_expand, :] = r.g_project[...].astype(BF16)
    for j in range(3):
        at = z.at_expand + j * z.R
        r.rows[at : at + z.R, :] = expand[:, j * z.C : (j + 1) * z.C].astype(BF16)
    r.rows[z.at_squeeze : z.at_small, :] = squeeze.astype(BF16)
    small = [total(share[j] * summed + dpool) for j in range(2)]
    small += [total(r.vec[0]), r.feed_small[: 3 + z.H // z.C, :]]
    small += [expand_bias[:, j * z.C : (j + 1) * z.C] for j in range(3)]
    small += [jnp.concatenate([total(dact), jnp.zeros((1, z.C - z.R), F32)], axis=1)]
    used = sum(row.shape[0] for row in small)
    small += [jnp.zeros((z.parts * z.shared - z.at_small - used, z.C), F32)]
    r.rows[z.at_small :, :] = jnp.concatenate(small, axis=0).astype(BF16)
    put_blocks(z, r.place[0], r.rows, z.shared, r.here, r.away)
    r.token[...] = jnp.zeros_like(r.token)


def mix_back_kernel(z, l, last, r):
    for ref in (r.back_h, r.back_w):
        clear_edges(z, ref)
    gain = r.norm_gain[l, 0:1]
    size = z.run_mix
    push = [tile(r.push[j], size) for j in range(3)]

    def spread(rows, at):
        mask = r.mask[rows, :]
        parts = dot(r.mixed_grad[rows, :], r.scaled[...], (1, 1))
        for j, ref in enumerate((r.back_h, r.back_w, r.back_c)):
            ref[z.base + at : z.base + at + size, :] = parts[:, j * z.C : (j + 1) * z.C] + mask * push[j]

    over(z, spread, size)
    r.vec[...] = jnp.zeros_like(r.vec)

    def body(rows, at):
        start = z.base + at
        kind = kinds(z, size)
        high = jnp.where(kind == 2, near(r.back_h, start, z.W, size), near(r.back_h, start, -z.W, size))
        wide = jnp.where(kind == 2, near(r.back_w, start, z.I, size), near(r.back_w, start, -z.I, size))
        high = jnp.where(kind == 0, near(r.back_h, start, 0, size), high)
        wide = jnp.where(kind == 0, near(r.back_w, start, 0, size), wide * r.back[rows, :].astype(F32))
        grad = high + wide + near(r.back_c, start, 0, size)
        unit = r.unit1[rows, :].astype(F32)
        r.vec[0] += rows8(grad * unit)
        r.vec[1] += rows8(grad)
        grad = r.half_grad[rows, :] + norm_back(grad, unit, r.rstd1[rows, :].astype(F32), gain)
        if last:
            real = min(rows.stop, z.N0) - at
            r.state_grad[at : at + real, :] = (grad * r.mask[rows, :])[:real]
        else:
            r.state_grad[rows, :] = grad

    over(z, body, size)
    if z.N > z.N0:
        stray = r.back_h[z.base + z.N0 - z.W : z.base + z.N0, :]
        r.vec[1] -= rows8(jnp.where(kinds(z, z.W) == 1, stray, 0.0))
    r.first_norm[...] = jnp.concatenate([total(r.vec[0]), total(r.vec[1])], axis=0)
    r.token[...] = jnp.zeros_like(r.token)


def final_outputs(z):
    return dict(
        mix_weight=arr(z.L, 3, z.C, z.C), mix_bias=arr(z.L, 2, z.C), squeeze_weight=arr(z.L, z.R, z.C),
        squeeze_bias=arr(z.L, z.R), expand_weight=arr(z.L, z.R, 3 * z.C), expand_bias=arr(z.L, 3 * z.C),
        project_weight=arr(z.L, z.C, z.C), project_bias=arr(z.L, z.C), norm_gain=arr(z.L, 2, z.C),
        norm_bias=arr(z.L, 2, z.C), inner_weight=arr(z.L, z.units, z.C), inner_bias=arr(z.L, z.units),
        outer_weight=arr(z.L, z.units, z.C), outer_bias=arr(z.L, z.C), merge_weight=arr(z.O, 9 * z.C),
        merge_bias=arr(z.O),
    )


def last_kernel(z, r):
    me = r.place[0]
    half = z.parts // 2
    size = z.shared
    for at in range(z.parts):
        k = at % half
        have, merge = (r.have, r.merge_have) if at < half else (r.got, r.merge_got)
        rows = pl.ds(pl.multiple_of((me ^ z.found[at]) * z.shared, 16), z.shared)
        r.rows[0, rows, :] = have[k * size : (k + 1) * size, :]
        r.rows[1, rows, :] = merge[k, :size, :]
        rows = pl.ds(pl.multiple_of((me ^ z.found[at]) * z.merge, 16), z.merge)
        r.merge_rows[rows, :] = merge[k, size:, :]
    norms = r.have[half * size :, :].astype(F32) + r.got[half * size :, :].astype(F32)
    for l in range(z.L):
        rows = r.rows.at[l]

        def get(at, count):
            return rows[at : at + count, :].astype(F32)

        for j in range(3):
            r.mix_weight[l, j] = get(j * z.C, z.C)
            r.expand_weight[l, :, j * z.C : (j + 1) * z.C] = get(z.at_expand + j * z.R, z.R)
        r.project_weight[l] = get(z.at_project, z.C)
        r.squeeze_weight[l] = get(z.at_squeeze, z.R)
        small = get(z.at_small, 16)
        r.mix_bias[l] = small[0:2]
        r.project_bias[l : l + 1] = small[2:3]
        r.outer_bias[l : l + 1] = small[3:4]
        r.norm_gain[l] = jnp.concatenate([norms[2 * l : 2 * l + 1], small[4:5]], axis=0)
        r.norm_bias[l] = jnp.concatenate([norms[2 * l + 1 : 2 * l + 2], small[5:6]], axis=0)
        at = 6
        inner = jnp.zeros((1, z.units), F32)
        for k in range(z.H // z.C):
            for c in range(0, z.C, z.units):
                mine = jnp.where(me == (k * z.C + c) // z.units, 1.0, 0.0)
                inner = inner + small[at : at + 1, c : c + z.units] * mine
            at += 1
        r.inner_bias[l : l + 1] = inner
        for j in range(3):
            r.expand_bias[l : l + 1, j * z.C : (j + 1) * z.C] = small[at : at + 1]
            at += 1
        r.squeeze_bias[l : l + 1] = small[at : at + 1, : z.R]
        feed = r.feed_rows[2 * l * z.units : 2 * (l + 1) * z.units, :].astype(F32)
        r.inner_weight[l] = feed[: z.units]
        r.outer_weight[l] = feed[z.units :]
    for k in range(9):
        r.merge_weight[:, k * z.C : (k + 1) * z.C] = r.merge_rows[k * z.O : (k + 1) * z.O, :].astype(F32)
    small = r.merge_rows[9 * z.O : 9 * z.O + 16, :].astype(F32)
    r.merge_bias[: z.C] = small[0]
    r.merge_bias[z.C : 2 * z.C] = small[1]
    r.merge_bias[2 * z.C :] = small[2, : z.O - 2 * z.C]


def pack_kernel(z, r):
    u = z.units
    copies = [pltpu.make_async_copy(r.inner_bias, r.bias, r.sem.at[2 * z.L])]
    for l in range(z.L):
        for k, ref in enumerate((r.inner_weight, r.outer_weight)):
            at = (2 * l + k) * u
            copies.append(pltpu.make_async_copy(ref.at[l], r.block.at[at : at + u], r.sem.at[2 * l + k]))
    for copy in copies:
        copy.start()
    for copy in copies:
        copy.wait()
    bias = r.bias[...].astype(F32)
    if u < z.C:
        bias = jnp.concatenate([bias, jnp.zeros((z.L, z.C - u), F32)], axis=1)
    bias = jnp.concatenate([bias, jnp.zeros((16 - z.L, z.C), F32)], axis=0)
    r.block[2 * z.L * u :, :] = bias.astype(BF16)


def swap(x, axis, n, bit):
    return lax.ppermute(x, axis, [(a, a ^ bit) for a in range(n)])


def bits_of(n):
    return [1 << k for k in range(n.bit_length() - 1)]


def add(here, got, token):
    out = here.astype(F32) + got.astype(F32)
    if token is not None:
        out = out + token[0]
    return out.astype(BF16)


def take(tokens):
    return tokens.pop(0) if tokens else None


class Chain:
    def __init__(self, parts, hid):
        self.here = jnp.concatenate([part["here"] for part in parts], axis=1)
        self.away = jnp.concatenate([part["away"] for part in parts], axis=1)
        self.left = [("hid", hid, bit) for bit in exchange_order(hid)]

    def step(self, token=None, tie=None):
        axis, n, bit = self.left.pop(0)
        got = swap(self.away, axis, n, bit)
        if tie is not None:
            got, tie = lax.optimization_barrier((got, tie))
        x = add(self.here, got, token)
        if axis == "img":
            self.here = self.away = x
            return tie
        half = x.shape[0] // 2
        self.here, self.away = (x[:half], x[half:]) if half else (x[0], None)
        return tie

    def halve(self, token):
        while self.left:
            self.step(token)
        return self.here

    def widen(self, rows, img):
        self.here = self.away = rows
        self.left = [("img", img, bit) for bit in bits_of(img)]


def per_device(
    img, hid, images, sizes, cotangent, mix_weight, mix_bias, squeeze_weight, squeeze_bias, expand_weight, expand_bias,
    project_weight, project_bias, norm_gain, norm_bias, inner_weight, inner_bias, outer_weight, outer_bias,
    merge_weight, merge_bias,
):
    z = Sizes(
        images.shape[0], images.shape[1], images.shape[3], inner_weight.shape[2] * hid, squeeze_weight.shape[2],
        merge_weight.shape[1], mix_weight.shape[0], hid,
    )
    place = lax.axis_index("hid").reshape(1)
    flat = images.transpose(1, 2, 0, 3).reshape(z.N0, z.C)
    merge_t = merge_weight.T
    squeeze_t = squeeze_weight.transpose(0, 2, 1)
    far = [pltpu.with_memory_space_constraint(v, pltpu.HBM) for v in (inner_weight.transpose(0, 2, 1), outer_weight, inner_bias)]
    block = call(
        partial(pack_kernel, z),
        dict(place=place, inner_weight=far[0], outer_weight=far[1], inner_bias=far[2]),
        dict(block=kept(2 * z.L * z.units + 16, z.C, dtype=BF16)),
        dict(bias=kept(z.L, z.units, dtype=BF16), sem=pltpu.SemaphoreType.DMA((2 * z.L + 1,))),
        2, 1, dict(place=0), far=dict(inner_weight=0, outer_weight=0, inner_bias=0),
    )
    block = block["block"]
    smem = dict(sizes=0, place=0)
    small = dict(
        mix_weight=mix_weight, mix_bias=mix_bias, squeeze_weight=squeeze_t, squeeze_bias=squeeze_bias,
        project_weight=project_weight, project_bias=project_bias, norm_gain=norm_gain, norm_bias=norm_bias,
    )
    token = dict(token=arr(1, z.C))
    a = call(
        partial(front_kernel, z),
        dict(sizes=sizes, place=place, cotangent=cotangent, merge_weight=merge_t),
        dict(
            mask=kept(z.N, z.C), edge=kept(z.N, z.C, dtype=BF16), back=kept(z.N, z.C, dtype=BF16), cot=kept(z.I * z.M, z.O, dtype=BF16),
            grad=kept(z.tall, z.C), merge_bias_sums=kept(8, z.O), **token,
        ),
        dict(pgrad=kept(z.M + 8, 9 * z.C)),
        4, 3, smem,
    )
    order = bits_of(hid)[1:] + [1]

    def widen(have, bit, token):
        got = swap(have, "hid", hid, bit)
        return jnp.concatenate([have, got if token is None else got + token.astype(BF16)], axis=0)

    z.gathered = [0]
    for bit in order:
        z.gathered = z.gathered + [e ^ bit for e in z.gathered]
    have = widen(block[None], order[0], a["token"])
    b = call(
        partial(first_kernel, z),
        dict(
            images=flat, sizes=sizes, mask=a["mask"], edge=a["edge"], expand_weight=expand_weight, expand_bias=expand_bias,
            **small,
        ),
        dict(
            state=kept(z.N, z.C), perm=kept(3 * z.C, 3 * z.C, dtype=BF16), ewp=kept(z.L, z.R, 3 * z.C),
            ebp=kept(z.L, 3 * z.C), **saved_early(z), **token,
        ),
        dict(normed=kept(z.long, z.C), sums=kept(3, 8, z.C)),
        5, 5, smem, [have],
    )
    for bit in order[1:-1]:
        have = widen(have, bit, b["token"] if bit == order[1] else None)
    late, some_units = saved_late(z), kept(z.N, z.H // 2, dtype=BF16)
    h = call(
        partial(half_kernel, z),
        dict(gathered=have, normed2=b["normed2"], outer_bias=outer_bias),
        dict(partial=kept(z.N, z.C), act_rows=some_units, slope_rows=some_units, **token), {}, 4, 2,
    )
    have = widen(have, order[-1], h["token"])
    c = call(
        partial(second_kernel, z),
        dict(
            sizes=sizes, mask=a["mask"], edge=a["edge"], state_in=b["state"], normed2_0=b["normed2"], gathered=have,
            partial=h["partial"], place=place,
            ewp=b["ewp"], ebp=b["ebp"], outer_bias=outer_bias, cot=a["cot"], merge_bias_sums=a["merge_bias_sums"], **small,
        ),
        dict(
            patch=kept(z.I * z.M, 9 * z.C, dtype=BF16),
            merge_here=kept(z.parts // 2, z.merge, z.C, dtype=BF16), merge_away=kept(z.parts // 2, z.merge, z.C, dtype=BF16),
            inner=kept(z.L, z.H, z.C, dtype=BF16), outer=kept(z.L, z.H, z.C, dtype=BF16),
            act_rows_0=some_units, slope_rows_0=some_units, **saved_early(z), **late,
        ),
        dict(
            state=kept(z.N, z.C), normed=kept(z.tall, z.C), sums=kept(3, 8, z.C), inner_bias=kept(z.L, z.H),
            merge_rows=kept(z.parts * z.merge, z.C, dtype=BF16),
        ),
        11, 16, smem,
    )
    first = dict(b, act_rows=c["act_rows_0"], slope_rows=c["slope_rows_0"])
    before = dict(act_before=h["act_rows"], slope_before=h["slope_rows"])

    def some(s, **names):
        return {name: s[name] for name in names}

    grad = a["grad"]
    norms, chain = [None] * z.L, None
    merge = Chain([dict(here=c["merge_here"], away=c["merge_away"])], hid)
    for l in reversed(range(z.L)):
        s = c if l else first
        d = call(
            partial(feed_back_kernel, z, l),
            dict(
                place=place, mask=a["mask"], grad=grad, inner=c["inner"], outer=c["outer"], norm_gain=norm_gain,
                **some(s, act_rows=0, slope_rows=0, normed2=0, unit2=0, rstd2=0), **({} if l else before),
            ),
            dict(
                half_grad=kept(z.N, z.C), feed_small=arr(8, z.C), here=kept(z.parts // 2, 2 * z.units, z.C, dtype=BF16),
                away=kept(z.parts // 2, 2 * z.units, z.C, dtype=BF16), **token,
            ),
            dict(
                vec=kept(3, 8, z.C), inner_sums=kept(8, z.H), g_outer=kept(z.C, z.H), g_inner=kept(z.C, z.H),
                turned=kept(2, z.H, z.C, dtype=BF16), unit_sums=kept(z.parts, 1, z.units),
            ),
            6, 2, smem, [merge.here] + ([chain.here] if chain else []),
        )
        (chain or merge).step(d["token"])
        t = call(
            partial(token_back_kernel, z, l),
            dict(
                sizes=sizes, place=place, mask=a["mask"], half_grad=d["half_grad"], feed_small=d["feed_small"],
                perm=b["perm"], ewp=b["ewp"], **some(s, mixed=0, cat=0, share=0, pool=0, pooled=0, act=0, slope=0), **small,
            ),
            dict(
                mixed_grad=kept(z.N, z.I * z.C, dtype=BF16), scaled=kept(3 * z.C, z.I * z.C, dtype=BF16),
                push=kept(3, 8, z.C), here=kept(z.parts // 2, z.shared, z.C, dtype=BF16),
                away=kept(z.parts // 2, z.shared, z.C, dtype=BF16), **token,
            ),
            dict(
                vec=kept(2, 8, z.C), g_project=kept(z.C, z.C), g_mix=kept(z.I * z.C, 3 * z.C),
                rows=kept(z.parts * z.shared, z.C, dtype=BF16),
            ),
            4, 1, smem, [(chain or merge).here],
        )
        own = Chain([d, t], hid)
        if chain:
            rows = jnp.concatenate([chain.halve(t["token"]), merge.halve(t["token"])], axis=0)
            chain.widen(rows, img)
        if chain:
            own.step()
        held = [own.here] + ([chain.here] if chain else [])
        e = call(
            partial(mix_back_kernel, z, l, l == 0),
            dict(
                mask=a["mask"], back=a["back"], norm_gain=norm_gain, half_grad=d["half_grad"],
                **some(t, mixed_grad=0, scaled=0, push=0), **some(s, unit1=0, rstd1=0),
            ),
            dict(state_grad=kept(z.N, z.C) if l else arr(z.N0, z.C), first_norm=arr(2, z.C), **token),
            dict(back_h=kept(z.long, z.C), back_w=kept(z.long, z.C), back_c=kept(z.long, z.C), vec=kept(2, 8, z.C)),
            5, 0.05, (), held,
        )
        own.step(e["token"])
        if chain:
            chain.step(None, own.here)
        else:
            merge.step(e["token"])
        chain, last = chain or own, own
        grad, norms[l] = e["state_grad"], e["first_norm"]
    images_grad = grad.reshape(z.side, z.side, z.I, z.C).transpose(2, 0, 1, 3)

    f = call(
        partial(features_kernel, z),
        dict(patch=c["patch"], merge_weight=merge_t, merge_bias=merge_bias.reshape(1, -1)),
        dict(features=arr(z.I, z.half, z.half * z.O, dtype=BF16), **token), dict(merged=kept(z.I * z.M, z.O)), 6, 2, (), [last.here],
    )
    norm_rows = jnp.pad(jnp.concatenate(norms, axis=0), ((0, 16 - 2 * z.L), (0, 0))).astype(BF16)
    last.widen(jnp.concatenate([last.halve(f["token"]), norm_rows], axis=0), img)
    while chain.left:
        chain.step(None, last.here)
    feed, cut = 2 * z.units, 2 * z.units + z.shared
    merge = chain.here[None, feed:]
    bits = bits_of(hid)
    bits = bits[1:] + bits[:1]

    def widen_merge(merge, bit):
        return jnp.concatenate([merge, swap(merge, "hid", hid, bit)], axis=0)

    merge = widen_merge(merge, bits[0])
    while len(last.left) > 1:
        last.step()
    last.step(None, merge)
    feed_rows = jnp.concatenate([last.here[:feed], chain.here[:feed]], axis=0)
    have = last.here[feed:cut]
    norm_rows = last.here[cut:]
    z.found = [0]
    for step, bit in enumerate(bits):
        sent = jnp.concatenate([have, norm_rows], axis=0)
        got = swap(sent, "hid", hid, bit)
        z.found = z.found + [e ^ bit for e in z.found]
        if step + 2 < len(bits):
            merge = widen_merge(merge, bits[step + 1])
            got, _ = lax.optimization_barrier((got, merge))
        elif step + 2 == len(bits):
            merge_got = swap(merge, "hid", hid, bits[-1])
        if step + 1 < len(bits):
            have = jnp.concatenate([have, got[:-16]], axis=0)
            norm_rows = add(norm_rows, got[-16:], None)
    g = call(
        partial(last_kernel, z),
        dict(place=place, have=sent, got=got, merge_have=merge, merge_got=merge_got, feed_rows=feed_rows),
        final_outputs(z),
        dict(rows=kept(z.L, z.parts * z.shared, z.C, dtype=BF16), merge_rows=kept(z.parts * z.merge, z.C, dtype=BF16)),
        5, 2, smem,
    )
    return (
        f["features"], images_grad, g["mix_weight"], g["mix_bias"], g["squeeze_weight"].transpose(0, 2, 1),
        g["squeeze_bias"], g["expand_weight"], g["expand_bias"], g["project_weight"], g["project_bias"], g["norm_gain"],
        g["norm_bias"], g["inner_weight"].transpose(0, 2, 1), g["inner_bias"], g["outer_weight"], g["outer_bias"],
        g["merge_weight"].T, g["merge_bias"],
    )


def solution(mesh):
    maps = ("img", "hid")
    in_specs = (
        P(maps, None, None, None), P(maps, None), P(maps, None, None), P(), P(), P(), P(), P(), P(), P(), P(), P(), P(),
        P(None, None, "hid"), P(None, "hid"), P(None, "hid", None), P(), P(), P(),
    )
    out_specs = (
        P(maps, None, None), P(maps, None, None, None), P(), P(), P(), P(), P(), P(), P(), P(), P(), P(),
        P(None, None, "hid"), P(None, "hid"), P(None, "hid", None), P(), P(), P(),
    )
    return jax.shard_map(
        partial(per_device, mesh.shape["img"], mesh.shape["hid"]),
        mesh=mesh, in_specs=in_specs, out_specs=out_specs, check_vma=False,
    )
```
